32 devices in a mesh: group: 4 (over z), shard: 8 (over y, x, core).
Axes of the slice: x: 2, y: 2, z: 4, core: 2. Of those that a mesh axis runs over, the one named last changes fastest.
Arguments:
- features: bfloat16 [64, 512, 512], P(('group', 'shard')), may hold values from -6 to 6
- lengths: int32 [64], P(('group', 'shard')), may hold values from 128 to 512, as said below
- starts: int32 [64, 40], P(('group', 'shard')), may hold values from 0 to 511
- labels: int32 [64, 512], P(('group', 'shard')), may hold values from 0 to 499
- step_count: int32 [1], replicated, may hold values from 1 to 20
- weight_in: float32 [512, 768], P('shard'), may hold values from -0.25 to 0.25
- weight_rows: float32 [2, 768, 3072], P(None, 'shard'), may hold values from -0.21875 to 0.21875
- weight_down: float32 [3072, 768], P('shard'), may hold values from -0.109375 to 0.109375
- weight_head: float32 [1268, 256], P(None, 'shard'), may hold values from -0.21875 to 0.21875
- vectors: float32 [14, 3072], P(None, 'shard')
- moment_in: float32 [512, 768], P('shard'), may hold values from -5.722046e-06 to 5.722046e-06
- moment_rows: float32 [2, 768, 3072], P(None, 'shard'), may hold values from -5.722046e-06 to 5.722046e-06
- moment_down: float32 [3072, 768], P('shard'), may hold values from -5.722046e-06 to 5.722046e-06
- moment_head: float32 [1268, 256], P(None, 'shard'), may hold values from -5.722046e-06 to 5.722046e-06
- moment_vectors: float32 [14, 3072], P(None, 'shard'), may hold values from -5.722046e-06 to 5.722046e-06
- second_in: float32 [512, 768], P('shard'), may hold values from 1.2757185e-14 to 5.102874e-14
- second_rows: float32 [2, 768, 3072], P(None, 'shard'), may hold values from 1.2757185e-14 to 5.102874e-14
- second_down: float32 [3072, 768], P('shard'), may hold values from 1.2757185e-14 to 5.102874e-14
- second_head: float32 [1268, 256], P(None, 'shard'), may hold values from 1.2757185e-14 to 5.102874e-14
- second_vectors: float32 [14, 3072], P(None, 'shard'), may hold values from 1.2757185e-14 to 5.102874e-14
Outputs:
- new_weight_in: float32 [512, 768], P('shard')
- new_weight_rows: float32 [2, 768, 3072], P(None, 'shard')
- new_weight_down: float32 [3072, 768], P('shard')
- new_weight_head: float32 [1268, 256], P(None, 'shard')
- new_vectors: float32 [14, 3072], P(None, 'shard')
- new_moment_in: float32 [512, 768], P('shard')
- new_moment_rows: float32 [2, 768, 3072], P(None, 'shard')
- new_moment_down: float32 [3072, 768], P('shard')
- new_moment_head: float32 [1268, 256], P(None, 'shard')
- new_moment_vectors: float32 [14, 3072], P(None, 'shard')
- new_second_in: float32 [512, 768], P('shard')
- new_second_rows: float32 [2, 768, 3072], P(None, 'shard')
- new_second_down: float32 [3072, 768], P('shard')
- new_second_head: float32 [1268, 256], P(None, 'shard')
- new_second_vectors: float32 [14, 3072], P(None, 'shard')
- copy_in: bfloat16 [512, 768], P('shard')
- copy_rows: bfloat16 [2, 768, 3072], P(None, 'shard')
- copy_down: bfloat16 [3072, 768], P('shard')
- copy_head: bfloat16 [1268, 256], P(None, 'shard')
- copy_vectors: bfloat16 [14, 3072], P(None, 'shard')
- loss_value: float32 [1], replicated
- grad_norm: float32 [1], replicated
The draws below stay inside these ranges and needn't reach their ends.
Inputs may be any that keep to these rules, and one draw needn't show every extreme that they name: `lengths`: utterance 0 has exactly 512 valid frames.
All inputs are finite; a program needn't handle non-finite values.
Results may differ from the reference program's by a relative error of at most 0.004.
The reference program's roundings to bfloat16 on the way count: a program that leaves them out, or rounds other values in their place, can miss the bound.
Values may be sent and summed in bfloat16 or wider, within the bound.
A program may use at most 256 MiB of HBM per device.

```python
import math
import jax
import jax.numpy as jnp
from jax import lax

D = 768
CH = 512
HEADS = 12
HEAD_DIM = 64
FF = 3072
CD = 256
CODES = 500
LEN = 512
SPAN = 10
NSPAN = 40
UTTS = 64
NPARAM = 7838720


def draw_lengths(key, part):
    values = jax.random.randint(key, (UTTS,), LEN // 4, LEN + 1)
    return values.at[0].set(LEN).astype(jnp.int32)


def draw_vectors(key, part):
    base = jax.random.normal(key, (14, FF), jnp.float32)
    rows = jnp.arange(14)[:, None]
    gain_rows = (rows == 0) | (rows == 7) | (rows == 11)
    scaled = jnp.where(rows == 3, base, 0.3 * base)
    return jnp.where(gain_rows, 1.0 + 0.15 * base, scaled)


def touch_ends(result, stream_key, low, high):
    longest = result.shape.index(max(result.shape))
    spots = []
    for shift in (0, 1):
        where = [jax.random.randint(jax.random.fold_in(stream_key, axis), (), 0, length) for axis, length in enumerate(result.shape)]
        where[longest] = (where[longest] + shift) % result.shape[longest]
        spots.append(tuple(where))
    return result.at[spots[0]].set(low).at[spots[1]].set(high)


def block_levels(key, dims, shards, least, high):
    def one(dim, blocks):
        draws = jax.random.uniform(jax.random.fold_in(jax.random.fold_in(key, 6), dim), (blocks,), jnp.float32, least / len(shards), high / len(shards))
        return jnp.repeat(jnp.exp(draws), dims[dim] // blocks).reshape((-1,) + (1,) * (len(dims) - dim - 1))

    loudness = one(*shards[0])
    for cut in shards[1:]:
        loudness = loudness * one(*cut)
    return loudness


def noise(own_key, shape, spread, reach, pieces=(), held_as=jnp.bfloat16):
    values = jax.random.normal(own_key, shape, jnp.float32) * spread
    if len(pieces) > 0:
        values = block_levels(own_key, shape, pieces, -0.22, 0.18) * values
    return jnp.clip(values, min=-reach, max=reach).astype(held_as)


def setup_inputs(seed: int = 0) -> dict:
    streams_of = jax.random.split(jax.random.key(seed), 21)
    return {
        "features": noise(streams_of[0], (UTTS, LEN, CH), 1.0, 6.0, ((0, 32),)),
        "lengths": draw_lengths(jax.random.fold_in(streams_of[20], 71), 0),
        "starts": touch_ends(jax.random.randint(streams_of[2], (UTTS, NSPAN), 0, LEN), jax.random.fold_in(streams_of[2], 1), 0, LEN - 1).astype(jnp.int32),
        "labels": touch_ends(jax.random.randint(streams_of[3], (UTTS, LEN), 0, CODES), jax.random.fold_in(streams_of[3], 1), 0, CODES - 1).astype(jnp.int32),
        "step_count": jax.random.randint(streams_of[4], (1,), 1, 21).astype(jnp.int32),
        "weight_in": noise(streams_of[5], (CH, D), CH ** -0.5, 0.25, ((0, 8),), jnp.float32),
        "weight_rows": noise(streams_of[6], (2, D, FF), D ** -0.5, 0.21875, ((1, 8),), jnp.float32),
        "weight_down": noise(streams_of[7], (FF, D), FF ** -0.5, 0.109375, ((0, 8),), jnp.float32),
        "weight_head": noise(streams_of[8], (D + CODES, CD), D ** -0.5, 0.21875, ((1, 8),), jnp.float32),
        "vectors": draw_vectors(jax.random.fold_in(streams_of[20], 71), 0),
        "moment_in": noise(streams_of[10], (CH, D), (0.0011 / NPARAM ** 0.5), 5.7220458984375e-06, ((0, 8),), jnp.float32),
        "moment_rows": noise(streams_of[11], (2, D, FF), (0.0011 / NPARAM ** 0.5), 5.7220458984375e-06, ((1, 8),), jnp.float32),
        "moment_down": noise(streams_of[12], (FF, D), (0.0011 / NPARAM ** 0.5), 5.7220458984375e-06, ((0, 8),), jnp.float32),
        "moment_head": noise(streams_of[13], (D + CODES, CD), (0.0011 / NPARAM ** 0.5), 5.7220458984375e-06, ((1, 8),), jnp.float32),
        "moment_vectors": noise(streams_of[14], (14, FF), (0.0011 / NPARAM ** 0.5), 5.7220458984375e-06, ((1, 8),), jnp.float32),
        "second_in": jnp.clip(jnp.exp(math.log(5.1028740965814584e-14) - 1.3862944 * jax.random.uniform(streams_of[15], (CH, D), jnp.float32) ** block_levels(streams_of[15], (CH, D), ((0, 8),), -0.2, 0.2)), 1.2757185241453646e-14, 5.1028740965814584e-14),
        "second_rows": jnp.clip(jnp.exp(math.log(5.1028740965814584e-14) - 1.3862944 * jax.random.uniform(streams_of[16], (2, D, FF), jnp.float32) ** block_levels(streams_of[16], (2, D, FF), ((1, 8),), -0.2, 0.2)), 1.2757185241453646e-14, 5.1028740965814584e-14),
        "second_down": jnp.clip(jnp.exp(math.log(5.1028740965814584e-14) - 1.3862944 * jax.random.uniform(streams_of[17], (FF, D), jnp.float32) ** block_levels(streams_of[17], (FF, D), ((0, 8),), -0.2, 0.2)), 1.2757185241453646e-14, 5.1028740965814584e-14),
        "second_head": jnp.clip(jnp.exp(math.log(5.1028740965814584e-14) - 1.3862944 * jax.random.uniform(streams_of[18], (D + CODES, CD), jnp.float32) ** block_levels(streams_of[18], (D + CODES, CD), ((1, 8),), -0.2, 0.2)), 1.2757185241453646e-14, 5.1028740965814584e-14),
        "second_vectors": jnp.clip(jnp.exp(math.log(5.1028740965814584e-14) - 1.3862944 * jax.random.uniform(streams_of[19], (14, FF), jnp.float32) ** block_levels(streams_of[19], (14, FF), ((1, 8),), -0.2, 0.2)), 1.2757185241453646e-14, 5.1028740965814584e-14),
    }


@jax.custom_vjp
def low(v):
    return lax.optimization_barrier(v.astype(jnp.bfloat16)).astype(jnp.float32)

@jax.custom_vjp
def low_back(v):
    return v

def low_keep(v):
    return (low(v), None)

def low_pass(kept, grad):
    return (grad,)

def back_keep(v):
    return (v, None)

def back_low(kept, grad):
    return (low(grad),)
low.defvjp(low_keep, low_pass)
low_back.defvjp(back_keep, back_low)
highest = lax.Precision.HIGHEST
beta_one = 0.9
beta_two = 0.999
rate = 0.03
decay = 0.01
adam_eps = 1e-08
clip_norm = 0.01
temper = 10.0

def matmul(left, right):
    return jnp.dot(left, right, precision=highest)

def layer_norm(values, gain, shift):
    centred = values - lax.optimization_barrier(jnp.mean(values, -1, keepdims=True))
    return centred * lax.rsqrt(lax.optimization_barrier(jnp.mean(centred * centred, -1, keepdims=True)) + 1e-05) * gain + shift

def unit_rows(values):
    return values * lax.rsqrt(lax.optimization_barrier(jnp.sum(values * values, -1, keepdims=True)) + 1e-06)

def span_mask(length, begins):
    position = jnp.arange(LEN, dtype=jnp.int32)
    first = begins % (length - SPAN + 1)
    inside = (position[None, :] >= first[:, None]) & (position[None, :] < first[:, None] + SPAN)
    return jnp.any(inside, 0) & (position < length)

def utterance_loss(weights, frames, length, begins, label_row):
    w_input, w_block, w_lower, w_final, vecs = weights
    valid = jnp.arange(LEN, dtype=jnp.int32) < length
    masked = span_mask(length, begins)
    normed = low(layer_norm(frames, vecs[0, :CH], vecs[1, :CH]))
    hidden = low_back(matmul(normed, w_input) + vecs[2, :D])
    hidden = jnp.where(masked[:, None], vecs[3, :D][None, :], hidden)
    bias_qkv = jnp.concatenate([vecs[4, :D], jnp.zeros((D,), jnp.float32), vecs[5, :D]])
    triple = low(low_back(matmul(low(hidden), w_block[0, :, :3 * D]) + bias_qkv))
    query = triple[:, :D].reshape(LEN, HEADS, HEAD_DIM)
    keys = triple[:, D:2 * D].reshape(LEN, HEADS, HEAD_DIM)
    values = triple[:, 2 * D:].reshape(LEN, HEADS, HEAD_DIM)
    raw = jnp.einsum('qhd,khd->hqk', query, keys, precision=highest)
    scores = low_back(raw) * HEAD_DIM ** (-0.5)
    scores = jnp.where(valid[None, None, :], scores, -1e+30)
    probs = jax.nn.softmax(scores, -1)
    attended = jnp.einsum('hqk,khd->qhd', low(probs), values, precision=highest).reshape(LEN, D)
    attended = low(low_back(attended))
    branch = low_back(matmul(attended, w_block[0, :, 3 * D:]) + vecs[6, :D])
    first = layer_norm(hidden + branch, vecs[7, :D], vecs[8, :D])
    before = low_back(matmul(low(first), w_block[1]) + vecs[9])
    active = low(jax.nn.gelu(before, approximate=False))
    lowered = low_back(matmul(active, w_lower) + vecs[10, :D])
    second = layer_norm(first + lowered, vecs[11, :D], vecs[12, :D])
    head = low_back(matmul(low(second), w_final[:D]) + vecs[13, :CD])
    codes_unit = low(unit_rows(w_final[D:]))
    logits = temper * low_back(matmul(low(unit_rows(head)), codes_unit.T))
    picked = lax.optimization_barrier(jnp.sum(jnp.where(label_row[:, None] == jnp.arange(CODES, dtype=jnp.int32)[None, :], logits, 0.0), -1))
    losses = jax.nn.logsumexp(logits, -1) - picked
    return jnp.sum(jnp.where(masked, losses, 0.0))

def reference(features, lengths, starts, labels, step_count, weight_in, weight_rows, weight_down, weight_head, vectors, moment_in, moment_rows, moment_down, moment_head, moment_vectors, second_in, second_rows, second_down, second_head, second_vectors):
    masks = jax.vmap(span_mask)(lengths, starts)
    count = jnp.sum(masks.astype(jnp.float32))
    frames_all = features.astype(jnp.float32)
    masters = (weight_in, weight_rows, weight_down, weight_head, vectors)
    checked = jax.checkpoint(utterance_loss)

    def total(weights):
        lowered = tuple((low(w) for w in weights))

        def one(carry, item):
            frames, length, begins, label_row = item
            return (carry + checked(lowered, frames, length, begins, label_row), None)
        summed, _ = lax.scan(one, jnp.zeros((), jnp.float32), (frames_all, lengths, starts, labels))
        return summed / count
    loss, backfn = jax.vjp(total, masters)
    grads = backfn(jnp.ones((), jnp.float32))[0]
    norm = jnp.sqrt(sum((jnp.sum(g * g) for g in grads)))
    factor = jnp.minimum(1.0, clip_norm / (norm + 1e-06))
    steps = step_count[0].astype(jnp.float32)
    fix_one = 1.0 - jnp.power(beta_one, steps)
    fix_two = 1.0 - jnp.power(beta_two, steps)
    moments = (moment_in, moment_rows, moment_down, moment_head, moment_vectors)
    seconds = (second_in, second_rows, second_down, second_head, second_vectors)
    decays = (decay, decay, decay, decay, 0.0)
    new_w, new_m, new_v = ([], [], [])
    for weight, grad, moment, square, shrink in zip(masters, grads, moments, seconds, decays):
        grad = grad * factor
        moment = beta_one * moment + (1.0 - beta_one) * grad
        square = beta_two * square + (1.0 - beta_two) * grad * grad
        stepped = moment / fix_one / (jnp.sqrt(square / fix_two) + adam_eps)
        new_w.append(weight - rate * (stepped + shrink * weight))
        new_m.append(moment)
        new_v.append(square)
    copies = [w.astype(jnp.bfloat16) for w in new_w]
    return (new_w[0], new_w[1], new_w[2], new_w[3], new_w[4], new_m[0], new_m[1], new_m[2], new_m[3], new_m[4], new_v[0], new_v[1], new_v[2], new_v[3], new_v[4], copies[0], copies[1], copies[2], copies[3], copies[4], jnp.reshape(loss, (1,)), jnp.reshape(norm, (1,)))
```

```python
import functools

import jax
import jax.numpy as jnp
from jax import lax
from jax.experimental import pallas as pl
from jax.experimental.pallas import tpu as pltpu
from jax.sharding import PartitionSpec as P

D = 768
CH = 512
HEADS = 12
HEAD_DIM = 64
FF = 3072
CD = 256
CODES = 500
CPAD = 512
LEN = 512
SPAN = 10
NVEC = 14

beta_one = 0.9
beta_two = 0.999
rate = 0.03
decay = 0.01
adam_eps = 1e-08
clip_norm = 0.01
temper = 10.0

F32 = jnp.float32
BF16 = jnp.bfloat16
VMEM_BYTES = 60 * 1024 * 1024


def product(left, right):
    return jnp.dot(left, right, preferred_element_type=F32)


def product_nt(left, right):
    return lax.dot_general(left, right, (((1,), (1,)), ((), ())), preferred_element_type=F32)


def product_tn(left, right):
    return lax.dot_general(left, right, (((0,), (0,)), ((), ())), preferred_element_type=F32)


def norm_parts(values):
    centred = values - jnp.mean(values, -1, keepdims=True)
    root = lax.rsqrt(jnp.mean(centred * centred, -1, keepdims=True) + 1e-05)
    return centred * root, root


def norm_back(upstream, hat, root, gain):
    scaled = upstream * gain
    return root * (
        scaled
        - jnp.mean(scaled, -1, keepdims=True)
        - hat * jnp.mean(scaled * hat, -1, keepdims=True)
    )


def column_sum(values):
    return jnp.sum(values, 0, keepdims=True)


def gelu_pair(e):
    root = 0.7071067811865476
    reach = jnp.abs(e) * root
    tail = jnp.exp(-0.5 * e * e)
    t = 1.0 / (1.0 + 0.3275911 * reach)
    poly = t * (
        0.254829592
        + t * (-0.284496736 + t * (1.421413741 + t * (-1.453152027 + t * 1.061405429)))
    )
    half = 0.5 * poly * tail
    phi = jnp.where(e < 0.0, half, 1.0 - half)
    return e * phi, phi + e * tail * 0.3989422804014327


def params(limit=VMEM_BYTES):
    return pltpu.CompilerParams(vmem_limit_bytes=limit)


def whole(shape):
    return pl.BlockSpec(shape, lambda *_: (0,) * len(shape), pipeline_mode=pl.Buffered(1))


def rows_of(tile, width):
    return pl.BlockSpec((tile, width), lambda i: (i, 0))


def project_kernel(x_ref, mask_ref, win_ref, w0_ref, vec_ref, a_ref, h_ref, hb_ref, t_ref):
    hat, _ = norm_parts(x_ref[...].astype(F32))
    normed = (hat * vec_ref[0:1, :CH].astype(F32) + vec_ref[1:2, :CH].astype(F32)).astype(BF16)
    a_ref[...] = normed
    hidden = product(normed, win_ref[...]) + vec_ref[2:3, :D].astype(F32)
    hidden = jnp.where(mask_ref[...] > 0.0, vec_ref[3:4, :D].astype(F32), hidden)
    h_ref[...] = hidden
    low = hidden.astype(BF16)
    hb_ref[...] = low
    t_ref[:, :D] = (
        product(low, w0_ref[:, :D]) + vec_ref[4:5, :D].astype(F32)
    ).astype(BF16)
    t_ref[:, D : 2 * D] = product(low, w0_ref[:, D : 2 * D]).astype(BF16)
    t_ref[:, 2 * D : 3 * D] = (
        product(low, w0_ref[:, 2 * D : 3 * D]) + vec_ref[5:6, :D].astype(F32)
    ).astype(BF16)


def project(x, masked, win, w0, vecs, tile):
    n = x.shape[0]
    return pl.pallas_call(
        project_kernel,
        grid=(n // tile,),
        in_specs=[
            rows_of(tile, CH),
            rows_of(tile, 1),
            whole((CH, D)),
            whole((D, FF)),
            whole((NVEC, FF)),
        ],
        out_specs=[rows_of(tile, CH), rows_of(tile, D), rows_of(tile, D), rows_of(tile, 3 * D)],
        out_shape=[
            jax.ShapeDtypeStruct((n, CH), BF16),
            jax.ShapeDtypeStruct((n, D), F32),
            jax.ShapeDtypeStruct((n, D), BF16),
            jax.ShapeDtypeStruct((n, 3 * D), BF16),
        ],
        compiler_params=params(),
        name="project",
    )(x, masked, win, w0, vecs)


def half_masks():
    lane = lax.broadcasted_iota(jnp.int32, (1, 128), 1)
    return [(lane < HEAD_DIM).astype(BF16), (lane >= HEAD_DIM).astype(BF16)]


def attend_kernel(len_ref, q_ref, k_ref, v_ref, o_ref):
    length = len_ref[pl.program_id(0)]
    shift = jnp.where(lax.broadcasted_iota(jnp.int32, (1, LEN), 1) < length, 0.0, -1e30)
    keys = k_ref[...]
    total = None
    for half in half_masks():
        scores = product_nt(q_ref[...] * half, keys) * HEAD_DIM ** (-0.5) + shift
        power = jnp.exp(scores - jnp.max(scores, -1, keepdims=True))
        probs = (power * (1.0 / jnp.sum(power, -1, keepdims=True))).astype(BF16)
        part = product(probs, v_ref[...] * half)
        total = part if total is None else total + part
    o_ref[...] = total.astype(BF16)


def attend(lengths, triple):
    n = triple.shape[0]
    pairs = D // 128
    return pl.pallas_call(
        attend_kernel,
        grid_spec=pltpu.PrefetchScalarGridSpec(
            num_scalar_prefetch=1,
            grid=(n // LEN, pairs),
            in_specs=[
                pl.BlockSpec((LEN, 128), lambda u, j, _: (u, j)),
                pl.BlockSpec((LEN, 128), lambda u, j, _: (u, pairs + j)),
                pl.BlockSpec((LEN, 128), lambda u, j, _: (u, 2 * pairs + j)),
            ],
            out_specs=pl.BlockSpec((LEN, 128), lambda u, j, _: (u, j)),
        ),
        out_shape=jax.ShapeDtypeStruct((n, D), BF16),
        compiler_params=params(),
        name="attend",
    )(lengths, triple, triple, triple)


def feed_kernel(
    scale_ref,
    att_ref,
    h_ref,
    mask_ref,
    label_ref,
    w0_ref,
    wu_ref,
    wd_ref,
    wh_ref,
    cu_ref,
    vec_ref,
    loss_ref,
    z1_ref,
    act_ref,
    de_ref,
    df_ref,
    z2_ref,
    dc_ref,
    dlog_ref,
    uc_ref,
    dr1_ref,
    dy_ref,
    do_ref,
    gv_ref,
    slope_ref,
):
    @pl.when(pl.program_id(0) == 0)
    def _():
        gv_ref[...] = jnp.zeros_like(gv_ref)
        loss_ref[...] = jnp.zeros_like(loss_ref)

    def vec(row, width=D):
        return vec_ref[row : row + 1, :width].astype(F32)

    masked = mask_ref[...]
    wo = w0_ref[:, 3 * D :]
    resid_one = h_ref[...] + product(att_ref[...], wo) + vec(6)
    hat_one, root_one = norm_parts(resid_one)
    first = hat_one * vec(7) + vec(8)
    first_low = first.astype(BF16)
    z1_ref[...] = first_low
    lowered = None
    for c in range(FF // D):
        cols = slice(c * D, (c + 1) * D)
        before = product(first_low, wu_ref[:, cols]) + vec_ref[9:10, cols].astype(F32)
        active, slope = gelu_pair(before)
        active = active.astype(BF16)
        act_ref[:, cols] = active
        slope_ref[:, cols] = slope
        part = product(active, wd_ref[cols, :])
        lowered = part if lowered is None else lowered + part
    resid_two = first + lowered + vec(10)
    hat_two, root_two = norm_parts(resid_two)
    second_low = (hat_two * vec(11) + vec(12)).astype(BF16)
    z2_ref[...] = second_low
    head = product(second_low, wh_ref[...]) + vec(13, CD)
    root_head = lax.rsqrt(jnp.sum(head * head, -1, keepdims=True) + 1e-06)
    unit = head * root_head
    unit_low = unit.astype(BF16)
    uc_ref[...] = unit_low
    logits = temper * product_nt(unit_low, cu_ref[...])
    code = lax.broadcasted_iota(jnp.int32, logits.shape, 1)
    logits = jnp.where(code < CODES, logits, -1e30)
    top = jnp.max(logits, -1, keepdims=True)
    power = jnp.exp(logits - top)
    total = jnp.sum(power, -1, keepdims=True)
    onehot = code == label_ref[...]
    picked = jnp.sum(jnp.where(onehot, logits, 0.0), -1, keepdims=True)
    losses = top + jnp.log(total) - picked
    loss_ref[...] += jnp.sum(jnp.where(masked > 0.0, losses, 0.0), 0, keepdims=True)
    chances = power * (1.0 / total)
    d_logit = (
        temper
        * (
            jnp.where(masked > 0.0, chances - jnp.where(onehot, 1.0, 0.0), 0.0)
            * scale_ref[0]
        )
    ).astype(BF16)
    dlog_ref[...] = d_logit
    d_unit = product(d_logit, cu_ref[...])
    d_head = (root_head * (d_unit - unit * jnp.sum(d_unit * unit, -1, keepdims=True))).astype(BF16)
    dc_ref[...] = d_head
    gv_ref[13:14, :CD] += column_sum(d_head.astype(F32))
    d_second = product_nt(d_head, wh_ref[...])
    gv_ref[11:12, :D] += column_sum(d_second * hat_two)
    gv_ref[12:13, :D] += column_sum(d_second)
    d_resid_two = norm_back(d_second, hat_two, root_two, vec(11))
    d_lower = d_resid_two.astype(BF16)
    df_ref[...] = d_lower
    gv_ref[10:11, :D] += column_sum(d_lower.astype(F32))
    d_first = d_resid_two
    for c in range(FF // D):
        cols = slice(c * D, (c + 1) * D)
        d_before = (slope_ref[:, cols] * product_nt(d_lower, wd_ref[cols, :])).astype(BF16)
        de_ref[:, cols] = d_before
        gv_ref[9:10, cols] += column_sum(d_before.astype(F32))
        d_first = d_first + product_nt(d_before, wu_ref[:, cols])
    gv_ref[7:8, :D] += column_sum(d_first * hat_one)
    gv_ref[8:9, :D] += column_sum(d_first)
    d_resid_one = norm_back(d_first, hat_one, root_one, vec(7))
    dr1_ref[...] = d_resid_one
    d_branch = d_resid_one.astype(BF16)
    dy_ref[...] = d_branch
    gv_ref[6:7, :D] += column_sum(d_branch.astype(F32))
    do_ref[...] = product_nt(d_branch, wo).astype(BF16)


def feed(scale, att, hidden, masked, label, w0, wu, wd, wh, cu, vecs, tile):
    n = att.shape[0]
    outs = [
        (D, BF16),
        (FF, BF16),
        (FF, BF16),
        (D, BF16),
        (D, BF16),
        (CD, BF16),
        (CPAD, BF16),
        (CD, BF16),
        (D, F32),
        (D, BF16),
        (D, BF16),
    ]
    return pl.pallas_call(
        feed_kernel,
        grid=(n // tile,),
        in_specs=[
            pl.BlockSpec(memory_space=pltpu.SMEM),
            rows_of(tile, D),
            rows_of(tile, D),
            rows_of(tile, 1),
            rows_of(tile, 1),
            whole((D, FF)),
            whole((D, FF)),
            whole((FF, D)),
            whole((D, CD)),
            whole((CPAD, CD)),
            whole((NVEC, FF)),
        ],
        out_specs=[pl.BlockSpec((1, 1), lambda i: (0, 0))]
        + [rows_of(tile, width) for width, _ in outs]
        + [pl.BlockSpec((16, FF), lambda i: (0, 0))],
        out_shape=[jax.ShapeDtypeStruct((1, 1), F32)]
        + [jax.ShapeDtypeStruct((n, width), kind) for width, kind in outs]
        + [jax.ShapeDtypeStruct((16, FF), F32)],
        scratch_shapes=[pltpu.VMEM((tile, FF), F32)],
        compiler_params=params(),
        name="feed",
    )(scale, att, hidden, masked, label, w0, wu, wd, wh, cu, vecs)


def attend_back_kernel(len_ref, q_ref, k_ref, v_ref, do_ref, dq_ref, dk_ref, dv_ref):
    length = len_ref[pl.program_id(0)]
    shift = jnp.where(lax.broadcasted_iota(jnp.int32, (LEN, 1), 0) < length, 0.0, -1e30)
    keys, values = k_ref[...], v_ref[...]
    dq = dk = dv = None
    for half in half_masks():
        query = q_ref[...] * half
        upstream = do_ref[...] * half
        scores = product_nt(keys, query) * HEAD_DIM ** (-0.5) + shift
        power = jnp.exp(scores - jnp.max(scores, 0, keepdims=True))
        probs = power * (1.0 / jnp.sum(power, 0, keepdims=True))
        part_v = product(probs.astype(BF16), upstream)
        d_probs = product_nt(values, upstream)
        weight = jnp.sum(probs * d_probs, 0, keepdims=True)
        d_scores = (probs * (d_probs - weight) * HEAD_DIM ** (-0.5)).astype(BF16)
        part_k = product(d_scores, query)
        part_q = product_tn(d_scores, keys * half)
        dq = part_q if dq is None else dq + part_q
        dk = part_k if dk is None else dk + part_k
        dv = part_v if dv is None else dv + part_v
    dq_ref[...] = dq.astype(BF16)
    dk_ref[...] = dk.astype(BF16)
    dv_ref[...] = dv.astype(BF16)


def attend_back(lengths, triple, d_att):
    n = triple.shape[0]
    pairs = D // 128
    block = pl.BlockSpec((LEN, 128), lambda u, j, _: (u, j))
    return pl.pallas_call(
        attend_back_kernel,
        grid_spec=pltpu.PrefetchScalarGridSpec(
            num_scalar_prefetch=1,
            grid=(n // LEN, pairs),
            in_specs=[
                block,
                pl.BlockSpec((LEN, 128), lambda u, j, _: (u, pairs + j)),
                pl.BlockSpec((LEN, 128), lambda u, j, _: (u, 2 * pairs + j)),
                block,
            ],
            out_specs=[block] * 3,
        ),
        out_shape=[jax.ShapeDtypeStruct((n, D), BF16)] * 3,
        compiler_params=params(),
        name="attend_back",
    )(lengths, triple, triple, triple, d_att)


def project_back_kernel(
    dq_ref, dk_ref, dv_ref, dr1_ref, mask_ref, x_ref, win_ref, w0_ref, gvin_ref, dhh_ref, gv_ref
):
    @pl.when(pl.program_id(0) == 0)
    def _():
        gv_ref[...] = gvin_ref[...]

    dq, dk, dv = dq_ref[...], dk_ref[...], dv_ref[...]
    gv_ref[4:5, :D] += column_sum(dq.astype(F32))
    gv_ref[5:6, :D] += column_sum(dv.astype(F32))
    d_hidden = (
        dr1_ref[...]
        + product_nt(dq, w0_ref[:, :D])
        + product_nt(dk, w0_ref[:, D : 2 * D])
        + product_nt(dv, w0_ref[:, 2 * D : 3 * D])
    )
    masked = mask_ref[...] > 0.0
    gv_ref[3:4, :D] += column_sum(jnp.where(masked, d_hidden, 0.0))
    d_proj = jnp.where(masked, 0.0, d_hidden).astype(BF16)
    dhh_ref[...] = d_proj
    gv_ref[2:3, :D] += column_sum(d_proj.astype(F32))
    d_normed = product_nt(d_proj, win_ref[...])
    hat, _ = norm_parts(x_ref[...].astype(F32))
    gv_ref[0:1, :CH] += column_sum(d_normed * hat)
    gv_ref[1:2, :CH] += column_sum(d_normed)


def project_back(dq, dk, dv, dr1, masked, x, win, w0, gv, tile):
    n = x.shape[0]
    return pl.pallas_call(
        project_back_kernel,
        grid=(n // tile,),
        in_specs=[
            rows_of(tile, D),
            rows_of(tile, D),
            rows_of(tile, D),
            rows_of(tile, D),
            rows_of(tile, 1),
            rows_of(tile, CH),
            whole((CH, D)),
            whole((D, FF)),
            whole((16, FF)),
        ],
        out_specs=[rows_of(tile, D), pl.BlockSpec((16, FF), lambda i: (0, 0))],
        out_shape=[
            jax.ShapeDtypeStruct((n, D), BF16),
            jax.ShapeDtypeStruct((16, FF), F32),
        ],
        compiler_params=params(),
        name="project_back",
    )(dq, dk, dv, dr1, masked, x, win, w0, gv)


def unit_rows(values):
    return values * lax.rsqrt(jnp.sum(values * values, -1, keepdims=True) + 1e-06)


def span_mask(length, begins):
    position = jnp.arange(LEN, dtype=jnp.int32)
    first = begins % (length - SPAN + 1)
    inside = (position[None, :] >= first[:, None]) & (position[None, :] < first[:, None] + SPAN)
    return jnp.any(inside, 0) & (position < length)


def per_device(
    features,
    lengths,
    starts,
    labels,
    step_count,
    weight_in,
    weight_rows,
    weight_down,
    weight_head,
    vectors,
    moment_in,
    moment_rows,
    moment_down,
    moment_head,
    moment_vectors,
    second_in,
    second_rows,
    second_down,
    second_head,
    second_vectors,
):
    masters = (weight_in, weight_rows, weight_down, weight_head, vectors)
    moments = (moment_in, moment_rows, moment_down, moment_head, moment_vectors)
    seconds = (second_in, second_rows, second_down, second_head, second_vectors)
    utters = features.shape[0]
    n = utters * LEN
    masked = jax.vmap(span_mask)(lengths, starts)
    count = lax.psum(jnp.sum(masked.astype(F32)), ("group", "shard"))
    scale = jnp.reshape(1.0 / count, (1,))
    masked = masked.astype(F32).reshape(n, 1)
    label = labels.reshape(n, 1)
    x = features.reshape(n, CH)
    low = tuple(w.astype(BF16) for w in masters)
    win = lax.all_gather(low[0], "shard", axis=0, tiled=True)
    vecs = lax.all_gather(low[4], "shard", axis=1, tiled=True)
    w0 = lax.all_gather(low[1][0], "shard", axis=0, tiled=True)
    wu = lax.all_gather(low[1][1], "shard", axis=0, tiled=True)
    wd = lax.all_gather(low[2], "shard", axis=0, tiled=True)
    whead = lax.all_gather(low[3], "shard", axis=1, tiled=True)
    wh = whead[:D]
    codes = jnp.pad(whead[D:].astype(F32), ((0, CPAD - CODES), (0, 0)))
    cu = unit_rows(codes).astype(BF16)

    a, hidden, hid_low, triple = project(x, masked, win, w0, vecs, 256)
    att = attend(lengths, triple)
    loss, z1, act, de, df, z2, dc, dlog, uc, dr1, dy, d_att, gv = feed(
        scale, att, hidden, masked, label, w0, wu, wd, wh, cu, vecs, 256
    )
    g_lower = product_tn(act, df)
    g_up = product_tn(z1, de)
    g_final = product_tn(z2, dc)
    d_codes_unit = product_tn(dlog, uc)
    _, codes_back = jax.vjp(unit_rows, codes)
    g_codes = codes_back(d_codes_unit)[0][:CODES]
    dq, dk, dv = attend_back(lengths, triple, d_att)
    dhh, gv = project_back(dq, dk, dv, dr1, masked, x, win, w0, gv, 256)
    g_block = jnp.concatenate(
        [
            product_tn(hid_low, dq),
            product_tn(hid_low, dk),
            product_tn(hid_low, dv),
            product_tn(att, dy),
        ],
        1,
    )
    g_input = product_tn(a, dhh)
    scattered = (
        lax.psum_scatter(g_input, "shard", scatter_dimension=0, tiled=True),
        jnp.stack(
            [
                lax.psum_scatter(g_block, "shard", scatter_dimension=0, tiled=True),
                lax.psum_scatter(g_up, "shard", scatter_dimension=0, tiled=True),
            ]
        ),
        lax.psum_scatter(g_lower, "shard", scatter_dimension=0, tiled=True),
        lax.psum_scatter(
            jnp.concatenate([g_final, g_codes], 0), "shard", scatter_dimension=1, tiled=True
        ),
        lax.psum_scatter(gv[:NVEC], "shard", scatter_dimension=1, tiled=True),
    )
    summed = lax.psum(scattered, "group")
    loss = lax.psum(loss[0, 0], ("group", "shard")) / count
    local_squares = sum((jnp.sum(g * g) for g in summed))
    norm = jnp.sqrt(lax.psum(local_squares, "shard"))
    factor = jnp.minimum(1.0, clip_norm / (norm + 1e-06))
    steps = step_count[0].astype(F32)
    fix_one = 1.0 - jnp.power(beta_one, steps)
    fix_two = 1.0 - jnp.power(beta_two, steps)
    decays = (decay, decay, decay, decay, 0.0)
    new_w, new_m, new_v = ([], [], [])
    for weight, grad, moment, square, shrink in zip(masters, summed, moments, seconds, decays):
        grad = grad * factor
        moment = beta_one * moment + (1.0 - beta_one) * grad
        square = beta_two * square + (1.0 - beta_two) * grad * grad
        stepped = moment / fix_one / (jnp.sqrt(square / fix_two) + adam_eps)
        new_w.append(weight - rate * (stepped + shrink * weight))
        new_m.append(moment)
        new_v.append(square)
    copies = [w.astype(BF16) for w in new_w]
    return (
        *new_w,
        *new_m,
        *new_v,
        *copies,
        jnp.reshape(loss, (1,)),
        jnp.reshape(norm, (1,)),
    )


def solution(mesh):
    weights = (
        P("shard", None),
        P(None, "shard", None),
        P("shard", None),
        P(None, "shard"),
        P(None, "shard"),
    )
    both = ("group", "shard")
    in_specs = (P(both, None, None), P(both), P(both, None), P(both, None), P()) + weights * 3
    out_specs = weights * 4 + (P(), P())
    return jax.shard_map(
        per_device, mesh=mesh, in_specs=in_specs, out_specs=out_specs, check_vma=False
    )
```

```python
import functools

import jax
import jax.numpy as jnp
from jax import lax
from jax.experimental import pallas as pl
from jax.experimental.pallas import tpu as pltpu
from jax.sharding import PartitionSpec as P

D = 768
CH = 512
HEADS = 12
HEAD_DIM = 64
FF = 3072
CD = 256
CODES = 500
CPAD = 512
LEN = 512
SPAN = 10
NVEC = 14

beta_one = 0.9
beta_two = 0.999
rate = 0.03
decay = 0.01
adam_eps = 1e-08
clip_norm = 0.01
temper = 10.0

F32 = jnp.float32
BF16 = jnp.bfloat16
VMEM_BYTES = 60 * 1024 * 1024


def product(left, right):
    return jnp.dot(left, right, preferred_element_type=F32)


def product_nt(left, right):
    return lax.dot_general(left, right, (((1,), (1,)), ((), ())), preferred_element_type=F32)


def product_tn(left, right):
    return lax.dot_general(left, right, (((0,), (0,)), ((), ())), preferred_element_type=F32)


def norm_parts(values):
    centred = values - jnp.mean(values, -1, keepdims=True)
    root = lax.rsqrt(jnp.mean(centred * centred, -1, keepdims=True) + 1e-05)
    return centred * root, root


def norm_back(upstream, hat, root, gain):
    scaled = upstream * gain
    return root * (
        scaled
        - jnp.mean(scaled, -1, keepdims=True)
        - hat * jnp.mean(scaled * hat, -1, keepdims=True)
    )


def column_sum(values):
    return jnp.sum(values, 0, keepdims=True)


def gelu_pair(e):
    root = 0.7071067811865476
    reach = jnp.abs(e) * root
    tail = jnp.exp(-0.5 * e * e)
    t = 1.0 / (1.0 + 0.3275911 * reach)
    poly = t * (
        0.254829592
        + t * (-0.284496736 + t * (1.421413741 + t * (-1.453152027 + t * 1.061405429)))
    )
    half = 0.5 * poly * tail
    phi = jnp.where(e < 0.0, half, 1.0 - half)
    return e * phi, phi + e * tail * 0.3989422804014327


def params(limit=VMEM_BYTES):
    return pltpu.CompilerParams(vmem_limit_bytes=limit)


def whole(shape):
    return pl.BlockSpec(shape, lambda *_: (0,) * len(shape), pipeline_mode=pl.Buffered(1))


def rows_of(tile, width):
    return pl.BlockSpec((tile, width), lambda i: (i, 0))


def project_kernel(x_ref, mask_ref, win_ref, w0_ref, vec_ref, a_ref, h_ref, hb_ref, t_ref):
    hat, _ = norm_parts(x_ref[...].astype(F32))
    normed = (hat * vec_ref[0:1, :CH].astype(F32) + vec_ref[1:2, :CH].astype(F32)).astype(BF16)
    a_ref[...] = normed
    hidden = product(normed, win_ref[...]) + vec_ref[2:3, :D].astype(F32)
    hidden = jnp.where(mask_ref[...] > 0.0, vec_ref[3:4, :D].astype(F32), hidden)
    h_ref[...] = hidden
    low = hidden.astype(BF16)
    hb_ref[...] = low
    t_ref[:, :D] = (
        product(low, w0_ref[:, :D]) + vec_ref[4:5, :D].astype(F32)
    ).astype(BF16)
    t_ref[:, D : 2 * D] = product(low, w0_ref[:, D : 2 * D]).astype(BF16)
    t_ref[:, 2 * D : 3 * D] = (
        product(low, w0_ref[:, 2 * D : 3 * D]) + vec_ref[5:6, :D].astype(F32)
    ).astype(BF16)


def project(x, masked, win, w0, vecs, tile):
    n = x.shape[0]
    return pl.pallas_call(
        project_kernel,
        grid=(n // tile,),
        in_specs=[
            rows_of(tile, CH),
            rows_of(tile, 1),
            whole((CH, D)),
            whole((D, FF)),
            whole((NVEC, FF)),
        ],
        out_specs=[rows_of(tile, CH), rows_of(tile, D), rows_of(tile, D), rows_of(tile, 3 * D)],
        out_shape=[
            jax.ShapeDtypeStruct((n, CH), BF16),
            jax.ShapeDtypeStruct((n, D), F32),
            jax.ShapeDtypeStruct((n, D), BF16),
            jax.ShapeDtypeStruct((n, 3 * D), BF16),
        ],
        compiler_params=params(),
        name="project",
    )(x, masked, win, w0, vecs)


def half_masks():
    lane = lax.broadcasted_iota(jnp.int32, (1, 128), 1)
    return [(lane < HEAD_DIM).astype(BF16), (lane >= HEAD_DIM).astype(BF16)]


def attend_kernel(len_ref, q_ref, k_ref, v_ref, o_ref):
    length = len_ref[pl.program_id(0)]
    shift = jnp.where(lax.broadcasted_iota(jnp.int32, (1, LEN), 1) < length, 0.0, -1e30)
    keys = k_ref[...]
    total = None
    for half in half_masks():
        scores = product_nt(q_ref[...] * half, keys) * HEAD_DIM ** (-0.5) + shift
        power = jnp.exp(scores - jnp.max(scores, -1, keepdims=True))
        probs = (power * (1.0 / jnp.sum(power, -1, keepdims=True))).astype(BF16)
        part = product(probs, v_ref[...] * half)
        total = part if total is None else total + part
    o_ref[...] = total.astype(BF16)


def attend(lengths, triple):
    n = triple.shape[0]
    pairs = D // 128
    return pl.pallas_call(
        attend_kernel,
        grid_spec=pltpu.PrefetchScalarGridSpec(
            num_scalar_prefetch=1,
            grid=(n // LEN, pairs),
            in_specs=[
                pl.BlockSpec((LEN, 128), lambda u, j, _: (u, j)),
                pl.BlockSpec((LEN, 128), lambda u, j, _: (u, pairs + j)),
                pl.BlockSpec((LEN, 128), lambda u, j, _: (u, 2 * pairs + j)),
            ],
            out_specs=pl.BlockSpec((LEN, 128), lambda u, j, _: (u, j)),
        ),
        out_shape=jax.ShapeDtypeStruct((n, D), BF16),
        compiler_params=params(),
        name="attend",
    )(lengths, triple, triple, triple)


def feed_kernel(
    scale_ref,
    att_ref,
    h_ref,
    mask_ref,
    label_ref,
    w0_ref,
    wu_ref,
    wd_ref,
    wh_ref,
    cu_ref,
    vec_ref,
    loss_ref,
    z1_ref,
    act_ref,
    de_ref,
    df_ref,
    z2_ref,
    dc_ref,
    dlog_ref,
    uc_ref,
    dr1_ref,
    dy_ref,
    do_ref,
    gv_ref,
    slope_ref,
):
    @pl.when(pl.program_id(0) == 0)
    def _():
        gv_ref[...] = jnp.zeros_like(gv_ref)
        loss_ref[...] = jnp.zeros_like(loss_ref)

    def vec(row, width=D):
        return vec_ref[row : row + 1, :width].astype(F32)

    masked = mask_ref[...]
    wo = w0_ref[:, 3 * D :]
    resid_one = h_ref[...] + product(att_ref[...], wo) + vec(6)
    hat_one, root_one = norm_parts(resid_one)
    first = hat_one * vec(7) + vec(8)
    first_low = first.astype(BF16)
    z1_ref[...] = first_low
    lowered = None
    for c in range(FF // D):
        cols = slice(c * D, (c + 1) * D)
        before = product(first_low, wu_ref[:, cols]) + vec_ref[9:10, cols].astype(F32)
        active, slope = gelu_pair(before)
        active = active.astype(BF16)
        act_ref[:, cols] = active
        slope_ref[:, cols] = slope
        part = product(active, wd_ref[cols, :])
        lowered = part if lowered is None else lowered + part
    resid_two = first + lowered + vec(10)
    hat_two, root_two = norm_parts(resid_two)
    second_low = (hat_two * vec(11) + vec(12)).astype(BF16)
    z2_ref[...] = second_low
    head = product_nt(second_low, wh_ref[...]) + vec(13, CD)
    root_head = lax.rsqrt(jnp.sum(head * head, -1, keepdims=True) + 1e-06)
    unit = head * root_head
    unit_low = unit.astype(BF16)
    uc_ref[...] = unit_low
    logits = temper * product(unit_low, cu_ref[...])
    code = lax.broadcasted_iota(jnp.int32, logits.shape, 1)
    logits = jnp.where(code < CODES, logits, -1e30)
    top = jnp.max(logits, -1, keepdims=True)
    power = jnp.exp(logits - top)
    total = jnp.sum(power, -1, keepdims=True)
    onehot = code == label_ref[...]
    picked = jnp.sum(jnp.where(onehot, logits, 0.0), -1, keepdims=True)
    losses = top + jnp.log(total) - picked
    loss_ref[...] += jnp.sum(jnp.where(masked > 0.0, losses, 0.0), 0, keepdims=True)
    chances = power * (1.0 / total)
    d_logit = (
        temper
        * (
            jnp.where(masked > 0.0, chances - jnp.where(onehot, 1.0, 0.0), 0.0)
            * scale_ref[0]
        )
    ).astype(BF16)
    dlog_ref[...] = d_logit
    d_unit = product_nt(d_logit, cu_ref[...])
    d_head = (root_head * (d_unit - unit * jnp.sum(d_unit * unit, -1, keepdims=True))).astype(BF16)
    dc_ref[...] = d_head
    gv_ref[13:14, :CD] += column_sum(d_head.astype(F32))
    d_second = product(d_head, wh_ref[...])
    gv_ref[11:12, :D] += column_sum(d_second * hat_two)
    gv_ref[12:13, :D] += column_sum(d_second)
    d_resid_two = norm_back(d_second, hat_two, root_two, vec(11))
    d_lower = d_resid_two.astype(BF16)
    df_ref[...] = d_lower
    gv_ref[10:11, :D] += column_sum(d_lower.astype(F32))
    d_first = d_resid_two
    for c in range(FF // D):
        cols = slice(c * D, (c + 1) * D)
        d_before = (slope_ref[:, cols] * product_nt(d_lower, wd_ref[cols, :])).astype(BF16)
        de_ref[:, cols] = d_before
        gv_ref[9:10, cols] += column_sum(d_before.astype(F32))
        d_first = d_first + product_nt(d_before, wu_ref[:, cols])
    gv_ref[7:8, :D] += column_sum(d_first * hat_one)
    gv_ref[8:9, :D] += column_sum(d_first)
    d_resid_one = norm_back(d_first, hat_one, root_one, vec(7))
    dr1_ref[...] = d_resid_one
    d_branch = d_resid_one.astype(BF16)
    dy_ref[...] = d_branch
    gv_ref[6:7, :D] += column_sum(d_branch.astype(F32))
    do_ref[...] = product_nt(d_branch, wo).astype(BF16)


def feed(scale, att, hidden, masked, label, w0, wu, wd, wh, cu, vecs, tile):
    n = att.shape[0]
    outs = [
        (D, BF16),
        (FF, BF16),
        (FF, BF16),
        (D, BF16),
        (D, BF16),
        (CD, BF16),
        (CPAD, BF16),
        (CD, BF16),
        (D, F32),
        (D, BF16),
        (D, BF16),
    ]
    return pl.pallas_call(
        feed_kernel,
        grid=(n // tile,),
        in_specs=[
            pl.BlockSpec(memory_space=pltpu.SMEM),
            rows_of(tile, D),
            rows_of(tile, D),
            rows_of(tile, 1),
            rows_of(tile, 1),
            whole((D, FF)),
            whole((D, FF)),
            whole((FF, D)),
            whole((CD, D)),
            whole((CD, CPAD)),
            whole((NVEC, FF)),
        ],
        out_specs=[pl.BlockSpec((1, 1), lambda i: (0, 0))]
        + [rows_of(tile, width) for width, _ in outs]
        + [pl.BlockSpec((16, FF), lambda i: (0, 0))],
        out_shape=[jax.ShapeDtypeStruct((1, 1), F32)]
        + [jax.ShapeDtypeStruct((n, width), kind) for width, kind in outs]
        + [jax.ShapeDtypeStruct((16, FF), F32)],
        scratch_shapes=[pltpu.VMEM((tile, FF), F32)],
        compiler_params=params(),
        name="feed",
    )(scale, att, hidden, masked, label, w0, wu, wd, wh, cu, vecs)


def attend_back_kernel(len_ref, q_ref, k_ref, v_ref, do_ref, dq_ref, dk_ref, dv_ref):
    length = len_ref[pl.program_id(0)]
    shift = jnp.where(lax.broadcasted_iota(jnp.int32, (LEN, 1), 0) < length, 0.0, -1e30)
    keys, values = k_ref[...], v_ref[...]
    dq = dk = dv = None
    for half in half_masks():
        query = q_ref[...] * half
        upstream = do_ref[...] * half
        scores = product_nt(keys, query) * HEAD_DIM ** (-0.5) + shift
        power = jnp.exp(scores - jnp.max(scores, 0, keepdims=True))
        probs = power * (1.0 / jnp.sum(power, 0, keepdims=True))
        part_v = product(probs.astype(BF16), upstream)
        d_probs = product_nt(values, upstream)
        weight = jnp.sum(probs * d_probs, 0, keepdims=True)
        d_scores = (probs * (d_probs - weight) * HEAD_DIM ** (-0.5)).astype(BF16)
        part_k = product(d_scores, query)
        part_q = product_tn(d_scores, keys * half)
        dq = part_q if dq is None else dq + part_q
        dk = part_k if dk is None else dk + part_k
        dv = part_v if dv is None else dv + part_v
    dq_ref[...] = dq.astype(BF16)
    dk_ref[...] = dk.astype(BF16)
    dv_ref[...] = dv.astype(BF16)


def attend_back(lengths, triple, d_att):
    n = triple.shape[0]
    pairs = D // 128
    block = pl.BlockSpec((LEN, 128), lambda u, j, _: (u, j))
    return pl.pallas_call(
        attend_back_kernel,
        grid_spec=pltpu.PrefetchScalarGridSpec(
            num_scalar_prefetch=1,
            grid=(n // LEN, pairs),
            in_specs=[
                block,
                pl.BlockSpec((LEN, 128), lambda u, j, _: (u, pairs + j)),
                pl.BlockSpec((LEN, 128), lambda u, j, _: (u, 2 * pairs + j)),
                block,
            ],
            out_specs=[block] * 3,
        ),
        out_shape=[jax.ShapeDtypeStruct((n, D), BF16)] * 3,
        compiler_params=params(),
        name="attend_back",
    )(lengths, triple, triple, triple, d_att)


def project_back_kernel(
    dq_ref, dk_ref, dv_ref, dr1_ref, mask_ref, x_ref, win_ref, w0_ref, gvin_ref, dhh_ref, gv_ref
):
    @pl.when(pl.program_id(0) == 0)
    def _():
        gv_ref[...] = gvin_ref[...]

    dq, dk, dv = dq_ref[...], dk_ref[...], dv_ref[...]
    gv_ref[4:5, :D] += column_sum(dq.astype(F32))
    gv_ref[5:6, :D] += column_sum(dv.astype(F32))
    d_hidden = (
        dr1_ref[...]
        + product_nt(dq, w0_ref[:, :D])
        + product_nt(dk, w0_ref[:, D : 2 * D])
        + product_nt(dv, w0_ref[:, 2 * D : 3 * D])
    )
    masked = mask_ref[...] > 0.0
    gv_ref[3:4, :D] += column_sum(jnp.where(masked, d_hidden, 0.0))
    d_proj = jnp.where(masked, 0.0, d_hidden).astype(BF16)
    dhh_ref[...] = d_proj
    gv_ref[2:3, :D] += column_sum(d_proj.astype(F32))
    d_normed = product_nt(d_proj, win_ref[...])
    hat, _ = norm_parts(x_ref[...].astype(F32))
    gv_ref[0:1, :CH] += column_sum(d_normed * hat)
    gv_ref[1:2, :CH] += column_sum(d_normed)


def project_back(dq, dk, dv, dr1, masked, x, win, w0, gv, tile):
    n = x.shape[0]
    return pl.pallas_call(
        project_back_kernel,
        grid=(n // tile,),
        in_specs=[
            rows_of(tile, D),
            rows_of(tile, D),
            rows_of(tile, D),
            rows_of(tile, D),
            rows_of(tile, 1),
            rows_of(tile, CH),
            whole((CH, D)),
            whole((D, FF)),
            whole((16, FF)),
        ],
        out_specs=[rows_of(tile, D), pl.BlockSpec((16, FF), lambda i: (0, 0))],
        out_shape=[
            jax.ShapeDtypeStruct((n, D), BF16),
            jax.ShapeDtypeStruct((16, FF), F32),
        ],
        compiler_params=params(),
        name="project_back",
    )(dq, dk, dv, dr1, masked, x, win, w0, gv)


MESH = pl.DeviceIdType.MESH


def ceil_to(value, step):
    return -(-value // step) * step


class Chunk:
    def __init__(self, names, rows, group, wide_xy, wide_z):
        self.names = names
        self.used = sum(rows)
        self.starts = [sum(rows[:i]) for i in range(len(rows))]
        self.piece_rows = rows
        self.rows = ceil_to(self.used, 16 * group)
        self.part = self.rows // group
        self.kind_xy = F32 if wide_xy else BF16
        self.kind_z = F32 if wide_z else BF16


def tiles(rows, step, body):
    def once(i, carry):
        body(pl.ds(pl.multiple_of(i * step, step), step))
        return carry

    lax.fori_loop(0, rows // step, once, 0)


def reduce_kernel(chunks, groups, shards, *refs):
    chips = shards // 2
    n = len(chunks)
    refs = list(refs)

    def take(count):
        out = refs[:count]
        del refs[:count]
        return out

    pieces = [take(len(c.names)) for c in chunks]
    (loss_ref,) = take(1)
    outs = take(n)
    (stat_ref,) = take(1)
    first = take(n)
    own_st, rec_st = take(2)
    send_xy, recv_xy, acc = take(n), take(n), take(n)
    send_z, recv_z, ring = take(n), take(n), take(n)
    loss_all, stat_all = take(2)
    core_sems, load_sems, xy_sems, z_sems, right_sems, left_sems, loss_sems, stat_sems = take(8)

    g = lax.axis_index("group")
    s = lax.axis_index("shard")
    core = lax.rem(s, 2)
    chip = s // 2
    sibling = s + 1 - 2 * core

    barrier = pltpu.get_barrier_semaphore()
    for e in range(1, shards):
        pl.semaphore_signal(
            barrier, 1, device_id=(g, lax.rem(s + e, shards)), device_id_type=MESH
        )
    for e in range(1, groups):
        pl.semaphore_signal(
            barrier, 1, device_id=(lax.rem(g + e, groups), s), device_id_type=MESH
        )
    pl.semaphore_wait(barrier, shards - 1 + groups - 1)

    def remote(src, dst, sems, where, device):
        return pltpu.make_async_remote_copy(
            src_ref=src,
            dst_ref=dst,
            send_sem=sems.at[(0,) + where],
            recv_sem=sems.at[(1,) + where],
            device_id=device,
            device_id_type=MESH,
        )

    def core_copy(t, i):
        c = chunks[t]
        return remote(
            pieces[t][i].at[:, 1 - core],
            first[t].at[:, pl.ds(c.starts[i], c.piece_rows[i])],
            core_sems,
            (t, i),
            (g, sibling),
        )

    def loss_copy(e):
        return remote(
            loss_ref, loss_all.at[g], loss_sems, (e,), (lax.rem(g + e, groups), s)
        )

    for t in range(n):
        for i in range(len(chunks[t].names)):
            core_copy(t, i).start()
    for e in range(1, groups):
        loss_copy(e).start()
    loss_all[g] = loss_ref[...]

    def chip_at(d):
        return lax.rem(chip + d, chips)

    def loads(t, d):
        c = chunks[t]
        q = chip_at(d)
        return [
            pltpu.make_async_copy(
                pieces[t][i].at[q, core],
                own_st.at[d, pl.ds(c.starts[i], c.piece_rows[i])],
                load_sems.at[0, d, i],
            )
            for i in range(len(c.names))
        ]

    def late_load(t, d):
        c = chunks[t]
        return pltpu.make_async_copy(
            first[t].at[chip_at(d), pl.ds(0, c.used)],
            rec_st.at[d, pl.ds(0, c.used)],
            load_sems.at[1, d, 0],
        )

    def xy_copy(t, d):
        return remote(
            send_xy[t].at[d - 1],
            recv_xy[t].at[d - 1],
            xy_sems,
            (t, d),
            (g, 2 * chip_at(d) + core),
        )

    def stage_chips(t):
        c = chunks[t]
        order = list(range(1, chips)) + [0]
        for d in order:
            for copy in loads(t, d):
                copy.start()
        for i in range(len(c.names)):
            core_copy(t, i).wait_recv()
        for d in order:
            late_load(t, d).start()
        for d in order:
            for copy in loads(t, d):
                copy.wait()
            late_load(t, d).wait()
            if c.rows > c.used:
                pad = (c.rows - c.used, D)
                own_st[d, c.used : c.rows] = jnp.zeros(pad, F32)
                rec_st[d, c.used : c.rows] = jnp.zeros(pad, F32)
            if d == 0:

                def keep(rows):
                    acc[t][rows] = own_st[0, rows] + rec_st[0, rows]

                tiles(c.rows, 32, keep)
            else:

                def send(rows):
                    send_xy[t][d - 1, rows] = (own_st[d, rows] + rec_st[d, rows]).astype(c.kind_xy)

                tiles(c.rows, 32, send)
                xy_copy(t, d).start()

    def part_rows(t, p):
        return pl.ds(pl.multiple_of(p * chunks[t].part, 16), chunks[t].part)

    def z_copy(t, e):
        return remote(
            send_z[t].at[e - 1],
            recv_z[t].at[e - 1],
            z_sems,
            (t, e),
            (lax.rem(g + e, groups), s),
        )

    def stage_group(t):
        c = chunks[t]
        for d in range(1, chips):
            xy_copy(t, d).wait_recv()

        def add(rows):
            total = acc[t][rows]
            for d in range(1, chips):
                total = total + recv_xy[t][d - 1, rows].astype(F32)
            acc[t][rows] = total

        tiles(c.rows, 32, add)
        for e in range(1, groups):
            base = pl.multiple_of(lax.rem(g + e, groups) * c.part, 16)

            def send(rows):
                here = pl.ds(pl.multiple_of(base + rows.start, 16), 16)
                send_z[t][e - 1, rows] = acc[t][here].astype(BF16)

            tiles(c.part, 16, send)
            z_copy(t, e).start()

    def ring_copy(t, k, way):
        p = g - k if way == 0 else g + k
        side = g + 1 if way == 0 else g - 1
        sems = right_sems if way == 0 else left_sems
        rows = part_rows(t, p)
        return pltpu.make_async_remote_copy(
            src_ref=ring[t].at[rows],
            dst_ref=ring[t].at[rows],
            send_sem=sems.at[0, t, k],
            recv_sem=sems.at[1, t, k],
            device_id=(side, s),
            device_id_type=MESH,
        )

    def holds(k, way):
        return g >= k if way == 0 else g + k < groups

    def sends(k, way):
        return (g >= k) & (g < groups - 1) if way == 0 else (g + k < groups) & (g > 0)

    def arrived(t, k, way):
        p = g - k if way == 0 else g + k
        sems = right_sems if way == 0 else left_sems
        rows = part_rows(t, p)
        return pltpu.make_async_remote_copy(
            src_ref=ring[t].at[rows],
            dst_ref=ring[t].at[rows],
            send_sem=sems.at[0, t, k],
            recv_sem=sems.at[1, t, k - 1],
            device_id=(lax.rem(g + 1, groups), s),
            device_id_type=MESH,
        )

    def stage_total(t):
        c = chunks[t]
        for e in range(1, groups):
            z_copy(t, e).wait_recv()
        base = pl.multiple_of(g * c.part, 16)

        def add(rows):
            here = pl.ds(pl.multiple_of(base + rows.start, 16), 16)
            total = acc[t][here]
            for e in range(1, groups):
                total = total + recv_z[t][e - 1, rows].astype(F32)
            ring[t][here] = total.astype(c.kind_z)

        tiles(c.part, 16, add)
        for way in (0, 1):

            @pl.when(sends(0, way))
            def _():
                ring_copy(t, 0, way).start()

    def stage_ring(t, k):
        for way in (0, 1):

            @pl.when(holds(k, way))
            def _():
                arrived(t, k, way).wait_recv()

            if k < groups - 1:

                @pl.when(sends(k, way))
                def _():
                    ring_copy(t, k, way).start()

    def stage_end(t, squares):
        c = chunks[t]

        def once(i, total):
            rows = pl.ds(pl.multiple_of(i * 16, 16), 16)
            value = ring[t][rows].astype(F32)
            outs[t][rows] = value
            value = value * value
            return total + value[:8] + value[8:]

        return lax.fori_loop(0, c.rows // 16, once, squares)

    squares = jnp.zeros((8, D), F32)
    lag = 3 + groups
    for step in range(n + lag):
        for behind, stage in enumerate(
            [stage_chips, stage_group, stage_total]
            + [functools.partial(stage_ring, k=k) for k in range(1, groups)]
        ):
            if 0 <= step - behind < n:
                stage(step - behind)
        if 0 <= step - (2 + groups) < n:
            squares = stage_end(step - (2 + groups), squares)

    for e in range(1, groups):
        loss_copy(e).wait_recv()
    loss = loss_all[0]
    for p in range(1, groups):
        loss = loss + loss_all[p]
    lane = lax.broadcasted_iota(jnp.int32, (8, 128), 1)
    stat_ref[...] = jnp.where(lane == 0, jnp.sum(squares), loss)

    def stat_copy(e):
        return remote(
            stat_ref, stat_all.at[s], stat_sems, (e,), (g, lax.rem(s + e, shards))
        )

    for e in range(1, shards):
        stat_copy(e).start()
    stat_all[s] = stat_ref[...]
    for e in range(1, shards):
        stat_copy(e).wait_recv()
    for t in range(n):
        for i in range(len(chunks[t].names)):
            core_copy(t, i).wait_send()
        for d in range(1, chips):
            xy_copy(t, d).wait_send()
        for e in range(1, groups):
            z_copy(t, e).wait_send()
        for k in range(groups - 1):
            for way in (0, 1):

                @pl.when(sends(k, way))
                def _():
                    ring_copy(t, k, way).wait_send()

    for e in range(1, groups):
        loss_copy(e).wait_send()
    for e in range(1, shards):
        stat_copy(e).wait_send()
    total = stat_all[0]
    for p in range(1, shards):
        total = total + stat_all[p]
    stat_ref[...] = total


def reduce_all(chunks, groups, shards, pieces, loss):
    chips = shards // 2
    most = max(c.rows for c in chunks)
    many = max(len(c.names) for c in chunks)
    n = len(chunks)
    hbm = pl.BlockSpec(memory_space=pl.ANY)
    vmem = pl.BlockSpec(memory_space=pltpu.VMEM)
    dma = pltpu.SemaphoreType.DMA
    results = pl.pallas_call(
        functools.partial(reduce_kernel, chunks, groups, shards),
        in_specs=[hbm] * sum(len(p) for p in pieces) + [vmem],
        out_specs=[vmem] * n + [vmem] + [hbm] * n,
        out_shape=[jax.ShapeDtypeStruct((c.rows, D), F32) for c in chunks]
        + [jax.ShapeDtypeStruct((8, 128), F32)]
        + [jax.ShapeDtypeStruct((chips, c.rows, D), F32) for c in chunks],
        scratch_shapes=[pltpu.VMEM((chips, most, D), F32)] * 2
        + [pltpu.VMEM((chips - 1, c.rows, D), c.kind_xy) for c in chunks] * 2
        + [pltpu.VMEM((c.rows, D), F32) for c in chunks]
        + [pltpu.VMEM((groups - 1, c.part, D), BF16) for c in chunks] * 2
        + [pltpu.VMEM((c.rows, D), c.kind_z) for c in chunks]
        + [pltpu.VMEM((groups, 8, 128), F32), pltpu.VMEM((shards, 8, 128), F32)]
        + [
            dma((2, n, many)),
            dma((2, chips, many)),
            dma((2, n, chips)),
            dma((2, n, groups)),
            dma((2, n, groups)),
            dma((2, n, groups)),
            dma((2, groups)),
            dma((2, shards)),
        ],
        compiler_params=pltpu.CompilerParams(
            collective_id=1, has_side_effects=True, vmem_limit_bytes=VMEM_BYTES
        ),
        name="reduce",
    )(*[p for group in pieces for p in group], loss)
    return results[:n], results[n]


def adam_step(weight, grad, moment, square, shrink, scal_ref):
    grad = grad * scal_ref[0]
    moment = beta_one * moment + (1.0 - beta_one) * grad
    square = beta_two * square + (1.0 - beta_two) * grad * grad
    stepped = moment / scal_ref[1] / (jnp.sqrt(square / scal_ref[2]) + adam_eps)
    return weight - rate * (stepped + shrink * weight), moment, square


def adam_kernel(scal_ref, *refs):
    w, m, v = refs[0:5], refs[5:10], refs[10:15]
    g_in, g_qkvo, g_up, g_down, g_head, g_vec = refs[15:21]
    outs = [refs[21 + 5 * i : 26 + 5 * i] for i in range(4)]

    def update(i, grad, where=...):
        shrink = 0.0 if i == 4 else decay
        new = adam_step(w[i][where], grad, m[i][where], v[i][where], shrink, scal_ref)
        for out, value in zip(outs, new):
            out[i][where] = value
        outs[3][i][where] = new[0].astype(BF16)

    update(1, g_qkvo[...], 0)
    update(1, g_up[...], 1)
    update(2, g_down[...])

    @pl.when(pl.program_id(0) == 0)
    def _():
        update(0, g_in[...])
        update(3, g_head[...])
        update(4, g_vec[...])


def adam(scalars, weights, moments, seconds, grads):
    parts = FF // D
    depth = weights[1].shape[1]
    tall = weights[2].shape[0] // parts

    def fixed(a):
        return pl.BlockSpec(a.shape, lambda i: (0,) * a.ndim)

    w_specs = [
        fixed(weights[0]),
        pl.BlockSpec((2, depth, D), lambda i: (0, 0, i)),
        pl.BlockSpec((tall, D), lambda i: (i, 0)),
        fixed(weights[3]),
        fixed(weights[4]),
    ]
    band = pl.BlockSpec((depth, D), lambda i: (i, 0))
    g_specs = [fixed(grads[0]), band, band, w_specs[2], fixed(grads[4]), fixed(grads[5])]
    shapes = [jax.ShapeDtypeStruct(w.shape, F32) for w in weights]
    low = [jax.ShapeDtypeStruct(w.shape, BF16) for w in weights]
    outs = pl.pallas_call(
        adam_kernel,
        grid=(parts,),
        in_specs=[pl.BlockSpec(memory_space=pltpu.SMEM)] + w_specs * 3 + g_specs,
        out_specs=w_specs * 4,
        out_shape=shapes * 3 + low,
        compiler_params=params(),
        name="adam",
    )(scalars, *weights, *moments, *seconds, *grads)
    return [outs[i * 5 : (i + 1) * 5] for i in range(4)]


def span_mask(length, begins):
    position = jnp.arange(LEN, dtype=jnp.int32)
    first = begins % (length - SPAN + 1)
    inside = (position[None, :] >= first[:, None]) & (position[None, :] < first[:, None] + SPAN)
    return jnp.any(inside, 0) & (position < length)


def per_device(
    features,
    lengths,
    starts,
    labels,
    step_count,
    weight_in,
    weight_rows,
    weight_down,
    weight_head,
    vectors,
    moment_in,
    moment_rows,
    moment_down,
    moment_head,
    moment_vectors,
    second_in,
    second_rows,
    second_down,
    second_head,
    second_vectors,
):
    masters = (weight_in, weight_rows, weight_down, weight_head, vectors)
    moments = (moment_in, moment_rows, moment_down, moment_head, moment_vectors)
    seconds = (second_in, second_rows, second_down, second_head, second_vectors)
    utters = features.shape[0]
    n = utters * LEN
    masked = jax.vmap(span_mask)(lengths, starts)
    count = lax.psum(jnp.sum(masked.astype(F32)), ("group", "shard"))
    scale = jnp.reshape(1.0 / count, (1,))
    masked = masked.astype(F32).reshape(n, 1)
    label = labels.reshape(n, 1)
    x = features.reshape(n, CH)
    low = tuple(w.astype(BF16) for w in masters)
    win = lax.all_gather(low[0], "shard", axis=0, tiled=True)
    vecs = lax.all_gather(low[4], "shard", axis=1, tiled=True)
    w0 = lax.all_gather(low[1][0], "shard", axis=0, tiled=True)
    wu = lax.all_gather(low[1][1], "shard", axis=0, tiled=True)
    wd = lax.all_gather(low[2], "shard", axis=0, tiled=True)
    whead = lax.all_gather(low[3].T, "shard", axis=0, tiled=True)
    wh = whead[:, :D]
    codes = jnp.pad(whead[:, D:].astype(F32), ((0, 0), (0, CPAD - CODES)))
    codes_root = lax.rsqrt(jnp.sum(codes * codes, 0, keepdims=True) + 1e-06)
    codes_unit = codes * codes_root
    cu = codes_unit.astype(BF16)

    a, hidden, hid_low, triple = project(x, masked, win, w0, vecs, 256)
    att = attend(lengths, triple)
    loss, z1, act, de, df, z2, dc, dlog, uc, dr1, dy, d_att, gv = feed(
        scale, att, hidden, masked, label, w0, wu, wd, wh, cu, vecs, 256
    )
    groups, shards = lax.axis_size("group"), lax.axis_size("shard")

    def split(grad):
        return grad.reshape(shards // 2, 2, grad.shape[0] // shards, D)

    g_lower = split(product_tn(act, df))
    g_up = [split(product_tn(z1, de[:, c * D : (c + 1) * D])) for c in range(FF // D)]
    d_unit = product_tn(uc, dlog)
    g_codes = codes_root * (d_unit - codes_unit * jnp.sum(d_unit * codes_unit, 0, keepdims=True))
    g_head = [split(product_tn(dc, z2)), split(jnp.pad(g_codes, ((0, 0), (0, D - CPAD))))]
    dq, dk, dv = attend_back(lengths, triple, d_att)
    dhh, gv = project_back(dq, dk, dv, dr1, masked, x, win, w0, gv, 256)
    g_qkvo = [split(product_tn(hid_low, d)) for d in (dq, dk, dv)] + [split(product_tn(att, dy))]
    wide = FF // shards
    gv = jnp.swapaxes(gv.reshape(16, shards, wide), 0, 1)
    gv = jnp.pad(gv, ((0, 0), (0, 0), (0, D - wide))).reshape(shards // 2, 2, 16, D)
    g_tail = [split(product_tn(a, dhh)), gv]
    chunks = [
        Chunk("ht", [CD // shards] * 2, groups, True, True),
        Chunk("d", [FF // shards], groups, False, True),
        Chunk("0123", [D // shards] * 4, groups, False, False),
        Chunk("qkvo", [D // shards] * 4, groups, False, False),
        Chunk("iv", [CH // shards, 16], groups, False, True),
    ]
    (s_head, s_down, s_up, s_qkvo, s_tail), stat = reduce_all(
        chunks,
        groups,
        shards,
        [g_head, [g_lower], g_up, g_qkvo, g_tail],
        jnp.broadcast_to(loss, (8, 128)),
    )
    norm = jnp.sqrt(stat[0, 0])
    loss = stat[0, 1] / count
    factor = jnp.minimum(1.0, clip_norm / (norm + 1e-06))
    steps = step_count[0].astype(F32)
    fix_one = 1.0 - jnp.power(beta_one, steps)
    fix_two = 1.0 - jnp.power(beta_two, steps)
    scalars = jnp.stack([factor, fix_one, fix_two])
    deep = CD // shards
    first = CH // shards
    summed = [
        s_tail[:first],
        s_qkvo,
        s_up,
        s_down,
        jnp.concatenate([s_head[:deep], s_head[deep : 2 * deep, :CODES]], 1),
        s_tail[first : first + NVEC, :wide],
    ]

    def turned(arrays):
        return [a.T if i == 3 else a for i, a in enumerate(arrays)]

    new_w, new_m, new_v, copies = (
        turned(out)
        for out in adam(scalars, turned(masters), turned(moments), turned(seconds), summed)
    )
    return (
        *new_w,
        *new_m,
        *new_v,
        *copies,
        jnp.reshape(loss, (1,)),
        jnp.reshape(norm, (1,)),
    )


def solution(mesh):
    weights = (
        P("shard", None),
        P(None, "shard", None),
        P("shard", None),
        P(None, "shard"),
        P(None, "shard"),
    )
    both = ("group", "shard")
    in_specs = (P(both, None, None), P(both), P(both, None), P(both, None), P()) + weights * 3
    out_specs = weights * 4 + (P(), P())
    return jax.shard_map(
        per_device, mesh=mesh, in_specs=in_specs, out_specs=out_specs, check_vma=False
    )
```

```python
import functools

import jax
import jax.numpy as jnp
from jax import lax
from jax.experimental import pallas as pl
from jax.experimental.pallas import tpu as pltpu
from jax.sharding import PartitionSpec as P

D = 768
CH = 512
HEADS = 12
HEAD_DIM = 64
FF = 3072
CD = 256
CODES = 500
CPAD = 512
LEN = 512
SPAN = 10
NVEC = 14

beta_one = 0.9
beta_two = 0.999
rate = 0.03
decay = 0.01
adam_eps = 1e-08
clip_norm = 0.01
temper = 10.0

F32 = jnp.float32
BF16 = jnp.bfloat16
VMEM_BYTES = 60 * 1024 * 1024


def product(left, right):
    return jnp.dot(left, right, preferred_element_type=F32)


def product_nt(left, right):
    return lax.dot_general(left, right, (((1,), (1,)), ((), ())), preferred_element_type=F32)


def product_tn(left, right):
    return lax.dot_general(left, right, (((0,), (0,)), ((), ())), preferred_element_type=F32)


def norm_parts(values):
    centred = values - jnp.mean(values, -1, keepdims=True)
    root = lax.rsqrt(jnp.mean(centred * centred, -1, keepdims=True) + 1e-05)
    return centred * root, root


def norm_back(upstream, hat, root, gain):
    scaled = upstream * gain
    return root * (
        scaled
        - jnp.mean(scaled, -1, keepdims=True)
        - hat * jnp.mean(scaled * hat, -1, keepdims=True)
    )


def column_sum(values):
    return jnp.sum(values, 0, keepdims=True)


def gelu_pair(e):
    root = 0.7071067811865476
    reach = jnp.abs(e) * root
    tail = jnp.exp(-0.5 * e * e)
    t = 1.0 / (1.0 + 0.3275911 * reach)
    poly = t * (
        0.254829592
        + t * (-0.284496736 + t * (1.421413741 + t * (-1.453152027 + t * 1.061405429)))
    )
    half = 0.5 * poly * tail
    phi = jnp.where(e < 0.0, half, 1.0 - half)
    return e * phi, phi + e * tail * 0.3989422804014327


def params(limit=VMEM_BYTES):
    return pltpu.CompilerParams(vmem_limit_bytes=limit)


def whole(shape):
    return pl.BlockSpec(shape, lambda *_: (0,) * len(shape), pipeline_mode=pl.Buffered(1))


def rows_of(tile, width):
    return pl.BlockSpec((tile, width), lambda i: (i, 0))


def project_kernel(x_ref, mask_ref, win_ref, w0_ref, vec_ref, a_ref, h_ref, hb_ref, t_ref):
    hat, _ = norm_parts(x_ref[...].astype(F32))
    normed = (hat * vec_ref[0:1, :CH].astype(F32) + vec_ref[1:2, :CH].astype(F32)).astype(BF16)
    a_ref[...] = normed
    hidden = product(normed, win_ref[...]) + vec_ref[2:3, :D].astype(F32)
    hidden = jnp.where(mask_ref[...] > 0.0, vec_ref[3:4, :D].astype(F32), hidden)
    h_ref[...] = hidden
    low = hidden.astype(BF16)
    hb_ref[...] = low
    t_ref[:, :D] = (
        product(low, w0_ref[:, :D]) + vec_ref[4:5, :D].astype(F32)
    ).astype(BF16)
    t_ref[:, D : 2 * D] = product(low, w0_ref[:, D : 2 * D]).astype(BF16)
    t_ref[:, 2 * D : 3 * D] = (
        product(low, w0_ref[:, 2 * D : 3 * D]) + vec_ref[5:6, :D].astype(F32)
    ).astype(BF16)


def project(x, masked, win, w0, vecs, tile):
    n = x.shape[0]
    return pl.pallas_call(
        project_kernel,
        grid=(n // tile,),
        in_specs=[
            rows_of(tile, CH),
            rows_of(tile, 1),
            whole((CH, D)),
            whole((D, FF)),
            whole((NVEC, FF)),
        ],
        out_specs=[rows_of(tile, CH), rows_of(tile, D), rows_of(tile, D), rows_of(tile, 3 * D)],
        out_shape=[
            jax.ShapeDtypeStruct((n, CH), BF16),
            jax.ShapeDtypeStruct((n, D), F32),
            jax.ShapeDtypeStruct((n, D), BF16),
            jax.ShapeDtypeStruct((n, 3 * D), BF16),
        ],
        compiler_params=params(),
        name="project",
    )(x, masked, win, w0, vecs)


def half_masks():
    lane = lax.broadcasted_iota(jnp.int32, (1, 128), 1)
    return [(lane < HEAD_DIM).astype(BF16), (lane >= HEAD_DIM).astype(BF16)]


def attend_kernel(len_ref, q_ref, k_ref, v_ref, o_ref):
    length = len_ref[pl.program_id(0)]
    shift = jnp.where(lax.broadcasted_iota(jnp.int32, (1, LEN), 1) < length, 0.0, -1e30)
    keys = k_ref[...]
    total = None
    for half in half_masks():
        scores = product_nt(q_ref[...] * half, keys) * HEAD_DIM ** (-0.5) + shift
        power = jnp.exp(scores - jnp.max(scores, -1, keepdims=True))
        probs = (power * (1.0 / jnp.sum(power, -1, keepdims=True))).astype(BF16)
        part = product(probs, v_ref[...] * half)
        total = part if total is None else total + part
    o_ref[...] = total.astype(BF16)


def attend(lengths, triple):
    n = triple.shape[0]
    pairs = D // 128
    return pl.pallas_call(
        attend_kernel,
        grid_spec=pltpu.PrefetchScalarGridSpec(
            num_scalar_prefetch=1,
            grid=(n // LEN, pairs),
            in_specs=[
                pl.BlockSpec((LEN, 128), lambda u, j, _: (u, j)),
                pl.BlockSpec((LEN, 128), lambda u, j, _: (u, pairs + j)),
                pl.BlockSpec((LEN, 128), lambda u, j, _: (u, 2 * pairs + j)),
            ],
            out_specs=pl.BlockSpec((LEN, 128), lambda u, j, _: (u, j)),
        ),
        out_shape=jax.ShapeDtypeStruct((n, D), BF16),
        compiler_params=params(),
        name="attend",
    )(lengths, triple, triple, triple)


def feed_kernel(
    scale_ref,
    att_ref,
    h_ref,
    mask_ref,
    label_ref,
    w0_ref,
    wu_ref,
    wd_ref,
    wh_ref,
    cu_ref,
    vec_ref,
    loss_ref,
    z1_ref,
    act_ref,
    de_ref,
    df_ref,
    z2_ref,
    dc_ref,
    dlog_ref,
    uc_ref,
    dr1_ref,
    dy_ref,
    do_ref,
    gv_ref,
    slope_ref,
):
    @pl.when(pl.program_id(0) == 0)
    def _():
        gv_ref[...] = jnp.zeros_like(gv_ref)
        loss_ref[...] = jnp.zeros_like(loss_ref)

    def vec(row, width=D):
        return vec_ref[row : row + 1, :width].astype(F32)

    masked = mask_ref[...]
    wo = w0_ref[:, 3 * D :]
    resid_one = h_ref[...] + product(att_ref[...], wo) + vec(6)
    hat_one, root_one = norm_parts(resid_one)
    first = hat_one * vec(7) + vec(8)
    first_low = first.astype(BF16)
    z1_ref[...] = first_low
    lowered = None
    for c in range(FF // D):
        cols = slice(c * D, (c + 1) * D)
        before = product(first_low, wu_ref[:, cols]) + vec_ref[9:10, cols].astype(F32)
        active, slope = gelu_pair(before)
        active = active.astype(BF16)
        act_ref[:, cols] = active
        slope_ref[:, cols] = slope
        part = product(active, wd_ref[cols, :])
        lowered = part if lowered is None else lowered + part
    resid_two = first + lowered + vec(10)
    hat_two, root_two = norm_parts(resid_two)
    second_low = (hat_two * vec(11) + vec(12)).astype(BF16)
    z2_ref[...] = second_low
    head = product_nt(second_low, wh_ref[...]) + vec(13, CD)
    root_head = lax.rsqrt(jnp.sum(head * head, -1, keepdims=True) + 1e-06)
    unit = head * root_head
    unit_low = unit.astype(BF16)
    uc_ref[...] = unit_low
    logits = temper * product(unit_low, cu_ref[...])
    code = lax.broadcasted_iota(jnp.int32, logits.shape, 1)
    logits = jnp.where(code < CODES, logits, -1e30)
    top = jnp.max(logits, -1, keepdims=True)
    power = jnp.exp(logits - top)
    total = jnp.sum(power, -1, keepdims=True)
    onehot = code == label_ref[...]
    picked = jnp.sum(jnp.where(onehot, logits, 0.0), -1, keepdims=True)
    losses = top + jnp.log(total) - picked
    loss_ref[...] += jnp.sum(jnp.where(masked > 0.0, losses, 0.0), 0, keepdims=True)
    chances = power * (1.0 / total)
    d_logit = (
        temper
        * (
            jnp.where(masked > 0.0, chances - jnp.where(onehot, 1.0, 0.0), 0.0)
            * scale_ref[0]
        )
    ).astype(BF16)
    dlog_ref[...] = d_logit
    d_unit = product_nt(d_logit, cu_ref[...])
    d_head = (root_head * (d_unit - unit * jnp.sum(d_unit * unit, -1, keepdims=True))).astype(BF16)
    dc_ref[...] = d_head
    gv_ref[13:14, :CD] += column_sum(d_head.astype(F32))
    d_second = product(d_head, wh_ref[...])
    gv_ref[11:12, :D] += column_sum(d_second * hat_two)
    gv_ref[12:13, :D] += column_sum(d_second)
    d_resid_two = norm_back(d_second, hat_two, root_two, vec(11))
    d_lower = d_resid_two.astype(BF16)
    df_ref[...] = d_lower
    gv_ref[10:11, :D] += column_sum(d_lower.astype(F32))
    d_first = d_resid_two
    for c in range(FF // D):
        cols = slice(c * D, (c + 1) * D)
        d_before = (slope_ref[:, cols] * product_nt(d_lower, wd_ref[cols, :])).astype(BF16)
        de_ref[:, cols] = d_before
        gv_ref[9:10, cols] += column_sum(d_before.astype(F32))
        d_first = d_first + product_nt(d_before, wu_ref[:, cols])
    gv_ref[7:8, :D] += column_sum(d_first * hat_one)
    gv_ref[8:9, :D] += column_sum(d_first)
    d_resid_one = norm_back(d_first, hat_one, root_one, vec(7))
    dr1_ref[...] = d_resid_one
    d_branch = d_resid_one.astype(BF16)
    dy_ref[...] = d_branch
    gv_ref[6:7, :D] += column_sum(d_branch.astype(F32))
    do_ref[...] = product_nt(d_branch, wo).astype(BF16)


def feed(scale, att, hidden, masked, label, w0, wu, wd, wh, cu, vecs, tile):
    n = att.shape[0]
    outs = [
        (D, BF16),
        (FF, BF16),
        (FF, BF16),
        (D, BF16),
        (D, BF16),
        (CD, BF16),
        (CPAD, BF16),
        (CD, BF16),
        (D, F32),
        (D, BF16),
        (D, BF16),
    ]
    return pl.pallas_call(
        feed_kernel,
        grid=(n // tile,),
        in_specs=[
            pl.BlockSpec(memory_space=pltpu.SMEM),
            rows_of(tile, D),
            rows_of(tile, D),
            rows_of(tile, 1),
            rows_of(tile, 1),
            whole((D, FF)),
            whole((D, FF)),
            whole((FF, D)),
            whole((CD, D)),
            whole((CD, CPAD)),
            whole((NVEC, FF)),
        ],
        out_specs=[pl.BlockSpec((1, 1), lambda i: (0, 0))]
        + [rows_of(tile, width) for width, _ in outs]
        + [pl.BlockSpec((16, FF), lambda i: (0, 0))],
        out_shape=[jax.ShapeDtypeStruct((1, 1), F32)]
        + [jax.ShapeDtypeStruct((n, width), kind) for width, kind in outs]
        + [jax.ShapeDtypeStruct((16, FF), F32)],
        scratch_shapes=[pltpu.VMEM((tile, FF), F32)],
        compiler_params=params(),
        name="feed",
    )(scale, att, hidden, masked, label, w0, wu, wd, wh, cu, vecs)


MESH = pl.DeviceIdType.MESH


def ceil_to(value, step):
    return -(-value // step) * step


class Chunk:
    def __init__(self, rows, group, slot, sum_slot, wide_xy, wide_z):
        self.used = sum(rows)
        self.starts = [sum(rows[:i]) for i in range(len(rows))]
        self.rows = ceil_to(self.used, 16 * group)
        self.part = self.rows // group
        self.slot = slot
        self.sum_slot = sum_slot
        self.kind_xy = F32 if wide_xy else BF16
        self.kind_z = F32 if wide_z else BF16


HEAD_SLOT = 2


def gradient_chunks(groups, shards):
    down, band = FF // shards, D // shards
    half = down // 2
    return [
        Chunk([half], groups, 0, 0, False, True),
        Chunk([half], groups, 1, 1, False, True),
        Chunk([CD // shards] * 2, groups, HEAD_SLOT, 4, True, True),
        Chunk([band] * 2, groups, 0, 2, False, False),
        Chunk([band] * 2, groups, 1, 3, False, False),
        Chunk([band] * 2, groups, 0, 0, False, False),
        Chunk([band] * 2, groups, 1, 1, False, False),
        Chunk([CH // shards, 16], groups, 0, 5, False, True),
    ]


def tiles(rows, step, body):
    def once(i, carry):
        body(pl.ds(pl.multiple_of(i * step, step), step))
        return carry

    lax.fori_loop(0, rows // step, once, 0)


def backward_kernel(chunks, groups, shards, *refs):
    chips = shards // 2
    n = len(chunks)
    refs = list(refs)

    def take(count):
        out = refs[:count]
        del refs[:count]
        return out

    (
        act_hbm,
        df_hbm,
        z1_hbm,
        de_hbm,
        z2_hbm,
        dc_hbm,
        uc_hbm,
        dlog_hbm,
        triple_hbm,
        datt_hbm,
        hid_hbm,
        att_hbm,
        dy_hbm,
        a_hbm,
        dr1_hbm,
        x_hbm,
        w0_hbm,
        win_hbm,
        flag_ref,
        gvin_ref,
        code_ref,
        loss_ref,
    ) = take(22)
    ring = take(n)
    (stat_ref,) = take(1)
    pool, heads, dr1_ref, gv_ref = take(4)
    full = take(3)
    pair = take(3)
    send_xy, recv_xy = take(n), take(n)
    acc = take(6)
    send_z, recv_z = take(n), take(n)
    loss_all, stat_all = take(2)
    (
        load_sems,
        core_sems,
        credit,
        xy_sems,
        z_sems,
        right_sems,
        left_sems,
        loss_sems,
        stat_sems,
    ) = take(9)

    g = lax.axis_index("group")
    s = lax.axis_index("shard")
    core = lax.rem(s, 2)
    chip = s // 2
    sibling = s + 1 - 2 * core
    parts = FF // D
    frames = flag_ref.shape[0]

    def load(src, dst, sem):
        return pltpu.make_async_copy(src, dst, load_sems.at[sem])

    def cols(ref, c):
        return ref.at[:, c * D : (c + 1) * D]

    loads = {
        "df": load(df_hbm, pool.at[0], 0),
        "z1": load(z1_hbm, pool.at[3], 3),
        "z2": load(z2_hbm, heads.at[0], 8),
        "dc": load(dc_hbm, heads.at[1, :, 0:CD], 9),
        "uc": load(uc_hbm, heads.at[1, :, CD : 2 * CD], 10),
        "dlog": load(dlog_hbm, heads.at[2, :, 0:CPAD], 11),
        "hid": load(hid_hbm, pool.at[0], 0),
        "att": load(att_hbm, pool.at[4], 4),
        "dy": load(dy_hbm, pool.at[5], 5),
        "x": load(x_hbm, pool.at[5, :, 0:CH], 5),
        "win": load(win_hbm, pool.at[6, 0:CH], 6),
        "dr1": load(dr1_hbm, dr1_ref, 7),
        "q": load(cols(triple_hbm, 0), heads.at[0], 8),
        "k": load(cols(triple_hbm, 1), heads.at[1], 9),
        "v": load(cols(triple_hbm, 2), heads.at[2], 11),
        "do": load(datt_hbm, heads.at[3], 12),
        "a": load(a_hbm, heads.at[3, :, 0:CH], 12),
    }
    for c in range(parts):
        loads["act", c] = load(cols(act_hbm, c), pool.at[1 + c % 2], 1 + c % 2)
        loads["de", c] = load(cols(de_hbm, c), pool.at[1 + c % 2], 1 + c % 2)
    for c in range(3):
        loads["w", c] = load(cols(w0_hbm, c), pool.at[1 + c, 0:D], 1 + c)

    def fetch(*names):
        for name in names:
            loads[name].start()

    def ready(*names):
        for name in names:
            loads[name].wait()

    fetch("df", ("act", 0), ("act", 1), "z2", "dc", "uc", "dlog", "z1", "dr1")

    barrier = pltpu.get_barrier_semaphore()
    for e in range(1, shards):
        pl.semaphore_signal(
            barrier, 1, device_id=(g, lax.rem(s + e, shards)), device_id_type=MESH
        )
    for e in range(1, groups):
        pl.semaphore_signal(
            barrier, 1, device_id=(lax.rem(g + e, groups), s), device_id_type=MESH
        )
    pl.semaphore_wait(barrier, shards - 1 + groups - 1)

    def remote(src, dst, send_sem, recv_sem, device):
        return pltpu.make_async_remote_copy(
            src_ref=src,
            dst_ref=dst,
            send_sem=send_sem,
            recv_sem=recv_sem,
            device_id=device,
            device_id_type=MESH,
        )

    def loss_copy(e):
        return remote(
            loss_ref,
            loss_all.at[g],
            loss_sems.at[0, e],
            loss_sems.at[1, e],
            (lax.rem(g + e, groups), s),
        )

    for e in range(1, groups):
        loss_copy(e).start()
    loss_all[g] = loss_ref[...]

    def core_copy(t):
        c = chunks[t]
        return remote(
            full[c.slot].at[:, 1 - core, 0 : c.used],
            pair[c.slot].at[:, 0 : c.used],
            core_sems.at[0, t],
            core_sems.at[1, t],
            (g, sibling),
        )

    before = {}
    for t, c in enumerate(chunks):
        earlier = [i for i in range(t) if chunks[i].slot == c.slot]
        before[t] = earlier[-1] if earlier else None
    last_of = {c.slot: t for t, c in enumerate(chunks)}

    def free_buffer(t):
        if before[t] is not None:
            core_copy(before[t]).wait_send()

    def stage_pair(t):
        if before[t] is not None:
            pl.semaphore_wait(credit.at[chunks[t].slot], 1)
        core_copy(t).start()

    def chip_at(d):
        return lax.rem(chip + d, chips)

    def xy_copy(t, d):
        return remote(
            send_xy[t].at[d - 1],
            recv_xy[t].at[d - 1],
            xy_sems.at[0, t, d],
            xy_sems.at[1, t, d],
            (g, 2 * chip_at(d) + core),
        )

    def stage_chips(t):
        c = chunks[t]
        own, other = full[c.slot], pair[c.slot]
        core_copy(t).wait_recv()
        for d in list(range(1, chips)) + [0]:
            q = chip_at(d)
            if d == 0:

                def keep(rows):
                    acc[c.sum_slot][rows] = own[q, core, rows] + other[q, rows]

                tiles(c.used, 16, keep)
                if c.rows > c.used:
                    acc[c.sum_slot][c.used : c.rows] = jnp.zeros((c.rows - c.used, D), F32)
            else:

                def send(rows):
                    send_xy[t][d - 1, rows] = (own[q, core, rows] + other[q, rows]).astype(
                        c.kind_xy
                    )

                tiles(c.used, 16, send)
                xy_copy(t, d).start()
        if t != last_of[c.slot]:
            pl.semaphore_signal(
                credit.at[c.slot], 1, device_id=(g, sibling), device_id_type=MESH
            )

    def z_copy(t, e):
        return remote(
            send_z[t].at[e - 1],
            recv_z[t].at[e - 1],
            z_sems.at[0, t, e],
            z_sems.at[1, t, e],
            (lax.rem(g + e, groups), s),
        )

    def stage_group(t):
        c = chunks[t]
        total_ref = acc[c.sum_slot]
        for d in range(1, chips):
            xy_copy(t, d).wait_recv()

        def add(rows):
            total = total_ref[rows]
            for d in range(1, chips):
                total = total + recv_xy[t][d - 1, rows].astype(F32)
            total_ref[rows] = total

        tiles(c.used, 16, add)
        for e in range(1, groups):
            base = pl.multiple_of(lax.rem(g + e, groups) * c.part, 16)

            def send(rows):
                here = pl.ds(pl.multiple_of(base + rows.start, 16), 16)
                send_z[t][e - 1, rows] = total_ref[here].astype(BF16)

            tiles(c.part, 16, send)
            z_copy(t, e).start()

    def part_rows(t, p):
        return pl.ds(pl.multiple_of(p * chunks[t].part, 16), chunks[t].part)

    def ring_copy(t, k, way, back=0):
        p = g - k if way == 0 else g + k
        side = lax.rem(g + 1, groups) if way == 0 else lax.rem(g + groups - 1, groups)
        sems = right_sems if way == 0 else left_sems
        rows = part_rows(t, p)
        return remote(
            ring[t].at[rows],
            ring[t].at[rows],
            sems.at[0, t, k],
            sems.at[1, t, k - back],
            (side, s),
        )

    def holds(k, way):
        return g >= k if way == 0 else g + k < groups

    def sends(k, way):
        return (g >= k) & (g < groups - 1) if way == 0 else (g + k < groups) & (g > 0)

    def stage_total(t):
        c = chunks[t]
        total_ref = acc[c.sum_slot]
        for e in range(1, groups):
            z_copy(t, e).wait_recv()
        base = pl.multiple_of(g * c.part, 16)

        def add(rows):
            here = pl.ds(pl.multiple_of(base + rows.start, 16), 16)
            total = total_ref[here]
            for e in range(1, groups):
                total = total + recv_z[t][e - 1, rows].astype(F32)
            ring[t][here] = total.astype(c.kind_z)

        tiles(c.part, 16, add)
        for way in (0, 1):

            @pl.when(sends(0, way))
            def _():
                ring_copy(t, 0, way).start()

    def stage_ring(t, k):
        for way in (0, 1):

            @pl.when(holds(k, way))
            def _():
                ring_copy(t, k, way, 1).wait_recv()

            if k < groups - 1:

                @pl.when(sends(k, way))
                def _():
                    ring_copy(t, k, way).start()

    def stage_end(t, squares):
        c = chunks[t]

        def once(i, total):
            value = ring[t][pl.ds(pl.multiple_of(i * 16, 16), 16)].astype(F32)
            value = value * value
            return total + value[:8] + value[8:]

        return lax.fori_loop(0, c.rows // 16, once, squares)

    done = [0] * n
    squares = [jnp.zeros((8, D), F32)]

    def step(t):
        now = done[t]
        done[t] += 1
        if now == 0:
            stage_pair(t)
        elif now == 1:
            stage_chips(t)
        elif now == 2:
            stage_group(t)
        elif now == 3:
            stage_total(t)
        elif now < 3 + groups:
            stage_ring(t, now - 3)
        else:
            squares[0] = stage_end(t, squares[0])

    def scatter(value, slots, at, per, first_shard):
        count = value.shape[0] // per
        each = per // len(slots)
        for k in range(count):
            shard = first_shard * 1 + k
            for i, slot in enumerate(slots):
                rows = value[k * per + i * each : k * per + (i + 1) * each]
                full[slot][shard // 2, lax.rem(shard, 2), at : at + each, 0 : rows.shape[1]] = rows

    def grad(left, right, slots, at, per, block):
        width = left.shape[1]

        def once(i, carry):
            some = left[:, pl.ds(pl.multiple_of(i * block, 128), block)]
            scatter(product_tn(some, right[...]), slots, at, per, i * (block // per))
            return carry

        lax.fori_loop(0, width // block, once, 0)

    down, band, deep, first = FF // shards, D // shards, CD // shards, CH // shards
    wide = FF // shards
    pairs = D // 128

    ready("df")
    for c in range(parts):
        ready(("act", c))
        for i in range(2):
            value = product_tn(
                pool[1 + c % 2, :, i * (D // 2) : (i + 1) * (D // 2)], pool[0]
            )
            scatter(value, [0, 1], 0, down, (c * D + i * (D // 2)) // down)
        if c + 2 < parts:
            fetch(("act", c + 2))
        else:
            fetch(("de", c - 2))
    step(0)
    step(1)
    fetch("hid")
    ready("z2", "dc", "uc", "dlog")
    scatter(product_tn(heads[1, :, 0:CD], heads[0]), [HEAD_SLOT], 0, deep, 0)
    d_unit = product_tn(heads[1, :, CD : 2 * CD], heads[2, :, 0:CPAD])
    codes = code_ref[...]
    root = lax.rsqrt(jnp.sum(codes * codes, 0, keepdims=True) + 1e-06)
    unit = codes * root
    d_codes = root * (d_unit - unit * jnp.sum(d_unit * unit, 0, keepdims=True))
    scatter(d_codes, [HEAD_SLOT], deep, deep, 0)
    full[HEAD_SLOT][:, :, deep : 2 * deep, CPAD:D] = jnp.zeros((chips, 2, deep, D - CPAD), F32)
    step(2)
    fetch("q", "k", "v", "do", "att", "dy", "win")
    step(0)
    step(1)
    ready("z1")
    for t, first_part in ((3, 0), (4, 2)):
        free_buffer(t)
        for i in range(2):
            c = first_part + i
            ready(("de", c))
            grad(pool.at[3], pool.at[1 + c % 2], [chunks[t].slot], i * band, band, D // 2)
            if c + 2 < parts:
                fetch(("de", c + 2))
        step(t)
    for c in range(3):
        fetch(("w", c))

    halves = half_masks()

    def attention(i, carry):
        rows = pl.ds(pl.multiple_of((i // pairs) * LEN, LEN), LEN)
        lanes = pl.ds(pl.multiple_of(lax.rem(i, pairs) * 128, 128), 128)
        shift = flag_ref[rows, 1:2]
        keys, values = heads[1, rows, lanes], heads[2, rows, lanes]
        dq = dk = dv = None
        for half in halves:
            query = heads[0, rows, lanes] * half
            upstream = heads[3, rows, lanes] * half
            scores = product_nt(keys, query) * HEAD_DIM ** (-0.5) + shift
            power = jnp.exp(scores - jnp.max(scores, 0, keepdims=True))
            probs = power * (1.0 / jnp.sum(power, 0, keepdims=True))
            part_v = product(probs.astype(BF16), upstream)
            d_probs = product_nt(values, upstream)
            weight = jnp.sum(probs * d_probs, 0, keepdims=True)
            d_scores = (probs * (d_probs - weight) * HEAD_DIM ** (-0.5)).astype(BF16)
            part_k = product(d_scores, query)
            part_q = product_tn(d_scores, keys * half)
            dq = part_q if dq is None else dq + part_q
            dk = part_k if dk is None else dk + part_k
            dv = part_v if dv is None else dv + part_v
        heads[0, rows, lanes] = dq.astype(BF16)
        heads[1, rows, lanes] = dk.astype(BF16)
        heads[2, rows, lanes] = dv.astype(BF16)
        return carry

    ready("q", "k", "v", "do")
    rounds = (frames // LEN) * pairs
    plan = [(3, 4, 2), (0,), (1, 0), (0, 1), (0, 1)]
    cut = [rounds * i // len(plan) for i in range(len(plan) + 1)]
    for i, some in enumerate(plan):
        lax.fori_loop(cut[i], cut[i + 1], attention, 0)
        for t in some:
            step(t)
    fetch("a")

    ready("hid", "att", "dy")
    free_buffer(5)
    grad(pool.at[0], heads.at[0], [0], 0, band, D // 2)
    grad(pool.at[0], heads.at[1], [0], band, band, D // 2)
    step(5)
    free_buffer(6)
    grad(pool.at[0], heads.at[2], [1], 0, band, D // 2)
    grad(pool.at[4], pool.at[5], [1], band, band, D // 2)
    step(6)
    fetch("x")
    step(5)
    step(3)
    step(6)
    ready(("w", 0), ("w", 1), ("w", 2), "win", "dr1", "x")

    gv_ref[...] = gvin_ref[...]

    def back(i, carry):
        rows = pl.ds(pl.multiple_of(i * 256, 256), 256)
        dq, dk, dv = heads[0, rows], heads[1, rows], heads[2, rows]
        gv_ref[4:5, :D] += column_sum(dq.astype(F32))
        gv_ref[5:6, :D] += column_sum(dv.astype(F32))
        d_hidden = (
            dr1_ref[rows]
            + product_nt(dq, pool[1, 0:D])
            + product_nt(dk, pool[2, 0:D])
            + product_nt(dv, pool[3, 0:D])
        )
        masked = flag_ref[rows, 0:1] > 0.0
        gv_ref[3:4, :D] += column_sum(jnp.where(masked, d_hidden, 0.0))
        d_proj = jnp.where(masked, 0.0, d_hidden).astype(BF16)
        pool[4, rows] = d_proj
        gv_ref[2:3, :D] += column_sum(d_proj.astype(F32))
        d_normed = product_nt(d_proj, pool[6, 0:CH])
        hat, _ = norm_parts(pool[5, rows, 0:CH].astype(F32))
        gv_ref[0:1, :CH] += column_sum(d_normed * hat)
        gv_ref[1:2, :CH] += column_sum(d_normed)
        return carry

    lax.fori_loop(0, frames // 256, back, 0)
    ready("a")
    free_buffer(7)
    grad(heads.at[3, :, 0:CH], pool.at[4], [0], 0, first, CH // 2)
    for b in range(shards):
        full[0][b // 2, b % 2, first : first + 16, 0:wide] = gv_ref[:, b * wide : (b + 1) * wide]
        full[0][b // 2, b % 2, first : first + 16, wide:D] = jnp.zeros((16, D - wide), F32)
    step(7)
    step(4)
    step(7)
    order = [0, 1, 3, 4, 2, 5, 6, 7]
    final = 4 + groups
    while min(done) < final:
        for i, t in enumerate(order):
            ahead = [done[u] for u in order[:i]]
            if done[t] < final and all(d > done[t] for d in ahead if d < final):
                step(t)

    for e in range(1, groups):
        loss_copy(e).wait_recv()
    loss = loss_all[0]
    for p in range(1, groups):
        loss = loss + loss_all[p]
    lane = lax.broadcasted_iota(jnp.int32, (8, 128), 1)
    stat_ref[...] = jnp.where(lane == 0, jnp.sum(squares[0]), loss)

    def stat_copy(e):
        return remote(
            stat_ref,
            stat_all.at[s],
            stat_sems.at[0, e],
            stat_sems.at[1, e],
            (g, lax.rem(s + e, shards)),
        )

    for e in range(1, shards):
        stat_copy(e).start()
    stat_all[s] = stat_ref[...]
    for e in range(1, shards):
        stat_copy(e).wait_recv()
    for t in range(n):
        if t == last_of[chunks[t].slot]:
            core_copy(t).wait_send()
        for d in range(1, chips):
            xy_copy(t, d).wait_send()
        for e in range(1, groups):
            z_copy(t, e).wait_send()
        for k in range(groups - 1):
            for way in (0, 1):

                @pl.when(sends(k, way))
                def _():
                    ring_copy(t, k, way).wait_send()

    for e in range(1, groups):
        loss_copy(e).wait_send()
    for e in range(1, shards):
        stat_copy(e).wait_send()
    total = stat_all[0]
    for p in range(1, shards):
        total = total + stat_all[p]
    stat_ref[...] = total


def backward(groups, shards, operands, small):
    chunks = gradient_chunks(groups, shards)
    chips = shards // 2
    n = len(chunks)
    frames = operands[0].shape[0]
    hbm = pl.BlockSpec(memory_space=pl.ANY)
    vmem = pl.BlockSpec(memory_space=pltpu.VMEM)
    dma = pltpu.SemaphoreType.DMA
    deepest = [max(c.used for c in chunks if c.slot == i) for i in range(3)]
    sums = [max(c.rows for c in chunks if c.sum_slot == i) for i in range(6)]
    results = pl.pallas_call(
        functools.partial(backward_kernel, chunks, groups, shards),
        in_specs=[hbm] * len(operands) + [vmem] * len(small),
        out_specs=[vmem] * (n + 1),
        out_shape=[jax.ShapeDtypeStruct((c.rows, D), c.kind_z) for c in chunks]
        + [jax.ShapeDtypeStruct((8, 128), F32)],
        scratch_shapes=[
            pltpu.VMEM((7, frames, D), BF16),
            pltpu.VMEM((4, frames, D), BF16),
            pltpu.VMEM((frames, D), F32),
            pltpu.VMEM((16, FF), F32),
        ]
        + [pltpu.VMEM((chips, 2, rows, D), F32) for rows in deepest]
        + [pltpu.VMEM((chips, rows, D), F32) for rows in deepest]
        + [pltpu.VMEM((chips - 1, c.used, D), c.kind_xy) for c in chunks] * 2
        + [pltpu.VMEM((rows, D), F32) for rows in sums]
        + [pltpu.VMEM((groups - 1, c.part, D), BF16) for c in chunks] * 2
        + [pltpu.VMEM((groups, 8, 128), F32), pltpu.VMEM((shards, 8, 128), F32)]
        + [
            dma((13,)),
            dma((2, n)),
            pltpu.SemaphoreType.REGULAR((3,)),
            dma((2, n, chips)),
            dma((2, n, groups)),
            dma((2, n, groups)),
            dma((2, n, groups)),
            dma((2, groups)),
            dma((2, shards)),
        ],
        compiler_params=pltpu.CompilerParams(
            collective_id=1, has_side_effects=True, vmem_limit_bytes=64 * 1024 * 1024 - 65536
        ),
        name="backward",
    )(*operands, *small)
    return results[:n], results[n]


def adam_step(weight, grad, moment, square, shrink, scal_ref):
    grad = grad * scal_ref[0]
    moment = beta_one * moment + (1.0 - beta_one) * grad
    square = beta_two * square + (1.0 - beta_two) * grad * grad
    stepped = moment / scal_ref[1] / (jnp.sqrt(square / scal_ref[2]) + adam_eps)
    return weight - rate * (stepped + shrink * weight), moment, square


def adam_kernel(scal_ref, *refs):
    w, m, v = refs[0:5], refs[5:10], refs[10:15]
    g_in, g_qkvo, g_up, g_down, g_head, g_vec = refs[15:21]
    outs = [refs[21 + 5 * i : 26 + 5 * i] for i in range(4)]

    def update(i, grad, where=...):
        shrink = 0.0 if i == 4 else decay
        new = adam_step(w[i][where], grad, m[i][where], v[i][where], shrink, scal_ref)
        for out, value in zip(outs, new):
            out[i][where] = value
        outs[3][i][where] = new[0].astype(BF16)

    update(1, g_qkvo[...].astype(F32), 0)
    update(1, g_up[...].astype(F32), 1)
    update(2, g_down[...])

    @pl.when(pl.program_id(0) == 0)
    def _():
        update(0, g_in[...])
        update(3, g_head[...])
        update(4, g_vec[...])


def adam(scalars, weights, moments, seconds, grads):
    parts = FF // D
    depth = weights[1].shape[1]
    tall = weights[2].shape[0] // parts

    def fixed(a):
        return pl.BlockSpec(a.shape, lambda i: (0,) * a.ndim)

    w_specs = [
        fixed(weights[0]),
        pl.BlockSpec((2, depth, D), lambda i: (0, 0, i)),
        pl.BlockSpec((tall, D), lambda i: (i, 0)),
        fixed(weights[3]),
        fixed(weights[4]),
    ]
    band = pl.BlockSpec((depth, D), lambda i: (i, 0))
    g_specs = [fixed(grads[0]), band, band, w_specs[2], fixed(grads[4]), fixed(grads[5])]
    shapes = [jax.ShapeDtypeStruct(w.shape, F32) for w in weights]
    low = [jax.ShapeDtypeStruct(w.shape, BF16) for w in weights]
    outs = pl.pallas_call(
        adam_kernel,
        grid=(parts,),
        in_specs=[pl.BlockSpec(memory_space=pltpu.SMEM)] + w_specs * 3 + g_specs,
        out_specs=w_specs * 4,
        out_shape=shapes * 3 + low,
        compiler_params=params(),
        name="adam",
    )(scalars, *weights, *moments, *seconds, *grads)
    return [outs[i * 5 : (i + 1) * 5] for i in range(4)]


def span_mask(length, begins):
    position = jnp.arange(LEN, dtype=jnp.int32)
    first = begins % (length - SPAN + 1)
    inside = (position[None, :] >= first[:, None]) & (position[None, :] < first[:, None] + SPAN)
    return jnp.any(inside, 0) & (position < length)


def per_device(
    features,
    lengths,
    starts,
    labels,
    step_count,
    weight_in,
    weight_rows,
    weight_down,
    weight_head,
    vectors,
    moment_in,
    moment_rows,
    moment_down,
    moment_head,
    moment_vectors,
    second_in,
    second_rows,
    second_down,
    second_head,
    second_vectors,
):
    masters = (weight_in, weight_rows, weight_down, weight_head, vectors)
    moments = (moment_in, moment_rows, moment_down, moment_head, moment_vectors)
    seconds = (second_in, second_rows, second_down, second_head, second_vectors)
    utters = features.shape[0]
    n = utters * LEN
    masked = jax.vmap(span_mask)(lengths, starts)
    count = lax.psum(jnp.sum(masked.astype(F32)), ("group", "shard"))
    scale = jnp.reshape(1.0 / count, (1,))
    masked = masked.astype(F32).reshape(n, 1)
    label = labels.reshape(n, 1)
    x = features.reshape(n, CH)
    low = tuple(w.astype(BF16) for w in masters)
    win = lax.all_gather(low[0], "shard", axis=0, tiled=True)
    vecs = lax.all_gather(low[4], "shard", axis=1, tiled=True)
    w0 = lax.all_gather(low[1][0], "shard", axis=0, tiled=True)
    wu = lax.all_gather(low[1][1], "shard", axis=0, tiled=True)
    wd = lax.all_gather(low[2], "shard", axis=0, tiled=True)
    whead = lax.all_gather(low[3].T, "shard", axis=0, tiled=True)
    wh = whead[:, :D]
    codes = jnp.pad(whead[:, D:].astype(F32), ((0, 0), (0, CPAD - CODES)))
    codes_root = lax.rsqrt(jnp.sum(codes * codes, 0, keepdims=True) + 1e-06)
    codes_unit = codes * codes_root
    cu = codes_unit.astype(BF16)

    a, hidden, hid_low, triple = project(x, masked, win, w0, vecs, 256)
    att = attend(lengths, triple)
    loss, z1, act, de, df, z2, dc, dlog, uc, dr1, dy, d_att, gv = feed(
        scale, att, hidden, masked, label, w0, wu, wd, wh, cu, vecs, 256
    )
    groups, shards = lax.axis_size("group"), lax.axis_size("shard")
    position = lax.broadcasted_iota(jnp.int32, (utters, LEN), 1)
    shift = jnp.where(position < lengths[:, None], 0.0, -1e30).reshape(n, 1)
    sums, stat = backward(
        groups,
        shards,
        [act, df, z1, de, z2, dc, uc, dlog, triple, d_att, hid_low, att, dy, a, dr1, x, w0, win],
        [jnp.concatenate([masked, shift], 1), gv, codes, jnp.broadcast_to(loss, (8, 128))],
    )
    norm = jnp.sqrt(stat[0, 0])
    loss = stat[0, 1] / count
    factor = jnp.minimum(1.0, clip_norm / (norm + 1e-06))
    steps = step_count[0].astype(F32)
    fix_one = 1.0 - jnp.power(beta_one, steps)
    fix_two = 1.0 - jnp.power(beta_two, steps)
    scalars = jnp.stack([factor, fix_one, fix_two])
    deep, band, first, wide = CD // shards, D // shards, CH // shards, FF // shards

    def bands(a, b):
        return jnp.concatenate([a[: 2 * band], b[: 2 * band]], 0)

    half = wide // 2
    summed = [
        sums[7][:first],
        bands(sums[5], sums[6]),
        bands(sums[3], sums[4]),
        jnp.concatenate([sums[0][:half], sums[1][:half]], 0),
        jnp.concatenate([sums[2][:deep], sums[2][deep : 2 * deep, :CODES]], 1),
        sums[7][first : first + NVEC, :wide],
    ]

    def turned(arrays):
        return [a.T if i == 3 else a for i, a in enumerate(arrays)]

    new_w, new_m, new_v, copies = (
        turned(out)
        for out in adam(scalars, turned(masters), turned(moments), turned(seconds), summed)
    )
    return (
        *new_w,
        *new_m,
        *new_v,
        *copies,
        jnp.reshape(loss, (1,)),
        jnp.reshape(norm, (1,)),
    )


def solution(mesh):
    weights = (
        P("shard", None),
        P(None, "shard", None),
        P("shard", None),
        P(None, "shard"),
        P(None, "shard"),
    )
    both = ("group", "shard")
    in_specs = (P(both, None, None), P(both), P(both, None), P(both, None), P()) + weights * 3
    out_specs = weights * 4 + (P(), P())
    return jax.shard_map(
        per_device, mesh=mesh, in_specs=in_specs, out_specs=out_specs, check_vma=False
    )
```

```python
import functools

import jax
import jax.numpy as jnp
from jax import lax
from jax.experimental import pallas as pl
from jax.experimental.pallas import tpu as pltpu
from jax.sharding import PartitionSpec as P

D = 768
CH = 512
HEADS = 12
HEAD_DIM = 64
FF = 3072
CD = 256
CODES = 500
CPAD = 512
LEN = 512
SPAN = 10
NVEC = 14

beta_one = 0.9
beta_two = 0.999
rate = 0.03
decay = 0.01
adam_eps = 1e-08
clip_norm = 0.01
temper = 10.0

F32 = jnp.float32
BF16 = jnp.bfloat16
VMEM_BYTES = 60 * 1024 * 1024


def product(left, right):
    return jnp.dot(left, right, preferred_element_type=F32)


def product_nt(left, right):
    return lax.dot_general(left, right, (((1,), (1,)), ((), ())), preferred_element_type=F32)


def product_tn(left, right):
    return lax.dot_general(left, right, (((0,), (0,)), ((), ())), preferred_element_type=F32)


def norm_parts(values):
    centred = values - jnp.mean(values, -1, keepdims=True)
    root = lax.rsqrt(jnp.mean(centred * centred, -1, keepdims=True) + 1e-05)
    return centred * root, root


def norm_back(upstream, hat, root, gain):
    scaled = upstream * gain
    return root * (
        scaled
        - jnp.mean(scaled, -1, keepdims=True)
        - hat * jnp.mean(scaled * hat, -1, keepdims=True)
    )


def column_sum(values):
    return jnp.sum(values, 0, keepdims=True)


def gelu_pair(e):
    root = 0.7071067811865476
    reach = jnp.abs(e) * root
    tail = jnp.exp(-0.5 * e * e)
    t = 1.0 / (1.0 + 0.3275911 * reach)
    poly = t * (
        0.254829592
        + t * (-0.284496736 + t * (1.421413741 + t * (-1.453152027 + t * 1.061405429)))
    )
    half = 0.5 * poly * tail
    phi = jnp.where(e < 0.0, half, 1.0 - half)
    return e * phi, phi + e * tail * 0.3989422804014327


def params(limit=VMEM_BYTES):
    return pltpu.CompilerParams(vmem_limit_bytes=limit)


def whole(shape):
    return pl.BlockSpec(shape, lambda *_: (0,) * len(shape), pipeline_mode=pl.Buffered(1))


def rows_of(tile, width):
    return pl.BlockSpec((tile, width), lambda i: (i, 0))


def half_masks():
    lane = lax.broadcasted_iota(jnp.int32, (1, 128), 1)
    return [(lane < HEAD_DIM).astype(BF16), (lane >= HEAD_DIM).astype(BF16)]


def feed_kernel(
    att_ref,
    h_ref,
    flag_ref,
    label_ref,
    wo_ref,
    wu_ref,
    wd_ref,
    head_ref,
    vec_ref,
    count_ref,
    loss_ref,
    z1_ref,
    act_ref,
    de_ref,
    df_ref,
    z2_ref,
    dc_ref,
    dlog_ref,
    uc_ref,
    dr1_ref,
    dy_ref,
    do_ref,
    gv_ref,
    slope_ref,
    cu_ref,
):
    @pl.when(pl.program_id(0) == 0)
    def _():
        gv_ref[...] = jnp.zeros_like(gv_ref)
        loss_ref[...] = jnp.zeros_like(loss_ref)
        codes = head_ref[:, D:].astype(F32)
        cu_ref[...] = (
            codes * lax.rsqrt(jnp.sum(codes * codes, 0, keepdims=True) + 1e-06)
        ).astype(BF16)

    def vec(row, width=D):
        return vec_ref[row : row + 1, :width]

    masked = flag_ref[:, 0:1]
    wo = wo_ref[...]
    wh = head_ref[:, :D]
    resid_one = h_ref[...] + product(att_ref[...], wo) + vec(6)
    hat_one, root_one = norm_parts(resid_one)
    first = hat_one * vec(7) + vec(8)
    first_low = first.astype(BF16)
    z1_ref[...] = first_low
    lowered = None
    for c in range(FF // D):
        cols = slice(c * D, (c + 1) * D)
        before = product(first_low, wu_ref[:, cols]) + vec_ref[9:10, cols]
        active, slope = gelu_pair(before)
        active = active.astype(BF16)
        act_ref[:, cols] = active
        slope_ref[:, cols] = slope
        part = product(active, wd_ref[cols, :])
        lowered = part if lowered is None else lowered + part
    resid_two = first + lowered + vec(10)
    hat_two, root_two = norm_parts(resid_two)
    second_low = (hat_two * vec(11) + vec(12)).astype(BF16)
    z2_ref[...] = second_low
    head = product_nt(second_low, wh) + vec(13, CD)
    root_head = lax.rsqrt(jnp.sum(head * head, -1, keepdims=True) + 1e-06)
    unit = head * root_head
    unit_low = unit.astype(BF16)
    uc_ref[...] = unit_low
    logits = temper * product(unit_low, cu_ref[...])
    code = lax.broadcasted_iota(jnp.int32, logits.shape, 1)
    logits = jnp.where(code < CODES, logits, -1e30)
    top = jnp.max(logits, -1, keepdims=True)
    power = jnp.exp(logits - top)
    total = jnp.sum(power, -1, keepdims=True)
    onehot = code == label_ref[...]
    picked = jnp.sum(jnp.where(onehot, logits, 0.0), -1, keepdims=True)
    losses = top + jnp.log(total) - picked
    loss_ref[...] += jnp.sum(jnp.where(masked > 0.0, losses, 0.0), 0, keepdims=True)
    chances = power * (1.0 / total)
    d_logit = (
        temper
        * (
            jnp.where(masked > 0.0, chances - jnp.where(onehot, 1.0, 0.0), 0.0)
            * (1.0 / count_ref[0:1, 0:1])
        )
    ).astype(BF16)
    dlog_ref[...] = d_logit
    d_unit = product_nt(d_logit, cu_ref[...])
    d_head = (root_head * (d_unit - unit * jnp.sum(d_unit * unit, -1, keepdims=True))).astype(BF16)
    dc_ref[...] = d_head
    gv_ref[13:14, :CD] += column_sum(d_head.astype(F32))
    d_second = product(d_head, wh)
    gv_ref[11:12, :D] += column_sum(d_second * hat_two)
    gv_ref[12:13, :D] += column_sum(d_second)
    d_resid_two = norm_back(d_second, hat_two, root_two, vec(11))
    d_lower = d_resid_two.astype(BF16)
    df_ref[...] = d_lower
    gv_ref[10:11, :D] += column_sum(d_lower.astype(F32))
    d_first = d_resid_two
    for c in range(FF // D):
        cols = slice(c * D, (c + 1) * D)
        d_before = (slope_ref[:, cols] * product_nt(d_lower, wd_ref[cols, :])).astype(BF16)
        de_ref[:, cols] = d_before
        gv_ref[9:10, cols] += column_sum(d_before.astype(F32))
        d_first = d_first + product_nt(d_before, wu_ref[:, cols])
    gv_ref[7:8, :D] += column_sum(d_first * hat_one)
    gv_ref[8:9, :D] += column_sum(d_first)
    d_resid_one = norm_back(d_first, hat_one, root_one, vec(7))
    dr1_ref[...] = d_resid_one
    d_branch = d_resid_one.astype(BF16)
    dy_ref[...] = d_branch
    gv_ref[6:7, :D] += column_sum(d_branch.astype(F32))
    do_ref[...] = product_nt(d_branch, wo).astype(BF16)


def feed(att, hidden, flags, label, wo, wu, wd, head, vecs, count, tile):
    n = att.shape[0]
    outs = [
        (D, BF16),
        (FF, BF16),
        (FF, BF16),
        (D, BF16),
        (D, BF16),
        (CD, BF16),
        (CPAD, BF16),
        (CD, BF16),
        (D, F32),
        (D, BF16),
        (D, BF16),
    ]
    return pl.pallas_call(
        feed_kernel,
        grid=(n // tile,),
        in_specs=[
            rows_of(tile, D),
            rows_of(tile, D),
            rows_of(tile, 2),
            rows_of(tile, 1),
            whole((D, D)),
            whole((D, FF)),
            whole((FF, D)),
            whole((CD, HEAD_COLS)),
            whole((16, FF)),
            whole((8, 128)),
        ],
        out_specs=[pl.BlockSpec((8, 128), lambda i: (0, 0))]
        + [rows_of(tile, width) for width, _ in outs]
        + [pl.BlockSpec((16, FF), lambda i: (0, 0))],
        out_shape=[jax.ShapeDtypeStruct((8, 128), F32)]
        + [jax.ShapeDtypeStruct((n, width), kind) for width, kind in outs]
        + [jax.ShapeDtypeStruct((16, FF), F32)],
        scratch_shapes=[pltpu.VMEM((tile, FF), F32), pltpu.VMEM((CD, CPAD), BF16)],
        compiler_params=params(),
        name="feed",
    )(att, hidden, flags, label, wo, wu, wd, head, vecs, count)


MESH = pl.DeviceIdType.MESH


def ceil_to(value, step):
    return -(-value // step) * step


class Part:
    def __init__(self, array, every, low, rows, col, cols):
        self.array, self.every, self.low, self.rows = array, every, low, rows
        self.col, self.cols = col, cols
        share = (rows * 2 // 5) // 16 * 16
        self.share = max(share, 16) if rows >= 32 else 0


HEAD_COLS = D + CPAD


def weight_parts(shards):
    band, down = D // shards, FF // shards
    third = down // 3
    return [
        Part(0, CH // shards, 0, CH // shards, 0, D),
        Part(1, band, 0, band, 0, 3 * D),
        Part(2, band, 0, band, 0, D),
        Part(5, CD // shards, 0, CD // shards, 0, HEAD_COLS),
        Part(3, band, 0, band, 0, 2 * D),
        Part(3, band, 0, band, 2 * D, 2 * D),
        Part(4, down, 0, third, 0, D),
        Part(4, down, third, third, 0, D),
        Part(4, down, 2 * third, third, 0, D),
    ]


def forward_kernel(parts, groups, shards, *refs):
    chips = shards // 2
    n = len(parts)
    refs = list(refs)

    def take(count):
        out = refs[:count]
        del refs[:count]
        return out

    x_ref, flag_ref, win_ref, rows_ref, down_ref, head_ref, vecs_ref, count_ref = take(8)
    out_w = take(6)
    (vec_out, total_ref, a_hbm, h_hbm, hb_hbm, t_hbm, att_hbm) = take(7)
    held = take(6)
    (vec_all, vec_ref, a_ref, h_ref, hb_ref, t_ref, att_ref, group_all, shard_all) = take(9)
    (xy_sems, z_sems, core_sems, vec_sems, group_sems, shard_sems, out_sems) = take(7)

    g = lax.axis_index("group")
    s = lax.axis_index("shard")
    core = lax.rem(s, 2)
    chip = s // 2
    sibling = s + 1 - 2 * core
    parity = lax.rem(g, 2)
    partner = g + 1 - 2 * parity
    frames = flag_ref.shape[0]
    band, first = D // shards, CH // shards
    wide = FF // shards

    barrier = pltpu.get_barrier_semaphore()
    for e in range(1, shards):
        pl.semaphore_signal(
            barrier, 1, device_id=(g, lax.rem(s + e, shards)), device_id_type=MESH
        )
    for e in range(1, groups):
        pl.semaphore_signal(
            barrier, 1, device_id=(lax.rem(g + e, groups), s), device_id_type=MESH
        )

    vec_all[s] = vecs_ref[...].astype(BF16)
    for ref, source, every in (
        (held[0], win_ref[...], first),
        (held[1], rows_ref[0, :, : 3 * D], band),
        (held[2], rows_ref[0, :, 3 * D :], band),
        (held[5], head_ref[...], CD // shards),
        (held[3], rows_ref[1], band),
        (held[4], down_ref[...], wide),
    ):
        ref[pl.ds(pl.multiple_of(s * every, 16), every)] = source.astype(BF16)
    pl.semaphore_wait(barrier, shards - 1 + groups - 1)

    def remote(ref, send_sem, recv_sem, device, dst=None):
        return pltpu.make_async_remote_copy(
            src_ref=ref,
            dst_ref=ref if dst is None else dst,
            send_sem=send_sem,
            recv_sem=recv_sem,
            device_id=device,
            device_id_type=MESH,
        )

    def region(i, shard, at, size):
        p = parts[i]
        rows = pl.ds(pl.multiple_of(shard * p.every + p.low + at, 16), size)
        return held[p.array].at[rows, p.col : p.col + p.cols]

    def chip_to(d):
        return lax.rem(chip + d, chips)

    def chip_from(d):
        return lax.rem(chip + chips - d, chips)

    def direct(i):
        return parity * parts[i].share, parts[i].rows - parts[i].share

    def xy_send(i, d):
        return remote(
            region(i, s, *direct(i)),
            xy_sems.at[0, i, d],
            xy_sems.at[1, i, d],
            (g, 2 * chip_to(d) + core),
        )

    def xy_here(i, d):
        return remote(
            region(i, 2 * chip_from(d) + core, *direct(i)),
            xy_sems.at[0, i, d],
            xy_sems.at[1, i, d],
            (g, 2 * chip_to(d) + core),
        )

    def z_copy(i, d, arriving):
        rest = parts[i].rows - parts[i].share
        start = (1 - parity if arriving else parity) * rest
        return remote(
            region(i, 2 * chip_from(d) + core, start, parts[i].share),
            z_sems.at[0, i, d],
            z_sems.at[1, i, d],
            (partner, s),
        )

    def core_copy(i, d, which, arriving):
        side = 1 - core if arriving else core
        shard = 2 * chip_from(d) + side
        if d == 0:
            span = (0, parts[i].rows)
        elif which == 0:
            span = direct(i)
        else:
            span = ((1 - parity) * (parts[i].rows - parts[i].share), parts[i].share)
        return remote(
            region(i, shard, *span),
            core_sems.at[0, i, d, which],
            core_sems.at[1, i, d, which],
            (g, sibling),
        )

    def vec_send(d):
        return remote(
            vec_all.at[s], vec_sems.at[0, d], vec_sems.at[1, d], (g, lax.rem(s + d, shards))
        )

    def vec_here(d):
        return remote(
            vec_all.at[lax.rem(s + shards - d, shards)],
            vec_sems.at[0, d],
            vec_sems.at[1, d],
            (g, lax.rem(s + d, shards)),
        )

    def group_copy(e):
        return remote(
            count_ref,
            group_sems.at[0, e],
            group_sems.at[1, e],
            (lax.rem(g + e, groups), s),
            group_all.at[g],
        )

    def shard_copy(e):
        return remote(
            total_ref,
            shard_sems.at[0, e],
            shard_sems.at[1, e],
            (g, lax.rem(s + e, shards)),
            shard_all.at[s],
        )

    for e in range(1, groups):
        group_copy(e).start()
    for d in range(1, shards):
        vec_send(d).start()
    for i in range(n):
        for d in range(1, chips):
            xy_send(i, d).start()
        core_copy(i, 0, 0, False).start()
    group_all[g] = count_ref[...]

    outs = [
        pltpu.make_async_copy(held[k], out_w[k], out_sems.at[k]) for k in range(6)
    ]

    def arrive(i):
        for d in range(1, chips):
            xy_here(i, d).wait_recv()
            if parts[i].share:
                z_copy(i, d, False).start()
            core_copy(i, d, 0, False).start()

    def relay(i):
        if parts[i].share:
            for d in range(1, chips):
                z_copy(i, d, True).wait_recv()
                core_copy(i, d, 1, False).start()

    def complete(i, whole_array=True):
        core_copy(i, 0, 0, True).wait_recv()
        for d in range(1, chips):
            core_copy(i, d, 0, True).wait_recv()
            if parts[i].share:
                core_copy(i, d, 1, True).wait_recv()
        if whole_array:
            outs[parts[i].array].start()

    for e in range(1, groups):
        group_copy(e).wait_recv()
    total = group_all[0]
    for p in range(1, groups):
        total = total + group_all[p]
    total_ref[...] = total
    for e in range(1, shards):
        shard_copy(e).start()
    shard_all[s] = total

    for d in range(1, shards):
        vec_here(d).wait_recv()
    for b in range(shards):
        vec_ref[:, b * wide : (b + 1) * wide] = vec_all[b].astype(F32)
    vec_copy = pltpu.make_async_copy(vec_ref, vec_out, out_sems.at[6])
    vec_copy.start()

    def normalise(i, carry):
        rows = pl.ds(pl.multiple_of(i * 256, 256), 256)
        hat, _ = norm_parts(x_ref[rows].astype(F32))
        a_ref[rows] = (hat * vec_ref[0:1, :CH] + vec_ref[1:2, :CH]).astype(BF16)
        return carry

    arrive(0)
    lax.fori_loop(0, frames // 256, normalise, 0)
    a_copy = pltpu.make_async_copy(a_ref, a_hbm, out_sems.at[7])
    a_copy.start()
    relay(0)
    arrive(1)
    complete(0)
    relay(1)

    def hide(i, carry):
        rows = pl.ds(pl.multiple_of(i * 256, 256), 256)
        hidden = product(a_ref[rows], held[0][...]) + vec_ref[2:3, :D]
        hidden = jnp.where(flag_ref[rows, 0:1] > 0.0, vec_ref[3:4, :D], hidden)
        h_ref[rows] = hidden
        hb_ref[rows] = hidden.astype(BF16)
        return carry

    lax.fori_loop(0, frames // 256, hide, 0)
    h_copy = pltpu.make_async_copy(h_ref, h_hbm, out_sems.at[8])
    hb_copy = pltpu.make_async_copy(hb_ref, hb_hbm, out_sems.at[9])
    h_copy.start()
    hb_copy.start()
    complete(1)

    def triple(i, carry):
        rows = pl.ds(pl.multiple_of(i * 256, 256), 256)
        low = hb_ref[rows]
        t_ref[rows, :D] = (product(low, held[1][:, :D]) + vec_ref[4:5, :D]).astype(BF16)
        t_ref[rows, D : 2 * D] = product(low, held[1][:, D : 2 * D]).astype(BF16)
        t_ref[rows, 2 * D :] = (product(low, held[1][:, 2 * D :]) + vec_ref[5:6, :D]).astype(BF16)
        return carry

    lax.fori_loop(0, frames // 256, triple, 0)
    t_copy = pltpu.make_async_copy(t_ref, t_hbm, out_sems.at[10])
    t_copy.start()
    arrive(2)
    relay(2)
    arrive(3)

    halves = half_masks()
    pairs = D // 128

    def attention(i, carry):
        u = i // pairs
        j = lax.rem(i, pairs)
        rows = pl.ds(pl.multiple_of(u * LEN, LEN), LEN)

        def lanes(block):
            return pl.ds(pl.multiple_of((j + block * pairs) * 128, 128), 128)

        shift = flag_ref[rows, 1:2]
        keys, values, query = (t_ref[rows, lanes(b)] for b in (1, 2, 0))
        out = None
        for half in halves:
            scores = product_nt(keys, query * half) * HEAD_DIM ** (-0.5) + shift
            power = jnp.exp(scores - jnp.max(scores, 0, keepdims=True))
            probs = (power * (1.0 / jnp.sum(power, 0, keepdims=True))).astype(BF16)
            part = product_tn(probs, values * half)
            out = part if out is None else out + part
        att_ref[rows, lanes(0)] = out.astype(BF16)
        return carry

    rounds = (frames // LEN) * pairs
    plan = [
        [(complete, 2), (relay, 3), (arrive, 4)],
        [(complete, 3), (relay, 4)],
        [(arrive, 5)],
        [(relay, 5), (arrive, 6)],
    ]
    cut = [rounds * i // len(plan) for i in range(len(plan) + 1)]
    for i, todo in enumerate(plan):
        lax.fori_loop(cut[i], cut[i + 1], attention, 0)
        for stage, part in todo:
            stage(part)
    att_copy = pltpu.make_async_copy(att_ref, att_hbm, out_sems.at[11])
    att_copy.start()

    complete(4, False)
    complete(5)
    relay(6)
    arrive(7)
    relay(7)
    complete(6, False)
    arrive(8)
    complete(7, False)
    relay(8)
    complete(8)

    for e in range(1, shards):
        shard_copy(e).wait_recv()
    for e in range(1, shards):
        shard_copy(e).wait_send()
    count = shard_all[0]
    for p in range(1, shards):
        count = count + shard_all[p]
    total_ref[...] = count

    for i in range(n):
        core_copy(i, 0, 0, False).wait_send()
        for d in range(1, chips):
            xy_send(i, d).wait_send()
            core_copy(i, d, 0, False).wait_send()
            if parts[i].share:
                z_copy(i, d, False).wait_send()
                core_copy(i, d, 1, False).wait_send()
    for d in range(1, shards):
        vec_send(d).wait_send()
    for e in range(1, groups):
        group_copy(e).wait_send()
    for copy in outs + [vec_copy, a_copy, h_copy, hb_copy, t_copy, att_copy]:
        copy.wait()


def forward(groups, shards, x, flags, weights, count):
    parts = weight_parts(shards)
    n = len(parts)
    chips = shards // 2
    frames = x.shape[0]
    hbm = pl.BlockSpec(memory_space=pl.ANY)
    vmem = pl.BlockSpec(memory_space=pltpu.VMEM)
    dma = pltpu.SemaphoreType.DMA
    arrays = [
        (CH, D),
        (D, 3 * D),
        (D, D),
        (D, FF),
        (FF, D),
        (CD, HEAD_COLS),
    ]
    values = [((CH,), BF16), ((D,), F32), ((D,), BF16), ((3 * D,), BF16), ((D,), BF16)]
    results = pl.pallas_call(
        functools.partial(forward_kernel, parts, groups, shards),
        in_specs=[vmem] * 8,
        out_specs=[hbm] * 7 + [vmem] + [hbm] * 5,
        out_shape=[jax.ShapeDtypeStruct(shape, BF16) for shape in arrays]
        + [jax.ShapeDtypeStruct((16, FF), F32), jax.ShapeDtypeStruct((8, 128), F32)]
        + [jax.ShapeDtypeStruct((frames,) + shape, kind) for shape, kind in values],
        scratch_shapes=[pltpu.VMEM(shape, BF16) for shape in arrays]
        + [pltpu.VMEM((shards, 16, FF // shards), BF16), pltpu.VMEM((16, FF), F32)]
        + [pltpu.VMEM((frames,) + shape, kind) for shape, kind in values]
        + [pltpu.VMEM((groups, 8, 128), F32), pltpu.VMEM((shards, 8, 128), F32)]
        + [
            dma((2, n, chips)),
            dma((2, n, chips)),
            dma((2, n, chips, 2)),
            dma((2, shards)),
            dma((2, groups)),
            dma((2, shards)),
            dma((12,)),
        ],
        compiler_params=pltpu.CompilerParams(
            collective_id=2, has_side_effects=True, vmem_limit_bytes=64 * 1024 * 1024 - 65536
        ),
        name="forward",
    )(x, flags, *weights, count)
    return results


class Chunk:
    def __init__(self, rows, group, slot, sum_slot, wide_xy, wide_z):
        self.used = sum(rows)
        self.starts = [sum(rows[:i]) for i in range(len(rows))]
        self.rows = ceil_to(self.used, 16 * group)
        self.part = self.rows // group
        self.slot = slot
        self.sum_slot = sum_slot
        self.kind_xy = F32 if wide_xy else BF16
        self.kind_z = F32 if wide_z else BF16


HEAD_SLOT = 2


def gradient_chunks(groups, shards):
    down, band = FF // shards, D // shards
    half = down // 2
    return [
        Chunk([half], groups, 0, 0, False, True),
        Chunk([half], groups, 1, 1, False, True),
        Chunk([CD // shards] * 2, groups, HEAD_SLOT, 4, True, True),
        Chunk([band] * 2, groups, 0, 2, False, False),
        Chunk([band] * 2, groups, 1, 3, False, False),
        Chunk([band] * 2, groups, 0, 0, False, False),
        Chunk([band] * 2, groups, 1, 1, False, False),
        Chunk([CH // shards, 16], groups, 0, 5, False, True),
    ]


def tiles(rows, step, body):
    def once(i, carry):
        body(pl.ds(pl.multiple_of(i * step, step), step))
        return carry

    lax.fori_loop(0, rows // step, once, 0)


def backward_kernel(chunks, groups, shards, *refs):
    chips = shards // 2
    n = len(chunks)
    refs = list(refs)

    def take(count):
        out = refs[:count]
        del refs[:count]
        return out

    (
        act_hbm,
        df_hbm,
        z1_hbm,
        de_hbm,
        z2_hbm,
        dc_hbm,
        uc_hbm,
        dlog_hbm,
        triple_hbm,
        datt_hbm,
        hid_hbm,
        att_hbm,
        dy_hbm,
        a_hbm,
        dr1_hbm,
        x_hbm,
        w0_hbm,
        win_hbm,
        head_hbm,
        flag_ref,
        gvin_ref,
        loss_ref,
    ) = take(22)
    ring = take(n)
    (stat_ref,) = take(1)
    pool, heads, dr1_ref, gv_ref, code_ref = take(5)
    full = take(3)
    pair = take(3)
    send_xy, recv_xy = take(n), take(n)
    acc = take(6)
    send_z, recv_z = take(n), take(n)
    loss_all, stat_all = take(2)
    (
        load_sems,
        core_sems,
        credit,
        xy_sems,
        z_sems,
        right_sems,
        left_sems,
        loss_sems,
        stat_sems,
    ) = take(9)

    g = lax.axis_index("group")
    s = lax.axis_index("shard")
    core = lax.rem(s, 2)
    chip = s // 2
    sibling = s + 1 - 2 * core
    parts = FF // D
    frames = flag_ref.shape[0]

    def load(src, dst, sem):
        return pltpu.make_async_copy(src, dst, load_sems.at[sem])

    def cols(ref, c):
        return ref.at[:, c * D : (c + 1) * D]

    loads = {
        "df": load(df_hbm, pool.at[0], 0),
        "z1": load(z1_hbm, pool.at[3], 3),
        "z2": load(z2_hbm, heads.at[0], 8),
        "dc": load(dc_hbm, heads.at[1, :, 0:CD], 9),
        "uc": load(uc_hbm, heads.at[1, :, CD : 2 * CD], 10),
        "dlog": load(dlog_hbm, heads.at[2, :, 0:CPAD], 11),
        "hid": load(hid_hbm, pool.at[0], 0),
        "att": load(att_hbm, pool.at[4], 4),
        "dy": load(dy_hbm, pool.at[5], 5),
        "x": load(x_hbm, pool.at[5, :, 0:CH], 5),
        "win": load(win_hbm, pool.at[6, 0:CH], 6),
        "dr1": load(dr1_hbm, dr1_ref, 7),
        "q": load(cols(triple_hbm, 0), heads.at[0], 8),
        "k": load(cols(triple_hbm, 1), heads.at[1], 9),
        "v": load(cols(triple_hbm, 2), heads.at[2], 11),
        "do": load(datt_hbm, heads.at[3], 12),
        "a": load(a_hbm, heads.at[3, :, 0:CH], 12),
        "codes": load(head_hbm.at[:, D:HEAD_COLS], code_ref, 13),
    }
    for c in range(parts):
        loads["act", c] = load(cols(act_hbm, c), pool.at[1 + c % 2], 1 + c % 2)
        loads["de", c] = load(cols(de_hbm, c), pool.at[1 + c % 2], 1 + c % 2)
    for c in range(3):
        loads["w", c] = load(cols(w0_hbm, c), pool.at[1 + c, 0:D], 1 + c)

    def fetch(*names):
        for name in names:
            loads[name].start()

    def ready(*names):
        for name in names:
            loads[name].wait()

    fetch("df", ("act", 0), ("act", 1), "z2", "dc", "uc", "dlog", "codes", "z1", "dr1")

    barrier = pltpu.get_barrier_semaphore()
    for e in range(1, shards):
        pl.semaphore_signal(
            barrier, 1, device_id=(g, lax.rem(s + e, shards)), device_id_type=MESH
        )
    for e in range(1, groups):
        pl.semaphore_signal(
            barrier, 1, device_id=(lax.rem(g + e, groups), s), device_id_type=MESH
        )
    pl.semaphore_wait(barrier, shards - 1 + groups - 1)

    def remote(src, dst, send_sem, recv_sem, device):
        return pltpu.make_async_remote_copy(
            src_ref=src,
            dst_ref=dst,
            send_sem=send_sem,
            recv_sem=recv_sem,
            device_id=device,
            device_id_type=MESH,
        )

    def loss_copy(e):
        return remote(
            loss_ref,
            loss_all.at[g],
            loss_sems.at[0, e],
            loss_sems.at[1, e],
            (lax.rem(g + e, groups), s),
        )

    for e in range(1, groups):
        loss_copy(e).start()
    loss_all[g] = loss_ref[...]

    def core_copy(t):
        c = chunks[t]
        return remote(
            full[c.slot].at[:, 1 - core, 0 : c.used],
            pair[c.slot].at[:, 0 : c.used],
            core_sems.at[0, t],
            core_sems.at[1, t],
            (g, sibling),
        )

    before = {}
    for t, c in enumerate(chunks):
        earlier = [i for i in range(t) if chunks[i].slot == c.slot]
        before[t] = earlier[-1] if earlier else None
    last_of = {c.slot: t for t, c in enumerate(chunks)}

    def free_buffer(t):
        if before[t] is not None:
            core_copy(before[t]).wait_send()

    def stage_pair(t):
        if before[t] is not None:
            pl.semaphore_wait(credit.at[chunks[t].slot], 1)
        core_copy(t).start()

    def chip_at(d):
        return lax.rem(chip + d, chips)

    def xy_copy(t, d):
        return remote(
            send_xy[t].at[d - 1],
            recv_xy[t].at[d - 1],
            xy_sems.at[0, t, d],
            xy_sems.at[1, t, d],
            (g, 2 * chip_at(d) + core),
        )

    def stage_chips(t):
        c = chunks[t]
        own, other = full[c.slot], pair[c.slot]
        core_copy(t).wait_recv()
        for d in list(range(1, chips)) + [0]:
            q = chip_at(d)
            if d == 0:

                def keep(rows):
                    acc[c.sum_slot][rows] = own[q, core, rows] + other[q, rows]

                tiles(c.used, 16, keep)
                if c.rows > c.used:
                    acc[c.sum_slot][c.used : c.rows] = jnp.zeros((c.rows - c.used, D), F32)
            else:

                def send(rows):
                    send_xy[t][d - 1, rows] = (own[q, core, rows] + other[q, rows]).astype(
                        c.kind_xy
                    )

                tiles(c.used, 16, send)
                xy_copy(t, d).start()
        if t != last_of[c.slot]:
            pl.semaphore_signal(
                credit.at[c.slot], 1, device_id=(g, sibling), device_id_type=MESH
            )

    def z_copy(t, e):
        return remote(
            send_z[t].at[e - 1],
            recv_z[t].at[e - 1],
            z_sems.at[0, t, e],
            z_sems.at[1, t, e],
            (lax.rem(g + e, groups), s),
        )

    def stage_group(t):
        c = chunks[t]
        total_ref = acc[c.sum_slot]
        for d in range(1, chips):
            xy_copy(t, d).wait_recv()

        def add(rows):
            total = total_ref[rows]
            for d in range(1, chips):
                total = total + recv_xy[t][d - 1, rows].astype(F32)
            total_ref[rows] = total

        tiles(c.used, 16, add)
        for e in range(1, groups):
            base = pl.multiple_of(lax.rem(g + e, groups) * c.part, 16)

            def send(rows):
                here = pl.ds(pl.multiple_of(base + rows.start, 16), 16)
                send_z[t][e - 1, rows] = total_ref[here].astype(BF16)

            tiles(c.part, 16, send)
            z_copy(t, e).start()

    def part_rows(t, p):
        return pl.ds(pl.multiple_of(p * chunks[t].part, 16), chunks[t].part)

    def ring_copy(t, k, way, back=0):
        p = g - k if way == 0 else g + k
        side = lax.rem(g + 1, groups) if way == 0 else lax.rem(g + groups - 1, groups)
        sems = right_sems if way == 0 else left_sems
        rows = part_rows(t, p)
        return remote(
            ring[t].at[rows],
            ring[t].at[rows],
            sems.at[0, t, k],
            sems.at[1, t, k - back],
            (side, s),
        )

    def holds(k, way):
        return g >= k if way == 0 else g + k < groups

    def sends(k, way):
        return (g >= k) & (g < groups - 1) if way == 0 else (g + k < groups) & (g > 0)

    def stage_total(t):
        c = chunks[t]
        total_ref = acc[c.sum_slot]
        for e in range(1, groups):
            z_copy(t, e).wait_recv()
        base = pl.multiple_of(g * c.part, 16)

        def add(rows):
            here = pl.ds(pl.multiple_of(base + rows.start, 16), 16)
            total = total_ref[here]
            for e in range(1, groups):
                total = total + recv_z[t][e - 1, rows].astype(F32)
            ring[t][here] = total.astype(c.kind_z)

        tiles(c.part, 16, add)
        for way in (0, 1):

            @pl.when(sends(0, way))
            def _():
                ring_copy(t, 0, way).start()

    def stage_ring(t, k):
        for way in (0, 1):

            @pl.when(holds(k, way))
            def _():
                ring_copy(t, k, way, 1).wait_recv()

            if k < groups - 1:

                @pl.when(sends(k, way))
                def _():
                    ring_copy(t, k, way).start()

    def stage_end(t, squares):
        c = chunks[t]

        def once(i, total):
            value = ring[t][pl.ds(pl.multiple_of(i * 16, 16), 16)].astype(F32)
            value = value * value
            return total + value[:8] + value[8:]

        return lax.fori_loop(0, c.rows // 16, once, squares)

    done = [0] * n
    squares = [jnp.zeros((8, D), F32)]

    def step(t):
        now = done[t]
        done[t] += 1
        if now == 0:
            stage_pair(t)
        elif now == 1:
            stage_chips(t)
        elif now == 2:
            stage_group(t)
        elif now == 3:
            stage_total(t)
        elif now < 3 + groups:
            stage_ring(t, now - 3)
        else:
            squares[0] = stage_end(t, squares[0])

    def scatter(value, slots, at, per, first_shard):
        count = value.shape[0] // per
        each = per // len(slots)
        for k in range(count):
            shard = first_shard * 1 + k
            for i, slot in enumerate(slots):
                rows = value[k * per + i * each : k * per + (i + 1) * each]
                full[slot][shard // 2, lax.rem(shard, 2), at : at + each, 0 : rows.shape[1]] = rows

    def grad(left, right, slots, at, per, block):
        width = left.shape[1]

        def once(i, carry):
            some = left[:, pl.ds(pl.multiple_of(i * block, 128), block)]
            scatter(product_tn(some, right[...]), slots, at, per, i * (block // per))
            return carry

        lax.fori_loop(0, width // block, once, 0)

    down, band, deep, first = FF // shards, D // shards, CD // shards, CH // shards
    wide = FF // shards
    pairs = D // 128

    ready("df")
    for c in range(parts):
        ready(("act", c))
        for i in range(2):
            value = product_tn(
                pool[1 + c % 2, :, i * (D // 2) : (i + 1) * (D // 2)], pool[0]
            )
            scatter(value, [0, 1], 0, down, (c * D + i * (D // 2)) // down)
        if c + 2 < parts:
            fetch(("act", c + 2))
        else:
            fetch(("de", c - 2))
    step(0)
    step(1)
    fetch("hid")
    ready("z2", "dc", "uc", "dlog", "codes")
    scatter(product_tn(heads[1, :, 0:CD], heads[0]), [HEAD_SLOT], 0, deep, 0)
    d_unit = product_tn(heads[1, :, CD : 2 * CD], heads[2, :, 0:CPAD])
    codes = code_ref[...].astype(F32)
    root = lax.rsqrt(jnp.sum(codes * codes, 0, keepdims=True) + 1e-06)
    unit = codes * root
    d_codes = root * (d_unit - unit * jnp.sum(d_unit * unit, 0, keepdims=True))
    scatter(d_codes, [HEAD_SLOT], deep, deep, 0)
    full[HEAD_SLOT][:, :, deep : 2 * deep, CPAD:D] = jnp.zeros((chips, 2, deep, D - CPAD), F32)
    step(2)
    fetch("q", "k", "v", "do", "att", "dy", "win")
    step(0)
    step(1)
    ready("z1")
    for t, first_part in ((3, 0), (4, 2)):
        free_buffer(t)
        for i in range(2):
            c = first_part + i
            ready(("de", c))
            grad(pool.at[3], pool.at[1 + c % 2], [chunks[t].slot], i * band, band, D // 2)
            if c + 2 < parts:
                fetch(("de", c + 2))
        step(t)
    for c in range(3):
        fetch(("w", c))

    halves = half_masks()

    def attention(i, carry):
        rows = pl.ds(pl.multiple_of((i // pairs) * LEN, LEN), LEN)
        lanes = pl.ds(pl.multiple_of(lax.rem(i, pairs) * 128, 128), 128)
        shift = flag_ref[rows, 1:2]
        keys, values = heads[1, rows, lanes], heads[2, rows, lanes]
        dq = dk = dv = None
        for half in halves:
            query = heads[0, rows, lanes] * half
            upstream = heads[3, rows, lanes] * half
            scores = product_nt(keys, query) * HEAD_DIM ** (-0.5) + shift
            power = jnp.exp(scores - jnp.max(scores, 0, keepdims=True))
            probs = power * (1.0 / jnp.sum(power, 0, keepdims=True))
            part_v = product(probs.astype(BF16), upstream)
            d_probs = product_nt(values, upstream)
            weight = jnp.sum(probs * d_probs, 0, keepdims=True)
            d_scores = (probs * (d_probs - weight) * HEAD_DIM ** (-0.5)).astype(BF16)
            part_k = product(d_scores, query)
            part_q = product_tn(d_scores, keys * half)
            dq = part_q if dq is None else dq + part_q
            dk = part_k if dk is None else dk + part_k
            dv = part_v if dv is None else dv + part_v
        heads[0, rows, lanes] = dq.astype(BF16)
        heads[1, rows, lanes] = dk.astype(BF16)
        heads[2, rows, lanes] = dv.astype(BF16)
        return carry

    ready("q", "k", "v", "do")
    rounds = (frames // LEN) * pairs
    plan = [(3, 4, 2), (0,), (1, 0), (0, 1), (0, 1)]
    cut = [rounds * i // len(plan) for i in range(len(plan) + 1)]
    for i, some in enumerate(plan):
        lax.fori_loop(cut[i], cut[i + 1], attention, 0)
        for t in some:
            step(t)
    fetch("a")

    ready("hid", "att", "dy")
    free_buffer(5)
    grad(pool.at[0], heads.at[0], [0], 0, band, D // 2)
    grad(pool.at[0], heads.at[1], [0], band, band, D // 2)
    step(5)
    free_buffer(6)
    grad(pool.at[0], heads.at[2], [1], 0, band, D // 2)
    grad(pool.at[4], pool.at[5], [1], band, band, D // 2)
    step(6)
    fetch("x")
    step(5)
    step(3)
    step(6)
    ready(("w", 0), ("w", 1), ("w", 2), "win", "dr1", "x")

    gv_ref[...] = gvin_ref[...]

    def back(i, carry):
        rows = pl.ds(pl.multiple_of(i * 256, 256), 256)
        dq, dk, dv = heads[0, rows], heads[1, rows], heads[2, rows]
        gv_ref[4:5, :D] += column_sum(dq.astype(F32))
        gv_ref[5:6, :D] += column_sum(dv.astype(F32))
        d_hidden = (
            dr1_ref[rows]
            + product_nt(dq, pool[1, 0:D])
            + product_nt(dk, pool[2, 0:D])
            + product_nt(dv, pool[3, 0:D])
        )
        masked = flag_ref[rows, 0:1] > 0.0
        gv_ref[3:4, :D] += column_sum(jnp.where(masked, d_hidden, 0.0))
        d_proj = jnp.where(masked, 0.0, d_hidden).astype(BF16)
        pool[4, rows] = d_proj
        gv_ref[2:3, :D] += column_sum(d_proj.astype(F32))
        d_normed = product_nt(d_proj, pool[6, 0:CH])
        hat, _ = norm_parts(pool[5, rows, 0:CH].astype(F32))
        gv_ref[0:1, :CH] += column_sum(d_normed * hat)
        gv_ref[1:2, :CH] += column_sum(d_normed)
        return carry

    lax.fori_loop(0, frames // 256, back, 0)
    ready("a")
    free_buffer(7)
    grad(heads.at[3, :, 0:CH], pool.at[4], [0], 0, first, CH // 2)
    for b in range(shards):
        full[0][b // 2, b % 2, first : first + 16, 0:wide] = gv_ref[:, b * wide : (b + 1) * wide]
        full[0][b // 2, b % 2, first : first + 16, wide:D] = jnp.zeros((16, D - wide), F32)
    step(7)
    step(4)
    step(7)
    order = [0, 1, 3, 4, 2, 5, 6, 7]
    final = 4 + groups
    while min(done) < final:
        for i, t in enumerate(order):
            ahead = [done[u] for u in order[:i]]
            if done[t] < final and all(d > done[t] for d in ahead if d < final):
                step(t)

    for e in range(1, groups):
        loss_copy(e).wait_recv()
    loss = loss_all[0]
    for p in range(1, groups):
        loss = loss + loss_all[p]
    lane = lax.broadcasted_iota(jnp.int32, (8, 128), 1)
    stat_ref[...] = jnp.where(lane == 0, jnp.sum(squares[0]), loss)

    def stat_copy(e):
        return remote(
            stat_ref,
            stat_all.at[s],
            stat_sems.at[0, e],
            stat_sems.at[1, e],
            (g, lax.rem(s + e, shards)),
        )

    for e in range(1, shards):
        stat_copy(e).start()
    stat_all[s] = stat_ref[...]
    for e in range(1, shards):
        stat_copy(e).wait_recv()
    for t in range(n):
        if t == last_of[chunks[t].slot]:
            core_copy(t).wait_send()
        for d in range(1, chips):
            xy_copy(t, d).wait_send()
        for e in range(1, groups):
            z_copy(t, e).wait_send()
        for k in range(groups - 1):
            for way in (0, 1):

                @pl.when(sends(k, way))
                def _():
                    ring_copy(t, k, way).wait_send()

    for e in range(1, groups):
        loss_copy(e).wait_send()
    for e in range(1, shards):
        stat_copy(e).wait_send()
    total = stat_all[0]
    for p in range(1, shards):
        total = total + stat_all[p]
    stat_ref[...] = total


def backward(groups, shards, operands, small):
    chunks = gradient_chunks(groups, shards)
    chips = shards // 2
    n = len(chunks)
    frames = operands[0].shape[0]
    hbm = pl.BlockSpec(memory_space=pl.ANY)
    vmem = pl.BlockSpec(memory_space=pltpu.VMEM)
    dma = pltpu.SemaphoreType.DMA
    deepest = [max(c.used for c in chunks if c.slot == i) for i in range(3)]
    sums = [max(c.rows for c in chunks if c.sum_slot == i) for i in range(6)]
    results = pl.pallas_call(
        functools.partial(backward_kernel, chunks, groups, shards),
        in_specs=[hbm] * len(operands) + [vmem] * len(small),
        out_specs=[vmem] * (n + 1),
        out_shape=[jax.ShapeDtypeStruct((c.rows, D), c.kind_z) for c in chunks]
        + [jax.ShapeDtypeStruct((8, 128), F32)],
        scratch_shapes=[
            pltpu.VMEM((7, frames, D), BF16),
            pltpu.VMEM((4, frames, D), BF16),
            pltpu.VMEM((frames, D), F32),
            pltpu.VMEM((16, FF), F32),
            pltpu.VMEM((CD, CPAD), BF16),
        ]
        + [pltpu.VMEM((chips, 2, rows, D), F32) for rows in deepest]
        + [pltpu.VMEM((chips, rows, D), F32) for rows in deepest]
        + [pltpu.VMEM((chips - 1, c.used, D), c.kind_xy) for c in chunks] * 2
        + [pltpu.VMEM((rows, D), F32) for rows in sums]
        + [pltpu.VMEM((groups - 1, c.part, D), BF16) for c in chunks] * 2
        + [pltpu.VMEM((groups, 8, 128), F32), pltpu.VMEM((shards, 8, 128), F32)]
        + [
            dma((14,)),
            dma((2, n)),
            pltpu.SemaphoreType.REGULAR((3,)),
            dma((2, n, chips)),
            dma((2, n, groups)),
            dma((2, n, groups)),
            dma((2, n, groups)),
            dma((2, groups)),
            dma((2, shards)),
        ],
        compiler_params=pltpu.CompilerParams(
            collective_id=1, has_side_effects=True, vmem_limit_bytes=64 * 1024 * 1024 - 65536
        ),
        name="backward",
    )(*operands, *small)
    return results[:n], results[n]


def adam_kernel(fix_ref, stat_ref, *refs):
    w, m, v = refs[0:5], refs[5:10], refs[10:15]
    g_head, g_tail = refs[15:17]
    halves = refs[17:23]
    outs = [refs[23 + 5 * i : 28 + 5 * i] for i in range(4)]
    norm_ref = refs[43]
    step = pl.program_id(0)
    norm = jnp.sqrt(stat_ref[0:1, 0:1])
    factor = jnp.minimum(1.0, clip_norm / (norm + 1e-06))

    def update(i, grad, where=...):
        shrink = 0.0 if i == 4 else decay
        weight, moment, square = w[i][where], m[i][where], v[i][where]
        grad = grad.astype(F32) * factor
        moment = beta_one * moment + (1.0 - beta_one) * grad
        square = beta_two * square + (1.0 - beta_two) * grad * grad
        stepped = moment / fix_ref[0] / (jnp.sqrt(square / fix_ref[1]) + adam_eps)
        weight = weight - rate * (stepped + shrink * weight)
        for out, value in zip(outs, (weight, moment, square, weight.astype(BF16))):
            out[i][where] = value

    def both(early):
        @pl.when(early == (step < 2))
        def _():
            qkvo, up, down = halves[0 if early else 1 :: 2]
            update(1, qkvo[...], 0)
            update(1, up[...], 1)
            update(2, down[...])

    both(True)
    both(False)

    @pl.when(step == 0)
    def _():
        first, deep = w[0].shape[0], w[3].shape[0]
        norm_ref[...] = norm
        update(0, g_tail[:first])
        update(3, g_head[:deep], (slice(None), slice(0, D)))
        update(3, g_head[deep : 2 * deep, :CODES], (slice(None), slice(D, D + CODES)))
        update(4, g_tail[first : first + NVEC, : w[4].shape[1]])


def adam(fixes, stat, weights, moments, seconds, sums):
    parts = FF // D
    depth = weights[1].shape[1]
    tall = weights[2].shape[0] // parts

    def fixed(a):
        return pl.BlockSpec(a.shape, lambda i: (0,) * a.ndim)

    w_specs = [
        fixed(weights[0]),
        pl.BlockSpec((2, depth, D), lambda i: (0, 0, i)),
        pl.BlockSpec((tall, D), lambda i: (i, 0)),
        fixed(weights[3]),
        fixed(weights[4]),
    ]
    g_specs = [fixed(sums[2]), fixed(sums[7])]
    for rows in (depth, depth, tall):
        g_specs.append(pl.BlockSpec((rows, D), lambda i: (jnp.minimum(i, 1), 0)))
        g_specs.append(pl.BlockSpec((rows, D), lambda i: (jnp.maximum(i - 2, 0), 0)))
    shapes = [jax.ShapeDtypeStruct(w.shape, F32) for w in weights]
    low = [jax.ShapeDtypeStruct(w.shape, BF16) for w in weights]
    outs = pl.pallas_call(
        adam_kernel,
        grid=(parts,),
        in_specs=[pl.BlockSpec(memory_space=pltpu.SMEM), fixed(stat)] + w_specs * 3 + g_specs,
        out_specs=w_specs * 4 + [pl.BlockSpec((1, 1), lambda i: (0, 0))],
        out_shape=shapes * 3 + low + [jax.ShapeDtypeStruct((1, 1), F32)],
        compiler_params=params(),
        name="adam",
    )(
        fixes,
        stat,
        *weights,
        *moments,
        *seconds,
        *[sums[i] for i in (2, 7, 5, 6, 3, 4, 0, 1)],
    )
    return [outs[i * 5 : (i + 1) * 5] for i in range(4)] + [outs[20]]


def span_mask(length, begins):
    position = jnp.arange(LEN, dtype=jnp.int32)
    first = begins % (length - SPAN + 1)
    inside = (position[None, :] >= first[:, None]) & (position[None, :] < first[:, None] + SPAN)
    return jnp.any(inside, 0) & (position < length)


def per_device(
    features,
    lengths,
    starts,
    labels,
    step_count,
    weight_in,
    weight_rows,
    weight_down,
    weight_head,
    vectors,
    moment_in,
    moment_rows,
    moment_down,
    moment_head,
    moment_vectors,
    second_in,
    second_rows,
    second_down,
    second_head,
    second_vectors,
):
    masters = (weight_in, weight_rows, weight_down, weight_head, vectors)
    moments = (moment_in, moment_rows, moment_down, moment_head, moment_vectors)
    seconds = (second_in, second_rows, second_down, second_head, second_vectors)
    utters = features.shape[0]
    n = utters * LEN
    groups, shards = lax.axis_size("group"), lax.axis_size("shard")
    masked = jax.vmap(span_mask)(lengths, starts).astype(F32)
    shift = jnp.where(jnp.arange(LEN, dtype=jnp.int32) < lengths[:, None], 0.0, -1e30)
    flags = jnp.stack([masked, shift], -1).reshape(n, 2)
    label = labels.reshape(n, 1)
    x = features.reshape(n, CH)

    def turned(arrays):
        return [a.T if i == 3 else a for i, a in enumerate(arrays)]

    shards_in = turned(masters)
    shards_in[3] = jnp.pad(shards_in[3], ((0, 0), (0, CPAD - CODES)))
    shards_in[4] = jnp.pad(shards_in[4], ((0, 16 - NVEC), (0, 0)))
    count = jnp.broadcast_to(jnp.sum(masked), (8, 128))
    win, wqkv, wo, wu, wd, head, vecs, count, a, hidden, hid_low, triple, att = forward(
        groups, shards, x, flags, shards_in, count
    )
    loss, z1, act, de, df, z2, dc, dlog, uc, dr1, dy, d_att, gv = feed(
        att, hidden, flags, label, wo, wu, wd, head, vecs, count, 256
    )
    sums, stat = backward(
        groups,
        shards,
        [act, df, z1, de, z2, dc, uc, dlog, triple, d_att, hid_low, att, dy, a, dr1, x, wqkv, win]
        + [head],
        [flags, gv, loss],
    )
    steps = step_count[0].astype(F32)
    fixes = jnp.stack([1.0 - jnp.power(beta_one, steps), 1.0 - jnp.power(beta_two, steps)])
    *updated, norm = adam(fixes, stat, turned(masters), turned(moments), turned(seconds), sums)
    new_w, new_m, new_v, copies = (turned(out) for out in updated)
    loss = stat[0, 1] / count[0, 0]
    return (
        *new_w,
        *new_m,
        *new_v,
        *copies,
        jnp.reshape(loss, (1,)),
        jnp.reshape(norm, (1,)),
    )


def solution(mesh):
    weights = (
        P("shard", None),
        P(None, "shard", None),
        P("shard", None),
        P(None, "shard"),
        P(None, "shard"),
    )
    both = ("group", "shard")
    in_specs = (P(both, None, None), P(both), P(both, None), P(both, None), P()) + weights * 3
    out_specs = weights * 4 + (P(), P())
    return jax.shard_map(
        per_device, mesh=mesh, in_specs=in_specs, out_specs=out_specs, check_vma=False
    )
```

```python
import functools

import jax
import jax.numpy as jnp
from jax import lax
from jax.experimental import pallas as pl
from jax.experimental.pallas import tpu as pltpu
from jax.sharding import PartitionSpec as P

D = 768
CH = 512
HEADS = 12
HEAD_DIM = 64
FF = 3072
CD = 256
CODES = 500
CPAD = 512
LEN = 512
SPAN = 10
NVEC = 14

beta_one = 0.9
beta_two = 0.999
rate = 0.03
decay = 0.01
adam_eps = 1e-08
clip_norm = 0.01
temper = 10.0

F32 = jnp.float32
BF16 = jnp.bfloat16
VMEM_BYTES = 60 * 1024 * 1024


def product(left, right):
    return jnp.dot(left, right, preferred_element_type=F32)


def product_nt(left, right):
    return lax.dot_general(left, right, (((1,), (1,)), ((), ())), preferred_element_type=F32)


def product_tn(left, right):
    return lax.dot_general(left, right, (((0,), (0,)), ((), ())), preferred_element_type=F32)


def norm_parts(values):
    centred = values - jnp.mean(values, -1, keepdims=True)
    root = lax.rsqrt(jnp.mean(centred * centred, -1, keepdims=True) + 1e-05)
    return centred * root, root


def norm_back(upstream, hat, root, gain):
    scaled = upstream * gain
    return root * (
        scaled
        - jnp.mean(scaled, -1, keepdims=True)
        - hat * jnp.mean(scaled * hat, -1, keepdims=True)
    )


def column_sum(values):
    return jnp.sum(values, 0, keepdims=True)


def gelu_pair(e):
    root = 0.7071067811865476
    reach = jnp.abs(e) * root
    tail = jnp.exp(-0.5 * e * e)
    t = 1.0 / (1.0 + 0.3275911 * reach)
    poly = t * (
        0.254829592
        + t * (-0.284496736 + t * (1.421413741 + t * (-1.453152027 + t * 1.061405429)))
    )
    half = 0.5 * poly * tail
    phi = jnp.where(e < 0.0, half, 1.0 - half)
    return e * phi, phi + e * tail * 0.3989422804014327


def params(limit=VMEM_BYTES):
    return pltpu.CompilerParams(vmem_limit_bytes=limit)


def half_masks():
    lane = lax.broadcasted_iota(jnp.int32, (1, 128), 1)
    return [(lane < HEAD_DIM).astype(BF16), (lane >= HEAD_DIM).astype(BF16)]


MESH = pl.DeviceIdType.MESH


def ceil_to(value, step):
    return -(-value // step) * step


class Part:
    def __init__(self, array, every, low, rows, col, cols):
        self.array, self.every, self.low, self.rows = array, every, low, rows
        self.col, self.cols = col, cols
        share = (rows * 2 // 5) // 16 * 16
        self.share = max(share, 16) if rows >= 32 else 0


HEAD_COLS = D + CPAD


def weight_parts(shards):
    band, down = D // shards, FF // shards
    third = down // 3
    return [
        Part(0, CH // shards, 0, CH // shards, 0, D),
        Part(1, band, 0, band, 0, 3 * D),
        Part(2, band, 0, band, 0, D),
        Part(5, CD // shards, 0, CD // shards, 0, HEAD_COLS),
        Part(3, band, 0, band, 0, 2 * D),
        Part(3, band, 0, band, 2 * D, 2 * D),
        Part(4, down, 0, third, 0, D),
        Part(4, down, third, third, 0, D),
        Part(4, down, 2 * third, third, 0, D),
    ]


def forward_kernel(parts, groups, shards, *refs):
    chips = shards // 2
    n = len(parts)
    refs = list(refs)

    def take(count):
        out = refs[:count]
        del refs[:count]
        return out

    len_ref, start_ref, x_ref, label_ref, win_ref, rows_ref, down_ref, head_ref, vecs_ref = take(9)
    out_w = take(6)
    vec_out, total_ref, loss_ref, gv_ref = take(4)
    out_v = take(len(FORWARD_VALUES))
    held = take(6)
    kept = take(len(FORWARD_VALUES) - 1)
    (
        flag_ref,
        a_ref,
        hb_ref,
        att_ref,
        r1_ref,
        z1_ref,
        act_ref,
        slope_ref,
        z2_ref,
        uc_ref,
        dlog_ref,
        dc_ref,
        df_ref,
        dr2_ref,
    ) = kept
    vec_all, vec_ref, cu_ref, count_ref, group_all, shard_all = take(6)
    h_ref = dr2_ref
    t_ref = act_ref
    kept.insert(3, act_ref.at[:, 0 : 3 * D])
    (xy_sems, z_sems, core_sems, vec_sems, group_sems, shard_sems, out_sems) = take(7)

    g = lax.axis_index("group")
    s = lax.axis_index("shard")
    core = lax.rem(s, 2)
    chip = s // 2
    sibling = s + 1 - 2 * core
    parity = lax.rem(g, 2)
    partner = g + 1 - 2 * parity
    frames = x_ref.shape[0]
    band, first = D // shards, CH // shards
    wide = FF // shards

    barrier = pltpu.get_barrier_semaphore()
    for e in range(1, shards):
        pl.semaphore_signal(
            barrier, 1, device_id=(g, lax.rem(s + e, shards)), device_id_type=MESH
        )
    for e in range(1, groups):
        pl.semaphore_signal(
            barrier, 1, device_id=(lax.rem(g + e, groups), s), device_id_type=MESH
        )

    vec_all[s] = jnp.zeros(vec_all.shape[1:], BF16)
    vec_all[s, 0:NVEC] = vecs_ref[...].astype(BF16)
    for ref, source, every in (
        (held[0], win_ref[...], first),
        (held[1], rows_ref[0, :, : 3 * D], band),
        (held[2], rows_ref[0, :, 3 * D :], band),
        (held[3], rows_ref[1], band),
        (held[4], down_ref[...], wide),
    ):
        ref[pl.ds(pl.multiple_of(s * every, 16), every)] = source.astype(BF16)
    every = CD // shards
    here = pl.ds(pl.multiple_of(s * every, 16), every)
    held[5][here, D + CPAD - 128 :] = jnp.zeros((every, 128), BF16)
    held[5][here, : D + CODES] = head_ref[...].astype(BF16)

    position = lax.broadcasted_iota(jnp.int32, (1, LEN), 1)
    local = jnp.zeros((1, 1), F32)
    for u in range(frames // LEN):
        length = len_ref[u]

        def span(j, inside):
            begin = lax.rem(start_ref[u, j], length - SPAN + 1)
            hit = (position >= begin) & (position < begin + SPAN)
            return jnp.where(hit, 1.0, inside)

        inside = lax.fori_loop(0, start_ref.shape[1], span, jnp.zeros((1, LEN), F32))
        masked = jnp.where(position < length, inside, 0.0)
        shift = jnp.where(position < length, 0.0, -1e30)
        label = label_ref[u : u + 1].astype(F32)
        lines = jnp.concatenate([masked, shift, label, jnp.zeros((5, LEN), F32)], 0)
        flag_ref[u * LEN : (u + 1) * LEN] = lines.T
        local = local + jnp.sum(masked, 1, keepdims=True)
    count_ref[...] = jnp.broadcast_to(local, (8, 128))
    pl.semaphore_wait(barrier, shards - 1 + groups - 1)

    def remote(ref, send_sem, recv_sem, device, dst=None):
        return pltpu.make_async_remote_copy(
            src_ref=ref,
            dst_ref=ref if dst is None else dst,
            send_sem=send_sem,
            recv_sem=recv_sem,
            device_id=device,
            device_id_type=MESH,
        )

    def region(i, shard, at, size):
        p = parts[i]
        rows = pl.ds(pl.multiple_of(shard * p.every + p.low + at, 16), size)
        return held[p.array].at[rows, p.col : p.col + p.cols]

    def chip_to(d):
        return lax.rem(chip + d, chips)

    def chip_from(d):
        return lax.rem(chip + chips - d, chips)

    def direct(i):
        return parity * parts[i].share, parts[i].rows - parts[i].share

    def xy_send(i, d):
        return remote(
            region(i, s, *direct(i)),
            xy_sems.at[0, i, d],
            xy_sems.at[1, i, d],
            (g, 2 * chip_to(d) + core),
        )

    def xy_here(i, d):
        return remote(
            region(i, 2 * chip_from(d) + core, *direct(i)),
            xy_sems.at[0, i, d],
            xy_sems.at[1, i, d],
            (g, 2 * chip_to(d) + core),
        )

    def z_copy(i, d, arriving):
        rest = parts[i].rows - parts[i].share
        start = (1 - parity if arriving else parity) * rest
        return remote(
            region(i, 2 * chip_from(d) + core, start, parts[i].share),
            z_sems.at[0, i, d],
            z_sems.at[1, i, d],
            (partner, s),
        )

    def core_copy(i, d, which, arriving):
        side = 1 - core if arriving else core
        shard = 2 * chip_from(d) + side
        if d == 0:
            span = (0, parts[i].rows)
        elif which == 0:
            span = direct(i)
        else:
            span = ((1 - parity) * (parts[i].rows - parts[i].share), parts[i].share)
        return remote(
            region(i, shard, *span),
            core_sems.at[0, i, d, which],
            core_sems.at[1, i, d, which],
            (g, sibling),
        )

    def vec_send(d):
        return remote(
            vec_all.at[s], vec_sems.at[0, d], vec_sems.at[1, d], (g, lax.rem(s + d, shards))
        )

    def vec_here(d):
        return remote(
            vec_all.at[lax.rem(s + shards - d, shards)],
            vec_sems.at[0, d],
            vec_sems.at[1, d],
            (g, lax.rem(s + d, shards)),
        )

    def group_copy(e):
        return remote(
            count_ref,
            group_sems.at[0, e],
            group_sems.at[1, e],
            (lax.rem(g + e, groups), s),
            group_all.at[g],
        )

    def shard_copy(e):
        return remote(
            total_ref,
            shard_sems.at[0, e],
            shard_sems.at[1, e],
            (g, lax.rem(s + e, shards)),
            shard_all.at[s],
        )

    for e in range(1, groups):
        group_copy(e).start()
    for d in range(1, shards):
        vec_send(d).start()
    for i in range(n):
        for d in range(1, chips):
            xy_send(i, d).start()
        core_copy(i, 0, 0, False).start()
    group_all[g] = count_ref[...]

    outs = [
        pltpu.make_async_copy(held[k], out_w[k], out_sems.at[k]) for k in range(6)
    ]

    def arrive(i):
        for d in range(1, chips):
            xy_here(i, d).wait_recv()
            if parts[i].share:
                z_copy(i, d, False).start()
            core_copy(i, d, 0, False).start()

    def relay(i):
        if parts[i].share:
            for d in range(1, chips):
                z_copy(i, d, True).wait_recv()
                core_copy(i, d, 1, False).start()

    def complete(i, whole_array=True):
        core_copy(i, 0, 0, True).wait_recv()
        for d in range(1, chips):
            core_copy(i, d, 0, True).wait_recv()
            if parts[i].share:
                core_copy(i, d, 1, True).wait_recv()
        if whole_array:
            outs[parts[i].array].start()

    for e in range(1, groups):
        group_copy(e).wait_recv()
    total = group_all[0]
    for p in range(1, groups):
        total = total + group_all[p]
    total_ref[...] = total
    for e in range(1, shards):
        shard_copy(e).start()
    shard_all[s] = total

    for d in range(1, shards):
        vec_here(d).wait_recv()
    for b in range(shards):
        vec_ref[:, b * wide : (b + 1) * wide] = vec_all[b].astype(F32)
    vec_copy = pltpu.make_async_copy(vec_ref, vec_out, out_sems.at[6])
    vec_copy.start()

    copies = [vec_copy]

    def leave(k):
        copy = pltpu.make_async_copy(kept[k], out_v[k], out_sems.at[7 + k])
        copy.start()
        copies.append(copy)

    def each_tile(body):
        def once(i, carry):
            body(pl.ds(pl.multiple_of(i * 256, 256), 256))
            return carry

        lax.fori_loop(0, frames // 256, once, 0)

    def vec(row, width=D):
        return vec_ref[row : row + 1, :width]

    def normalise(rows):
        hat, _ = norm_parts(x_ref[rows].astype(F32))
        a_ref[rows] = (hat * vec(0, CH) + vec(1, CH)).astype(BF16)

    arrive(0)
    each_tile(normalise)
    leave(0)
    leave(1)
    relay(0)
    arrive(1)
    complete(0)
    relay(1)

    def hide(rows):
        hidden = product(a_ref[rows], held[0][...]) + vec(2)
        hidden = jnp.where(flag_ref[rows, 0:1] > 0.0, vec(3), hidden)
        h_ref[rows] = hidden
        hb_ref[rows] = hidden.astype(BF16)

    each_tile(hide)
    leave(2)
    complete(1)

    def triple(rows):
        low = hb_ref[rows]
        t_ref[rows, :D] = (product(low, held[1][:, :D]) + vec(4)).astype(BF16)
        t_ref[rows, D : 2 * D] = product(low, held[1][:, D : 2 * D]).astype(BF16)
        t_ref[rows, 2 * D : 3 * D] = (product(low, held[1][:, 2 * D :]) + vec(5)).astype(BF16)

    each_tile(triple)
    leave(3)
    triple_copy = copies.pop()
    arrive(2)
    relay(2)
    arrive(3)

    halves = half_masks()
    pairs = D // 128

    def attention(i, carry):
        u = i // pairs
        j = lax.rem(i, pairs)
        rows = pl.ds(pl.multiple_of(u * LEN, LEN), LEN)

        def lanes(block):
            return pl.ds(pl.multiple_of((j + block * pairs) * 128, 128), 128)

        shift = flag_ref[rows, 1:2]
        keys, values, query = (t_ref[rows, lanes(b)] for b in (1, 2, 0))
        out = None
        for half in halves:
            scores = product_nt(keys, query * half) * HEAD_DIM ** (-0.5) + shift
            power = jnp.exp(scores - jnp.max(scores, 0, keepdims=True))
            probs = (power * (1.0 / jnp.sum(power, 0, keepdims=True))).astype(BF16)
            part = product_tn(probs, values * half)
            out = part if out is None else out + part
        att_ref[rows, lanes(0)] = out.astype(BF16)
        return carry

    rounds = (frames // LEN) * pairs
    plan = [
        [(complete, 2), (relay, 3), (arrive, 4)],
        [(complete, 3), (relay, 4)],
        [(arrive, 5)],
        [(relay, 5), (arrive, 6)],
    ]
    cut = [rounds * i // len(plan) for i in range(len(plan) + 1)]
    for i, todo in enumerate(plan):
        lax.fori_loop(cut[i], cut[i + 1], attention, 0)
        for stage, part in todo:
            stage(part)
    leave(4)
    triple_copy.wait()

    def branch(rows):
        resid = h_ref[rows] + product(att_ref[rows], held[2][...]) + vec(6)
        r1_ref[rows] = resid
        hat, _ = norm_parts(resid)
        first = hat * vec(7) + vec(8)
        h_ref[rows] = first
        z1_ref[rows] = first.astype(BF16)

    each_tile(branch)
    leave(5)
    leave(6)

    def upper(c):
        cols = slice(c * D, (c + 1) * D)

        def body(rows):
            before = product(z1_ref[rows], held[3][:, cols]) + vec_ref[9:10, cols]
            active, slope = gelu_pair(before)
            act_ref[rows, cols] = active.astype(BF16)
            slope_ref[rows, cols] = slope

        each_tile(body)

    complete(4, False)
    upper(0)
    relay(6)
    arrive(7)
    complete(5)
    upper(1)
    relay(7)
    arrive(8)
    upper(2)
    relay(8)
    complete(6, False)
    complete(7, False)
    upper(3)
    leave(7)
    leave(8)
    complete(8)

    for e in range(1, shards):
        shard_copy(e).wait_recv()
    for e in range(1, shards):
        shard_copy(e).wait_send()
    count = shard_all[0]
    for p in range(1, shards):
        count = count + shard_all[p]
    total_ref[...] = count
    scale = 1.0 / count[0:1, 0:1]
    codes = held[5][:, D:].astype(F32)
    cu_ref[...] = (
        codes * lax.rsqrt(jnp.sum(codes * codes, 0, keepdims=True) + 1e-06)
    ).astype(BF16)
    gv_ref[...] = jnp.zeros_like(gv_ref)
    loss_ref[...] = jnp.zeros_like(loss_ref)

    def lower(rows):
        masked = flag_ref[rows, 0:1]
        wh = held[5][:, :D]
        resid = h_ref[rows] + product(act_ref[rows], held[4][...]) + vec(10)
        hat, root = norm_parts(resid)
        second = (hat * vec(11) + vec(12)).astype(BF16)
        z2_ref[rows] = second
        head = product_nt(second, wh) + vec(13, CD)
        root_head = lax.rsqrt(jnp.sum(head * head, -1, keepdims=True) + 1e-06)
        unit = head * root_head
        unit_low = unit.astype(BF16)
        uc_ref[rows] = unit_low
        logits = temper * product(unit_low, cu_ref[...])
        code = lax.broadcasted_iota(jnp.int32, logits.shape, 1).astype(F32)
        logits = jnp.where(code < CODES, logits, -1e30)
        top = jnp.max(logits, -1, keepdims=True)
        power = jnp.exp(logits - top)
        total = jnp.sum(power, -1, keepdims=True)
        onehot = code == flag_ref[rows, 2:3]
        picked = jnp.sum(jnp.where(onehot, logits, 0.0), -1, keepdims=True)
        losses = top + jnp.log(total) - picked
        loss_ref[...] += jnp.sum(jnp.where(masked > 0.0, losses, 0.0), 0, keepdims=True)
        chances = power * (1.0 / total)
        d_logit = (
            temper
            * (jnp.where(masked > 0.0, chances - jnp.where(onehot, 1.0, 0.0), 0.0) * scale)
        ).astype(BF16)
        dlog_ref[rows] = d_logit
        d_unit = product_nt(d_logit, cu_ref[...])
        d_head = (
            root_head * (d_unit - unit * jnp.sum(d_unit * unit, -1, keepdims=True))
        ).astype(BF16)
        dc_ref[rows] = d_head
        gv_ref[13:14, :CD] += column_sum(d_head.astype(F32))
        d_second = product(d_head, wh)
        gv_ref[11:12, :D] += column_sum(d_second * hat)
        gv_ref[12:13, :D] += column_sum(d_second)
        d_resid = norm_back(d_second, hat, root, vec(11))
        dr2_ref[rows] = d_resid
        d_lower = d_resid.astype(BF16)
        df_ref[rows] = d_lower
        gv_ref[10:11, :D] += column_sum(d_lower.astype(F32))

    each_tile(lower)
    for k in range(9, len(kept)):
        leave(k)

    for i in range(n):
        core_copy(i, 0, 0, False).wait_send()
        for d in range(1, chips):
            xy_send(i, d).wait_send()
            core_copy(i, d, 0, False).wait_send()
            if parts[i].share:
                z_copy(i, d, False).wait_send()
                core_copy(i, d, 1, False).wait_send()
    for d in range(1, shards):
        vec_send(d).wait_send()
    for e in range(1, groups):
        group_copy(e).wait_send()
    for copy in outs + copies:
        copy.wait()


FORWARD_VALUES = (
    (8, F32),
    (CH, BF16),
    (D, BF16),
    (3 * D, BF16),
    (D, BF16),
    (D, F32),
    (D, BF16),
    (FF, BF16),
    (FF, F32),
    (D, BF16),
    (CD, BF16),
    (CPAD, BF16),
    (CD, BF16),
    (D, BF16),
    (D, F32),
)


def forward(groups, shards, lengths, starts, x, labels, weights):
    parts = weight_parts(shards)
    n = len(parts)
    chips = shards // 2
    frames = x.shape[0]
    hbm = pl.BlockSpec(memory_space=pl.ANY)
    vmem = pl.BlockSpec(memory_space=pltpu.VMEM)
    smem = pl.BlockSpec(memory_space=pltpu.SMEM)
    dma = pltpu.SemaphoreType.DMA
    arrays = [(CH, D), (D, 3 * D), (D, D), (D, FF), (FF, D), (CD, HEAD_COLS)]
    many = len(FORWARD_VALUES)
    results = pl.pallas_call(
        functools.partial(forward_kernel, parts, groups, shards),
        in_specs=[smem] * 2 + [vmem] * 7,
        out_specs=[hbm] * 7 + [vmem] * 3 + [hbm] * many,
        out_shape=[jax.ShapeDtypeStruct(shape, BF16) for shape in arrays]
        + [jax.ShapeDtypeStruct((16, FF), F32)]
        + [jax.ShapeDtypeStruct((8, 128), F32)] * 2
        + [jax.ShapeDtypeStruct((16, FF), F32)]
        + [jax.ShapeDtypeStruct((frames, width), kind) for width, kind in FORWARD_VALUES],
        scratch_shapes=[pltpu.VMEM(shape, BF16) for shape in arrays]
        + [
            pltpu.VMEM((frames, width), kind)
            for width, kind in FORWARD_VALUES
            if width != 3 * D
        ]
        + [
            pltpu.VMEM((shards, 16, FF // shards), BF16),
            pltpu.VMEM((16, FF), F32),
            pltpu.VMEM((CD, CPAD), BF16),
            pltpu.VMEM((8, 128), F32),
            pltpu.VMEM((groups, 8, 128), F32),
            pltpu.VMEM((shards, 8, 128), F32),
            dma((2, n, chips)),
            dma((2, n, chips)),
            dma((2, n, chips, 2)),
            dma((2, shards)),
            dma((2, groups)),
            dma((2, shards)),
            dma((7 + many,)),
        ],
        compiler_params=pltpu.CompilerParams(
            collective_id=2, has_side_effects=True, vmem_limit_bytes=64 * 1024 * 1024 - 65536
        ),
        name="forward",
    )(lengths, starts, x, labels, *weights)
    return results[:6], results[6], results[7], results[8], results[9], results[10:]


class Chunk:
    def __init__(self, rows, group, slot, sum_slot, wide_xy, wide_z):
        self.used = sum(rows)
        self.starts = [sum(rows[:i]) for i in range(len(rows))]
        self.rows = ceil_to(self.used, 16 * group)
        self.part = self.rows // group
        self.slot = slot
        self.sum_slot = sum_slot
        self.kind_xy = F32 if wide_xy else BF16
        self.kind_z = F32 if wide_z else BF16


HEAD_SLOT = 2


def gradient_chunks(groups, shards):
    down, band = FF // shards, D // shards
    half = down // 2
    return [
        Chunk([half], groups, 0, 0, False, True),
        Chunk([half], groups, 1, 1, False, True),
        Chunk([CD // shards] * 2, groups, HEAD_SLOT, 4, True, True),
        Chunk([band] * 2, groups, 0, 2, False, False),
        Chunk([band] * 2, groups, 1, 3, False, False),
        Chunk([band] * 2, groups, 0, 0, False, False),
        Chunk([band] * 2, groups, 1, 1, False, False),
        Chunk([CH // shards, 16], groups, 0, 5, False, True),
    ]


def tiles(rows, step, body):
    def once(i, carry):
        body(pl.ds(pl.multiple_of(i * step, step), step))
        return carry

    lax.fori_loop(0, rows // step, once, 0)


def backward_kernel(chunks, groups, shards, *refs):
    chips = shards // 2
    n = len(chunks)
    refs = list(refs)

    def take(count):
        out = refs[:count]
        del refs[:count]
        return out

    weights_hbm = take(6)
    vec_hbm, gvin_ref, loss_ref = take(3)
    (
        flag_hbm,
        a_hbm,
        hid_hbm,
        triple_hbm,
        att_hbm,
        r1_hbm,
        z1_hbm,
        act_hbm,
        slope_hbm,
        z2_hbm,
        uc_hbm,
        dlog_hbm,
        dc_hbm,
        df_hbm,
        dr2_hbm,
    ) = take(len(FORWARD_VALUES))
    (x_hbm,) = take(1)
    win_hbm, wqkv_hbm, wo_hbm, wu_hbm, wd_hbm, head_hbm = weights_hbm
    ring = take(n)
    (stat_out,) = take(1)
    pool, heads, dr1_ref, wide_ref, gv_ref, vec_ref, code_ref, flag_ref = take(8)
    full = take(3)
    pair = take(3)
    send_xy, recv_xy = take(3), take(n)
    acc = take(6)
    send_z, recv_z = take(n), take(n)
    stat_ref, group_all, stat_all = take(3)
    (
        load_sems,
        core_sems,
        credit,
        xy_sems,
        z_sems,
        right_sems,
        left_sems,
        loss_sems,
        stat_sems,
    ) = take(9)

    g = lax.axis_index("group")
    s = lax.axis_index("shard")
    core = lax.rem(s, 2)
    chip = s // 2
    sibling = s + 1 - 2 * core
    parts = FF // D
    frames = x_hbm.shape[0]

    def load(src, dst, sem):
        return pltpu.make_async_copy(src, dst, load_sems.at[sem])

    def cols(ref, c):
        return ref.at[:, c * D : (c + 1) * D]

    loads = {
        "df": load(df_hbm, pool.at[0], 0),
        "z1": load(z1_hbm, pool.at[3], 3),
        "z2": load(z2_hbm, heads.at[0], 8),
        "dc": load(dc_hbm, heads.at[1, :, 0:CD], 9),
        "uc": load(uc_hbm, heads.at[1, :, CD : 2 * CD], 10),
        "dlog": load(dlog_hbm, heads.at[2, :, 0:CPAD], 11),
        "hid": load(hid_hbm, pool.at[0], 0),
        "att": load(att_hbm, pool.at[4], 4),
        "x": load(x_hbm, pool.at[5, :, 0:CH], 5),
        "win": load(win_hbm, pool.at[6, 0:CH], 6),
        "dr2": load(dr2_hbm, dr1_ref, 7),
        "r1": load(r1_hbm, wide_ref, 14),
        "wo": load(wo_hbm, pool.at[2, 0:D], 2),
        "flags": load(flag_hbm, flag_ref, 15),
        "vec": load(vec_hbm, vec_ref, 16),
        "q": load(cols(triple_hbm, 0), heads.at[0], 8),
        "k": load(cols(triple_hbm, 1), heads.at[1], 9),
        "v": load(cols(triple_hbm, 2), heads.at[2], 11),
        "a": load(a_hbm, heads.at[3, :, 0:CH], 12),
        "codes": load(head_hbm.at[:, D:HEAD_COLS], code_ref, 13),
    }
    for c in range(parts):
        loads["act", c] = load(cols(act_hbm, c), pool.at[1 + c % 2], 1 + c % 2)
        loads["slope", c] = load(cols(slope_hbm, c), wide_ref, 14)
        loads["wd", c] = load(wd_hbm.at[c * D : (c + 1) * D], pool.at[2, 0:D], 2)
        loads["wu", c] = load(cols(wu_hbm, c), pool.at[5, 0:D], 5)
    for c in range(3):
        loads["w", c] = load(cols(wqkv_hbm, c), pool.at[1 + c, 0:D], 1 + c)

    def fetch(*names):
        for name in names:
            loads[name].start()

    def ready(*names):
        for name in names:
            loads[name].wait()

    fetch("df", ("act", 0), ("act", 1), "z2", "dc", "uc", "dlog", "codes", ("slope", 0), ("wu", 0))
    fetch("z1", "dr2", "flags", "vec")

    barrier = pltpu.get_barrier_semaphore()
    for e in range(1, shards):
        pl.semaphore_signal(
            barrier, 1, device_id=(g, lax.rem(s + e, shards)), device_id_type=MESH
        )
    for e in range(1, groups):
        pl.semaphore_signal(
            barrier, 1, device_id=(lax.rem(g + e, groups), s), device_id_type=MESH
        )
    pl.semaphore_wait(barrier, shards - 1 + groups - 1)

    def remote(src, dst, send_sem, recv_sem, device):
        return pltpu.make_async_remote_copy(
            src_ref=src,
            dst_ref=dst,
            send_sem=send_sem,
            recv_sem=recv_sem,
            device_id=device,
            device_id_type=MESH,
        )

    def core_copy(t):
        c = chunks[t]
        return remote(
            full[c.slot].at[:, 1 - core, 0 : c.used],
            pair[c.slot].at[:, 0 : c.used],
            core_sems.at[0, t],
            core_sems.at[1, t],
            (g, sibling),
        )

    before = {}
    for t, c in enumerate(chunks):
        earlier = [i for i in range(t) if chunks[i].slot == c.slot]
        before[t] = earlier[-1] if earlier else None
    last_of = {c.slot: t for t, c in enumerate(chunks)}

    def free_buffer(t):
        if before[t] is not None:
            core_copy(before[t]).wait_send()

    def stage_pair(t):
        if before[t] is not None:
            pl.semaphore_wait(credit.at[chunks[t].slot], 1)
        core_copy(t).start()

    def chip_at(d):
        return lax.rem(chip + d, chips)

    def xy_copy(t, d):
        return remote(
            send_xy[chunks[t].slot].at[d - 1, 0 : chunks[t].used],
            recv_xy[t].at[d - 1],
            xy_sems.at[0, t, d],
            xy_sems.at[1, t, d],
            (g, 2 * chip_at(d) + core),
        )

    def stage_chips(t):
        c = chunks[t]
        own, other = full[c.slot], pair[c.slot]
        core_copy(t).wait_recv()
        for d in list(range(1, chips)) + [0]:
            q = chip_at(d)
            if d > 0 and before[t] is not None:
                xy_copy(before[t], d).wait_send()
            if d == 0:

                def keep(rows):
                    acc[c.sum_slot][rows] = own[q, core, rows] + other[q, rows]

                tiles(c.used, 16, keep)
                if c.rows > c.used:
                    acc[c.sum_slot][c.used : c.rows] = jnp.zeros((c.rows - c.used, D), F32)
            else:

                def send(rows):
                    send_xy[c.slot][d - 1, rows] = (own[q, core, rows] + other[q, rows]).astype(
                        c.kind_xy
                    )

                tiles(c.used, 16, send)
                xy_copy(t, d).start()
        if t != last_of[c.slot]:
            pl.semaphore_signal(
                credit.at[c.slot], 1, device_id=(g, sibling), device_id_type=MESH
            )

    def z_copy(t, e):
        return remote(
            send_z[t].at[e - 1],
            recv_z[t].at[e - 1],
            z_sems.at[0, t, e],
            z_sems.at[1, t, e],
            (lax.rem(g + e, groups), s),
        )

    def stage_group(t):
        c = chunks[t]
        total_ref = acc[c.sum_slot]
        for d in range(1, chips):
            xy_copy(t, d).wait_recv()

        def add(rows):
            total = total_ref[rows]
            for d in range(1, chips):
                total = total + recv_xy[t][d - 1, rows].astype(F32)
            total_ref[rows] = total

        tiles(c.used, 16, add)
        for e in range(1, groups):
            base = pl.multiple_of(lax.rem(g + e, groups) * c.part, 16)

            def send(rows):
                here = pl.ds(pl.multiple_of(base + rows.start, 16), 16)
                send_z[t][e - 1, rows] = total_ref[here].astype(BF16)

            tiles(c.part, 16, send)
            z_copy(t, e).start()

    def part_rows(t, p):
        return pl.ds(pl.multiple_of(p * chunks[t].part, 16), chunks[t].part)

    def ring_copy(t, k, way, back=0):
        p = g - k if way == 0 else g + k
        side = lax.rem(g + 1, groups) if way == 0 else lax.rem(g + groups - 1, groups)
        sems = right_sems if way == 0 else left_sems
        rows = part_rows(t, p)
        return remote(
            ring[t].at[rows],
            ring[t].at[rows],
            sems.at[0, t, k],
            sems.at[1, t, k - back],
            (side, s),
        )

    def holds(k, way):
        return g >= k if way == 0 else g + k < groups

    def sends(k, way):
        return (g >= k) & (g < groups - 1) if way == 0 else (g + k < groups) & (g > 0)

    def stage_total(t):
        c = chunks[t]
        total_ref = acc[c.sum_slot]
        for e in range(1, groups):
            z_copy(t, e).wait_recv()
        base = pl.multiple_of(g * c.part, 16)

        def add(i, sums):
            rows = pl.ds(pl.multiple_of(i * 16, 16), 16)
            here = pl.ds(pl.multiple_of(base + i * 16, 16), 16)
            total = total_ref[here]
            for e in range(1, groups):
                total = total + recv_z[t][e - 1, rows].astype(F32)
            total = total.astype(c.kind_z)
            ring[t][here] = total
            total = total.astype(F32)
            total = total * total
            return sums + total[:8] + total[8:]

        squares[0] = lax.fori_loop(0, c.part // 16, add, squares[0])
        for way in (0, 1):

            @pl.when(sends(0, way))
            def _():
                ring_copy(t, 0, way).start()

    def stage_ring(t, k):
        for way in (0, 1):

            @pl.when(holds(k, way))
            def _():
                ring_copy(t, k, way, 1).wait_recv()

            if k < groups - 1:

                @pl.when(sends(k, way))
                def _():
                    ring_copy(t, k, way).start()

    done = [0] * n
    squares = [jnp.zeros((8, D), F32)]

    def step(t):
        now = done[t]
        done[t] += 1
        if now == 0:
            stage_pair(t)
        elif now == 1:
            stage_chips(t)
        elif now == 2:
            stage_group(t)
        elif now == 3:
            stage_total(t)
        else:
            stage_ring(t, now - 3)

    def scatter(value, slots, at, per, first_shard):
        count = value.shape[0] // per
        each = per // len(slots)
        for k in range(count):
            shard = first_shard * 1 + k
            for i, slot in enumerate(slots):
                rows = value[k * per + i * each : k * per + (i + 1) * each]
                full[slot][shard // 2, lax.rem(shard, 2), at : at + each, 0 : rows.shape[1]] = rows

    def grad(left, right, slots, at, per, block):
        width = left.shape[1]

        def once(i, carry):
            some = left[:, pl.ds(pl.multiple_of(i * block, 128), block)]
            scatter(product_tn(some, right[...]), slots, at, per, i * (block // per))
            return carry

        lax.fori_loop(0, width // block, once, 0)

    down, band, deep, first = FF // shards, D // shards, CD // shards, CH // shards
    wide = FF // shards
    pairs = D // 128

    ready("df")
    for c in range(parts):
        ready(("act", c))
        for i in range(2):
            value = product_tn(
                pool[1 + c % 2, :, i * (D // 2) : (i + 1) * (D // 2)], pool[0]
            )
            scatter(value, [0, 1], 0, down, (c * D + i * (D // 2)) // down)
        if c + 2 < parts:
            fetch(("act", c + 2))
    fetch(("wd", 0))
    step(0)
    step(1)
    ready("z2", "dc", "uc", "dlog", "codes")
    scatter(product_tn(heads[1, :, 0:CD], heads[0]), [HEAD_SLOT], 0, deep, 0)
    d_unit = product_tn(heads[1, :, CD : 2 * CD], heads[2, :, 0:CPAD])
    codes = code_ref[...].astype(F32)
    root = lax.rsqrt(jnp.sum(codes * codes, 0, keepdims=True) + 1e-06)
    unit = codes * root
    d_codes = root * (d_unit - unit * jnp.sum(d_unit * unit, 0, keepdims=True))
    scatter(d_codes, [HEAD_SLOT], deep, deep, 0)
    full[HEAD_SLOT][:, :, deep : 2 * deep, CPAD:D] = jnp.zeros((chips, 2, deep, D - CPAD), F32)
    step(2)
    fetch("q", "k", "v", "att", "win")
    step(0)
    step(1)
    ready("z1", "dr2", "flags", "vec")
    gv_ref[...] = gvin_ref[...]

    def each_tile(body):
        def once(i, carry):
            body(pl.ds(pl.multiple_of(i * 256, 256), 256))
            return carry

        lax.fori_loop(0, frames // 256, once, 0)

    for t, first_part in ((3, 0), (4, 2)):
        free_buffer(t)
        for i in range(2):
            c = first_part + i
            span = slice(c * D, (c + 1) * D)
            ready(("slope", c), ("wd", c), ("wu", c))

            def lower(rows):
                d_before = wide_ref[rows] * product_nt(pool[0, rows], pool[2, 0:D])
                d_before = d_before.astype(BF16)
                pool[1, rows] = d_before
                gv_ref[9:10, span] += column_sum(d_before.astype(F32))
                dr1_ref[rows] += product_nt(d_before, pool[5, 0:D])

            each_tile(lower)
            if c + 1 < parts:
                fetch(("slope", c + 1), ("wd", c + 1), ("wu", c + 1))
            else:
                fetch("r1", "wo", "hid")
            grad(pool.at[3], pool.at[1], [chunks[t].slot], i * band, band, D // 2)
        step(t)
    ready("r1", "wo")

    def branch(rows):
        hat, root = norm_parts(wide_ref[rows])
        d_first = dr1_ref[rows]
        gv_ref[7:8, :D] += column_sum(d_first * hat)
        gv_ref[8:9, :D] += column_sum(d_first)
        d_resid = norm_back(d_first, hat, root, vec_ref[7:8, :D])
        dr1_ref[rows] = d_resid
        d_branch = d_resid.astype(BF16)
        pool[5, rows] = d_branch
        gv_ref[6:7, :D] += column_sum(d_branch.astype(F32))
        heads[3, rows] = product_nt(d_branch, pool[2, 0:D]).astype(BF16)

    each_tile(branch)
    for c in range(3):
        fetch(("w", c))

    halves = half_masks()

    def attention(i, carry):
        rows = pl.ds(pl.multiple_of((i // pairs) * LEN, LEN), LEN)
        lanes = pl.ds(pl.multiple_of(lax.rem(i, pairs) * 128, 128), 128)
        shift = flag_ref[rows, 1:2]
        keys, values = heads[1, rows, lanes], heads[2, rows, lanes]
        dq = dk = dv = None
        for half in halves:
            query = heads[0, rows, lanes] * half
            upstream = heads[3, rows, lanes] * half
            scores = product_nt(keys, query) * HEAD_DIM ** (-0.5) + shift
            power = jnp.exp(scores - jnp.max(scores, 0, keepdims=True))
            probs = power * (1.0 / jnp.sum(power, 0, keepdims=True))
            part_v = product(probs.astype(BF16), upstream)
            d_probs = product_nt(values, upstream)
            weight = jnp.sum(probs * d_probs, 0, keepdims=True)
            d_scores = (probs * (d_probs - weight) * HEAD_DIM ** (-0.5)).astype(BF16)
            part_k = product(d_scores, query)
            part_q = product_tn(d_scores, keys * half)
            dq = part_q if dq is None else dq + part_q
            dk = part_k if dk is None else dk + part_k
            dv = part_v if dv is None else dv + part_v
        heads[0, rows, lanes] = dq.astype(BF16)
        heads[1, rows, lanes] = dk.astype(BF16)
        heads[2, rows, lanes] = dv.astype(BF16)
        return carry

    ready("q", "k", "v")
    rounds = (frames // LEN) * pairs
    plan = [(3, 4, 2), (0,), (1, 0), (0, 1), (0, 1)]
    cut = [rounds * i // len(plan) for i in range(len(plan) + 1)]
    for i, some in enumerate(plan):
        lax.fori_loop(cut[i], cut[i + 1], attention, 0)
        for t in some:
            step(t)
    fetch("a")

    ready("hid", "att")
    free_buffer(5)
    grad(pool.at[0], heads.at[0], [0], 0, band, D // 2)
    grad(pool.at[0], heads.at[1], [0], band, band, D // 2)
    step(5)
    free_buffer(6)
    grad(pool.at[0], heads.at[2], [1], 0, band, D // 2)
    grad(pool.at[4], pool.at[5], [1], band, band, D // 2)
    step(6)
    fetch("x")
    step(5)
    step(3)
    step(6)
    ready(("w", 0), ("w", 1), ("w", 2), "win", "x")

    def back(rows):
        dq, dk, dv = heads[0, rows], heads[1, rows], heads[2, rows]
        gv_ref[4:5, :D] += column_sum(dq.astype(F32))
        gv_ref[5:6, :D] += column_sum(dv.astype(F32))
        d_hidden = (
            dr1_ref[rows]
            + product_nt(dq, pool[1, 0:D])
            + product_nt(dk, pool[2, 0:D])
            + product_nt(dv, pool[3, 0:D])
        )
        masked = flag_ref[rows, 0:1] > 0.0
        gv_ref[3:4, :D] += column_sum(jnp.where(masked, d_hidden, 0.0))
        d_proj = jnp.where(masked, 0.0, d_hidden).astype(BF16)
        pool[4, rows] = d_proj
        gv_ref[2:3, :D] += column_sum(d_proj.astype(F32))
        d_normed = product_nt(d_proj, pool[6, 0:CH])
        hat, _ = norm_parts(pool[5, rows, 0:CH].astype(F32))
        gv_ref[0:1, :CH] += column_sum(d_normed * hat)
        gv_ref[1:2, :CH] += column_sum(d_normed)

    each_tile(back)
    ready("a")
    free_buffer(7)
    grad(heads.at[3, :, 0:CH], pool.at[4], [0], 0, first, CH // 2)
    for b in range(shards):
        full[0][b // 2, b % 2, first : first + 16, 0:wide] = gv_ref[:, b * wide : (b + 1) * wide]
        full[0][b // 2, b % 2, first : first + 16, wide:D] = jnp.zeros((16, D - wide), F32)
    step(7)
    step(4)
    step(7)
    order = [0, 1, 3, 4, 2, 5, 6, 7]
    final = 3 + groups
    last = order[-1]

    def advance(until):
        while done[last] < until:
            for i, t in enumerate(order):
                ahead = [done[u] for u in order[:i]]
                if done[t] < final and all(d > done[t] for d in ahead if d < final):
                    step(t)
                    if done[last] >= until:
                        return

    def group_copy(e):
        return remote(
            stat_ref.at[0],
            group_all.at[g],
            loss_sems.at[0, e],
            loss_sems.at[1, e],
            (lax.rem(g + e, groups), s),
        )

    def stat_copy(e):
        return remote(
            stat_ref.at[1],
            stat_all.at[s],
            stat_sems.at[0, e],
            stat_sems.at[1, e],
            (g, lax.rem(s + e, shards)),
        )

    advance(4)
    lane = lax.broadcasted_iota(jnp.int32, (8, 128), 1)
    stat_ref[0] = jnp.where(lane == 0, jnp.sum(squares[0]), loss_ref[...])
    for e in range(1, groups):
        group_copy(e).start()
    group_all[g] = stat_ref[0]
    advance(5)
    for e in range(1, groups):
        group_copy(e).wait_recv()
    total = group_all[0]
    for p in range(1, groups):
        total = total + group_all[p]
    stat_ref[1] = total
    for e in range(1, shards):
        stat_copy(e).start()
    stat_all[s] = total
    advance(final)
    for e in range(1, shards):
        stat_copy(e).wait_recv()
    total = stat_all[0]
    for p in range(1, shards):
        total = total + stat_all[p]
    stat_out[...] = total
    for t in range(n):
        if t == last_of[chunks[t].slot]:
            core_copy(t).wait_send()
            for d in range(1, chips):
                xy_copy(t, d).wait_send()
        for e in range(1, groups):
            z_copy(t, e).wait_send()
        for k in range(groups - 1):
            for way in (0, 1):

                @pl.when(sends(k, way))
                def _():
                    ring_copy(t, k, way).wait_send()

    for e in range(1, groups):
        group_copy(e).wait_send()
    for e in range(1, shards):
        stat_copy(e).wait_send()


def backward(groups, shards, weights, vecs, gv, loss, values, x):
    chunks = gradient_chunks(groups, shards)
    chips = shards // 2
    n = len(chunks)
    frames = x.shape[0]
    hbm = pl.BlockSpec(memory_space=pl.ANY)
    vmem = pl.BlockSpec(memory_space=pltpu.VMEM)
    dma = pltpu.SemaphoreType.DMA
    deepest = [max(c.used for c in chunks if c.slot == i) for i in range(3)]
    sums = [max(c.rows for c in chunks if c.sum_slot == i) for i in range(6)]
    results = pl.pallas_call(
        functools.partial(backward_kernel, chunks, groups, shards),
        in_specs=[hbm] * 7 + [vmem] * 2 + [hbm] * (len(values) + 1),
        out_specs=[vmem] * (n + 1),
        out_shape=[jax.ShapeDtypeStruct((c.rows, D), c.kind_z) for c in chunks]
        + [jax.ShapeDtypeStruct((8, 128), F32)],
        scratch_shapes=[
            pltpu.VMEM((7, frames, D), BF16),
            pltpu.VMEM((4, frames, D), BF16),
            pltpu.VMEM((frames, D), F32),
            pltpu.VMEM((frames, D), F32),
            pltpu.VMEM((16, FF), F32),
            pltpu.VMEM((16, FF), F32),
            pltpu.VMEM((CD, CPAD), BF16),
            pltpu.VMEM((frames, 8), F32),
        ]
        + [pltpu.VMEM((chips, 2, rows, D), F32) for rows in deepest]
        + [pltpu.VMEM((chips, rows, D), F32) for rows in deepest]
        + [
            pltpu.VMEM((chips - 1, rows, D), F32 if i == HEAD_SLOT else BF16)
            for i, rows in enumerate(deepest)
        ]
        + [pltpu.VMEM((chips - 1, c.used, D), c.kind_xy) for c in chunks]
        + [pltpu.VMEM((rows, D), F32) for rows in sums]
        + [pltpu.VMEM((groups - 1, c.part, D), BF16) for c in chunks] * 2
        + [
            pltpu.VMEM((2, 8, 128), F32),
            pltpu.VMEM((groups, 8, 128), F32),
            pltpu.VMEM((shards, 8, 128), F32),
        ]
        + [
            dma((17,)),
            dma((2, n)),
            pltpu.SemaphoreType.REGULAR((3,)),
            dma((2, n, chips)),
            dma((2, n, groups)),
            dma((2, n, groups)),
            dma((2, n, groups)),
            dma((2, groups)),
            dma((2, shards)),
        ],
        compiler_params=pltpu.CompilerParams(
            collective_id=1, has_side_effects=True, vmem_limit_bytes=64 * 1024 * 1024 - 65536
        ),
        name="backward",
    )(*weights, vecs, gv, loss, *values, x)
    return results[:n], results[n]


def adam_kernel(step_ref, stat_ref, count_ref, *refs):
    w, m, v = refs[0:5], refs[5:10], refs[10:15]
    g_head, g_tail = refs[15:17]
    halves = refs[17:23]
    outs = [refs[23 + 5 * i : 28 + 5 * i] for i in range(4)]
    norm_ref, loss_ref = refs[43:45]
    step = pl.program_id(0)
    fix_one, fix_two = (
        1.0 - lax.fori_loop(0, step_ref[0], lambda _, value: value * beta, jnp.float32(1.0))
        for beta in (beta_one, beta_two)
    )
    norm = jnp.sqrt(stat_ref[0:1, 0:1])
    factor = jnp.minimum(1.0, clip_norm / (norm + 1e-06))

    def update(i, grad, where=...):
        shrink = 0.0 if i == 4 else decay
        weight, moment, square = w[i][where], m[i][where], v[i][where]
        grad = grad.astype(F32) * factor
        moment = beta_one * moment + (1.0 - beta_one) * grad
        square = beta_two * square + (1.0 - beta_two) * grad * grad
        stepped = moment / fix_one / (jnp.sqrt(square / fix_two) + adam_eps)
        weight = weight - rate * (stepped + shrink * weight)
        for out, value in zip(outs, (weight, moment, square, weight.astype(BF16))):
            out[i][where] = value

    def both(early):
        @pl.when(early == (step < 2))
        def _():
            qkvo, up, down = halves[0 if early else 1 :: 2]
            update(1, qkvo[...], 0)
            update(1, up[...], 1)
            update(2, down[...])

    both(True)
    both(False)

    @pl.when(step == 0)
    def _():
        first, deep = w[0].shape[0], w[3].shape[0]
        norm_ref[...] = norm
        loss_ref[...] = stat_ref[0:1, 1:2] / count_ref[0:1, 0:1]
        update(0, g_tail[:first])
        update(3, g_head[:deep], (slice(None), slice(0, D)))
        update(3, g_head[deep : 2 * deep, :CODES], (slice(None), slice(D, D + CODES)))
        update(4, g_tail[first : first + NVEC, : w[4].shape[1]])


def adam(steps, stat, count, weights, moments, seconds, sums):
    parts = FF // D
    depth = weights[1].shape[1]
    tall = weights[2].shape[0] // parts

    def fixed(a):
        return pl.BlockSpec(a.shape, lambda i: (0,) * a.ndim)

    w_specs = [
        fixed(weights[0]),
        pl.BlockSpec((2, depth, D), lambda i: (0, 0, i)),
        pl.BlockSpec((tall, D), lambda i: (i, 0)),
        fixed(weights[3]),
        fixed(weights[4]),
    ]
    g_specs = [fixed(sums[2]), fixed(sums[7])]
    for rows in (depth, depth, tall):
        g_specs.append(pl.BlockSpec((rows, D), lambda i: (jnp.minimum(i, 1), 0)))
        g_specs.append(pl.BlockSpec((rows, D), lambda i: (jnp.maximum(i - 2, 0), 0)))
    shapes = [jax.ShapeDtypeStruct(w.shape, F32) for w in weights]
    low = [jax.ShapeDtypeStruct(w.shape, BF16) for w in weights]
    outs = pl.pallas_call(
        adam_kernel,
        grid=(parts,),
        in_specs=[pl.BlockSpec(memory_space=pltpu.SMEM), fixed(stat), fixed(count)]
        + w_specs * 3
        + g_specs,
        out_specs=w_specs * 4 + [pl.BlockSpec((1, 1), lambda i: (0, 0))] * 2,
        out_shape=shapes * 3 + low + [jax.ShapeDtypeStruct((1, 1), F32)] * 2,
        compiler_params=params(),
        name="adam",
    )(
        steps,
        stat,
        count,
        *weights,
        *moments,
        *seconds,
        *[sums[i] for i in (2, 7, 5, 6, 3, 4, 0, 1)],
    )
    return [outs[i * 5 : (i + 1) * 5] for i in range(4)] + list(outs[20:])


def per_device(
    features,
    lengths,
    starts,
    labels,
    step_count,
    weight_in,
    weight_rows,
    weight_down,
    weight_head,
    vectors,
    moment_in,
    moment_rows,
    moment_down,
    moment_head,
    moment_vectors,
    second_in,
    second_rows,
    second_down,
    second_head,
    second_vectors,
):
    masters = (weight_in, weight_rows, weight_down, weight_head, vectors)
    moments = (moment_in, moment_rows, moment_down, moment_head, moment_vectors)
    seconds = (second_in, second_rows, second_down, second_head, second_vectors)
    groups, shards = lax.axis_size("group"), lax.axis_size("shard")
    x = features.reshape(-1, CH)

    def turned(arrays):
        return [a.T if i == 3 else a for i, a in enumerate(arrays)]

    weights, vecs, count, loss, gv, values = forward(
        groups, shards, lengths, starts, x, labels, turned(masters)
    )
    sums, stat = backward(groups, shards, weights, vecs, gv, loss, values, x)
    *updated, norm, loss = adam(
        step_count, stat, count, turned(masters), turned(moments), turned(seconds), sums
    )
    new_w, new_m, new_v, copies = (turned(out) for out in updated)
    return (
        *new_w,
        *new_m,
        *new_v,
        *copies,
        jnp.reshape(loss, (1,)),
        jnp.reshape(norm, (1,)),
    )


def solution(mesh):
    weights = (
        P("shard", None),
        P(None, "shard", None),
        P("shard", None),
        P(None, "shard"),
        P(None, "shard"),
    )
    both = ("group", "shard")
    in_specs = (P(both, None, None), P(both), P(both, None), P(both, None), P()) + weights * 3
    out_specs = weights * 4 + (P(), P())
    return jax.shard_map(
        per_device, mesh=mesh, in_specs=in_specs, out_specs=out_specs, check_vma=False
    )
```

```python
import functools

import jax
import jax.numpy as jnp
from jax import lax
from jax.experimental import pallas as pl
from jax.experimental.pallas import tpu as pltpu
from jax.sharding import PartitionSpec as P

D = 768
CH = 512
HEADS = 12
HEAD_DIM = 64
FF = 3072
CD = 256
CODES = 500
CPAD = 512
LEN = 512
SPAN = 10
NVEC = 14

beta_one = 0.9
beta_two = 0.999
rate = 0.03
decay = 0.01
adam_eps = 1e-08
clip_norm = 0.01
temper = 10.0

F32 = jnp.float32
BF16 = jnp.bfloat16
VMEM_BYTES = 60 * 1024 * 1024


def product(left, right):
    return jnp.dot(left, right, preferred_element_type=F32)


def product_nt(left, right):
    return lax.dot_general(left, right, (((1,), (1,)), ((), ())), preferred_element_type=F32)


def product_tn(left, right):
    return lax.dot_general(left, right, (((0,), (0,)), ((), ())), preferred_element_type=F32)


def norm_parts(values):
    centred = values - jnp.mean(values, -1, keepdims=True)
    root = lax.rsqrt(jnp.mean(centred * centred, -1, keepdims=True) + 1e-05)
    return centred * root, root


def norm_back(upstream, hat, root, gain):
    scaled = upstream * gain
    return root * (
        scaled
        - jnp.mean(scaled, -1, keepdims=True)
        - hat * jnp.mean(scaled * hat, -1, keepdims=True)
    )


def column_sum(values):
    return jnp.sum(values, 0, keepdims=True)


def gelu_pair(e):
    root = 0.7071067811865476
    reach = jnp.abs(e) * root
    tail = jnp.exp(-0.5 * e * e)
    t = 1.0 / (1.0 + 0.3275911 * reach)
    poly = t * (
        0.254829592
        + t * (-0.284496736 + t * (1.421413741 + t * (-1.453152027 + t * 1.061405429)))
    )
    half = 0.5 * poly * tail
    phi = jnp.where(e < 0.0, half, 1.0 - half)
    return e * phi, phi + e * tail * 0.3989422804014327


def params(limit=VMEM_BYTES):
    return pltpu.CompilerParams(vmem_limit_bytes=limit)


def half_masks():
    lane = lax.broadcasted_iota(jnp.int32, (1, 128), 1)
    return [(lane < HEAD_DIM).astype(BF16), (lane >= HEAD_DIM).astype(BF16)]


MESH = pl.DeviceIdType.MESH


def ceil_to(value, step):
    return -(-value // step) * step


class Part:
    def __init__(self, array, every, low, rows, col, cols):
        self.array, self.every, self.low, self.rows = array, every, low, rows
        self.col, self.cols = col, cols
        share = (rows * 2 // 5) // 16 * 16
        self.share = max(share, 16) if rows >= 32 else 0


HEAD_COLS = D + CPAD


def weight_parts(shards):
    band, down = D // shards, FF // shards
    third = D // 3
    return [
        Part(0, CH // shards, 0, CH // shards, 0, D),
        Part(1, band, 0, band, 0, 3 * D),
        Part(2, band, 0, band, 0, D),
        Part(5, CD // shards, 0, CD // shards, 0, HEAD_COLS),
        Part(3, band, 0, band, 0, 2 * D),
        Part(3, band, 0, band, 2 * D, 2 * D),
        Part(4, down, 0, down, 0, third),
        Part(4, down, 0, down, third, third),
        Part(4, down, 0, down, 2 * third, third),
    ]


FORWARD_PLAN = (
    (),
    (0, 0, 0,),
    (1, 2, 3, 1, 4, 2, 1,),
    (3, 2,),
    (5, 4, 3,),
    (6,),
    (4,),
    (7, 5,),
    (8, 6, 5,),
    (7,),
    (6, 7,),
    (8,),
    (),
    (8,),
    (),
    (),
    (),
    (),
)
BACKWARD_PLAN = (
    (0, 1,),
    (2,),
    (0,),
    (1,),
    (2,),
    (3,),
    (),
    (3, 0,),
    (),
    (4,),
    (),
    (4, 1, 0,),
    (2,),
    (1,),
    (5, 0,),
    (5, 3, 0, 1, 2,),
    (),
    (4, 3, 0,),
    (6, 1, 2,),
    (6, 5,),
    (1, 3, 4, 2,),
    (7, 7, 5, 3, 6, 4, 2, 5, 3, 7, 6, 4, 5, 7, 6, 4, 5, 7, 7, 7, 6, 6,),
)


def forward_kernel(parts, groups, shards, *refs):
    chips = shards // 2
    n = len(parts)
    refs = list(refs)

    def take(count):
        out = refs[:count]
        del refs[:count]
        return out

    len_ref, start_ref, x_ref, label_ref, win_ref, rows_ref, down_ref, head_ref, vecs_ref = take(9)
    out_w = take(6)
    vec_out, total_ref, loss_ref, gv_ref = take(4)
    out_v = take(len(FORWARD_VALUES))
    held = take(6)
    kept = take(len(FORWARD_VALUES) - 1)
    (
        flag_ref,
        a_ref,
        hb_ref,
        att_ref,
        r1_ref,
        z1_ref,
        act_ref,
        slope_ref,
        z2_ref,
        uc_ref,
        dlog_ref,
        dc_ref,
        df_ref,
        dr2_ref,
    ) = kept
    vec_all, vec_ref, cu_ref, count_ref, group_all, shard_all = take(6)
    h_ref = dr2_ref
    t_ref = act_ref
    kept.insert(3, act_ref.at[:, 0 : 3 * D])
    (xy_sems, z_sems, core_sems, vec_sems, group_sems, shard_sems, out_sems) = take(7)

    g = lax.axis_index("group")
    s = lax.axis_index("shard")
    core = lax.rem(s, 2)
    chip = s // 2
    sibling = s + 1 - 2 * core
    parity = lax.rem(g, 2)
    partner = g + 1 - 2 * parity
    frames = x_ref.shape[0]
    band, first = D // shards, CH // shards
    wide = FF // shards

    barrier = pltpu.get_barrier_semaphore()
    for e in range(1, shards):
        pl.semaphore_signal(
            barrier, 1, device_id=(g, lax.rem(s + e, shards)), device_id_type=MESH
        )
    for e in range(1, groups):
        pl.semaphore_signal(
            barrier, 1, device_id=(lax.rem(g + e, groups), s), device_id_type=MESH
        )

    def remote(ref, send_sem, recv_sem, device, dst=None):
        return pltpu.make_async_remote_copy(
            src_ref=ref,
            dst_ref=ref if dst is None else dst,
            send_sem=send_sem,
            recv_sem=recv_sem,
            device_id=device,
            device_id_type=MESH,
        )

    def region(i, shard, at, size):
        p = parts[i]
        rows = pl.ds(pl.multiple_of(shard * p.every + p.low + at, 16), size)
        return held[p.array].at[rows, p.col : p.col + p.cols]

    def chip_to(d):
        return lax.rem(chip + d, chips)

    def chip_from(d):
        return lax.rem(chip + chips - d, chips)

    def direct(i):
        return parity * parts[i].share, parts[i].rows - parts[i].share

    def xy_send(i, d):
        return remote(
            region(i, s, *direct(i)),
            xy_sems.at[0, i, d],
            xy_sems.at[1, i, d],
            (g, 2 * chip_to(d) + core),
        )

    def xy_here(i, d):
        return remote(
            region(i, 2 * chip_from(d) + core, *direct(i)),
            xy_sems.at[0, i, d],
            xy_sems.at[1, i, d],
            (g, 2 * chip_to(d) + core),
        )

    def z_copy(i, d, arriving):
        rest = parts[i].rows - parts[i].share
        start = (1 - parity if arriving else parity) * rest
        return remote(
            region(i, 2 * chip_from(d) + core, start, parts[i].share),
            z_sems.at[0, i, d],
            z_sems.at[1, i, d],
            (partner, s),
        )

    def core_copy(i, d, which, arriving):
        side = 1 - core if arriving else core
        shard = 2 * chip_from(d) + side
        if d == 0:
            span = (0, parts[i].rows)
        elif which == 0:
            span = direct(i)
        else:
            span = ((1 - parity) * (parts[i].rows - parts[i].share), parts[i].share)
        return remote(
            region(i, shard, *span),
            core_sems.at[0, i, d, which],
            core_sems.at[1, i, d, which],
            (g, sibling),
        )

    def vec_send(d):
        return remote(
            vec_all.at[s], vec_sems.at[0, d], vec_sems.at[1, d], (g, lax.rem(s + d, shards))
        )

    def vec_here(d):
        return remote(
            vec_all.at[lax.rem(s + shards - d, shards)],
            vec_sems.at[0, d],
            vec_sems.at[1, d],
            (g, lax.rem(s + d, shards)),
        )

    def group_copy(e):
        return remote(
            count_ref,
            group_sems.at[0, e],
            group_sems.at[1, e],
            (lax.rem(g + e, groups), s),
            group_all.at[g],
        )

    def shard_copy(e):
        return remote(
            total_ref,
            shard_sems.at[0, e],
            shard_sems.at[1, e],
            (g, lax.rem(s + e, shards)),
            shard_all.at[s],
        )

    def settle(ref, source, every):
        ref[pl.ds(pl.multiple_of(s * every, 16), every)] = source.astype(BF16)

    def launch(*some):
        for i in some:
            for d in range(1, chips):
                xy_send(i, d).start()
            core_copy(i, 0, 0, False).start()

    vec_all[s] = jnp.zeros(vec_all.shape[1:], BF16)
    vec_all[s, 0:NVEC] = vecs_ref[...].astype(BF16)
    settle(held[0], win_ref[...], first)
    settle(held[1], rows_ref[0, :, : 3 * D], band)
    pl.semaphore_wait(barrier, shards - 1 + groups - 1)
    for d in range(1, shards):
        vec_send(d).start()
    launch(0, 1)
    settle(held[2], rows_ref[0, :, 3 * D :], band)
    every = CD // shards
    here = pl.ds(pl.multiple_of(s * every, 16), every)
    held[5][here, D + CPAD - 128 :] = jnp.zeros((every, 128), BF16)
    held[5][here, : D + CODES] = head_ref[...].astype(BF16)
    settle(held[3], rows_ref[1], band)
    settle(held[4], down_ref[...], wide)
    launch(*range(2, n))

    position = lax.broadcasted_iota(jnp.int32, (1, LEN), 1)
    local = jnp.zeros((1, 1), F32)
    for u in range(frames // LEN):
        length = len_ref[u]

        def span(j, inside):
            begin = lax.rem(start_ref[u, j], length - SPAN + 1)
            hit = (position >= begin) & (position < begin + SPAN)
            return jnp.where(hit, 1.0, inside)

        inside = lax.fori_loop(0, start_ref.shape[1], span, jnp.zeros((1, LEN), F32))
        masked = jnp.where(position < length, inside, 0.0)
        shift = jnp.where(position < length, 0.0, -1e30)
        label = label_ref[u : u + 1].astype(F32)
        lines = jnp.concatenate([masked, shift, label, jnp.zeros((5, LEN), F32)], 0)
        flag_ref[u * LEN : (u + 1) * LEN] = lines.T
        local = local + jnp.sum(masked, 1, keepdims=True)
    count_ref[...] = jnp.broadcast_to(local, (8, 128))
    for e in range(1, groups):
        group_copy(e).start()
    group_all[g] = count_ref[...]

    outs = [
        pltpu.make_async_copy(held[k], out_w[k], out_sems.at[k]) for k in range(6)
    ]

    def arrive(i):
        for d in range(1, chips):
            xy_here(i, d).wait_recv()
            if parts[i].share:
                z_copy(i, d, False).start()
            core_copy(i, d, 0, False).start()

    def relay(i):
        if parts[i].share:
            for d in range(1, chips):
                z_copy(i, d, True).wait_recv()
                core_copy(i, d, 1, False).start()

    def complete(i):
        core_copy(i, 0, 0, True).wait_recv()
        for d in range(1, chips):
            core_copy(i, d, 0, True).wait_recv()
            if parts[i].share:
                core_copy(i, d, 1, True).wait_recv()
        if all(done[k] == 3 for k in range(n) if parts[k].array == parts[i].array):
            outs[parts[i].array].start()

    done = [0] * n
    plan = iter(FORWARD_PLAN)

    def tick():
        for i in next(plan):
            done[i] += 1
            (arrive, relay, complete)[done[i] - 1](i)

    for e in range(1, groups):
        group_copy(e).wait_recv()
    total = group_all[0]
    for p in range(1, groups):
        total = total + group_all[p]
    total_ref[...] = total
    for e in range(1, shards):
        shard_copy(e).start()
    shard_all[s] = total

    for d in range(1, shards):
        vec_here(d).wait_recv()
    for b in range(shards):
        vec_ref[:, b * wide : (b + 1) * wide] = vec_all[b].astype(F32)
    vec_copy = pltpu.make_async_copy(vec_ref, vec_out, out_sems.at[6])
    vec_copy.start()

    copies = [vec_copy]

    def leave(k):
        copy = pltpu.make_async_copy(kept[k], out_v[k], out_sems.at[7 + k])
        copy.start()
        copies.append(copy)

    def each_tile(body):
        def once(i, carry):
            body(pl.ds(pl.multiple_of(i * 256, 256), 256))
            return carry

        lax.fori_loop(0, frames // 256, once, 0)

    def vec(row, width=D):
        return vec_ref[row : row + 1, :width]

    def normalise(rows):
        hat, _ = norm_parts(x_ref[rows].astype(F32))
        a_ref[rows] = (hat * vec(0, CH) + vec(1, CH)).astype(BF16)

    tick()
    each_tile(normalise)
    leave(0)
    leave(1)

    def hide(rows):
        hidden = product(a_ref[rows], held[0][...]) + vec(2)
        hidden = jnp.where(flag_ref[rows, 0:1] > 0.0, vec(3), hidden)
        h_ref[rows] = hidden
        hb_ref[rows] = hidden.astype(BF16)

    tick()
    each_tile(hide)
    leave(2)

    def triple(rows):
        low = hb_ref[rows]
        t_ref[rows, :D] = (product(low, held[1][:, :D]) + vec(4)).astype(BF16)
        t_ref[rows, D : 2 * D] = product(low, held[1][:, D : 2 * D]).astype(BF16)
        t_ref[rows, 2 * D : 3 * D] = (product(low, held[1][:, 2 * D :]) + vec(5)).astype(BF16)

    tick()
    each_tile(triple)
    leave(3)
    triple_copy = copies.pop()

    halves = half_masks()
    pairs = D // 128

    def attention(i, carry):
        u = i // pairs
        j = lax.rem(i, pairs)
        rows = pl.ds(pl.multiple_of(u * LEN, LEN), LEN)

        def lanes(block):
            return pl.ds(pl.multiple_of((j + block * pairs) * 128, 128), 128)

        shift = flag_ref[rows, 1:2]
        keys, values, query = (t_ref[rows, lanes(b)] for b in (1, 2, 0))
        out = None
        for half in halves:
            scores = product_nt(keys, query * half) * HEAD_DIM ** (-0.5) + shift
            power = jnp.exp(scores - jnp.max(scores, 0, keepdims=True))
            probs = (power * (1.0 / jnp.sum(power, 0, keepdims=True))).astype(BF16)
            part = product_tn(probs, values * half)
            out = part if out is None else out + part
        att_ref[rows, lanes(0)] = out.astype(BF16)
        return carry

    rounds = (frames // LEN) * pairs
    cut = [rounds * i // 6 for i in range(7)]
    for i in range(6):
        tick()
        lax.fori_loop(cut[i], cut[i + 1], attention, 0)
    leave(4)
    triple_copy.wait()

    def branch(rows):
        resid = h_ref[rows] + product(att_ref[rows], held[2][...]) + vec(6)
        r1_ref[rows] = resid
        hat, _ = norm_parts(resid)
        first = hat * vec(7) + vec(8)
        h_ref[rows] = first
        z1_ref[rows] = first.astype(BF16)

    tick()
    each_tile(branch)
    leave(5)
    leave(6)

    def upper(c):
        cols = slice(c * D, (c + 1) * D)

        def body(rows):
            before = product(z1_ref[rows], held[3][:, cols]) + vec_ref[9:10, cols]
            active, slope = gelu_pair(before)
            act_ref[rows, cols] = active.astype(BF16)
            slope_ref[rows, cols] = slope

        each_tile(body)

    for c in range(FF // D):
        tick()
        upper(c)
    leave(7)
    leave(8)

    def lower_some(k):
        cols = slice(k * (D // 3), (k + 1) * (D // 3))

        def body(rows):
            h_ref[rows, cols] += product(act_ref[rows], held[4][:, cols])

        each_tile(body)

    for k in range(3):
        tick()
        lower_some(k)
    tick()

    for e in range(1, shards):
        shard_copy(e).wait_recv()
    for e in range(1, shards):
        shard_copy(e).wait_send()
    count = shard_all[0]
    for p in range(1, shards):
        count = count + shard_all[p]
    total_ref[...] = count
    scale = 1.0 / count[0:1, 0:1]
    codes = held[5][:, D:].astype(F32)
    cu_ref[...] = (
        codes * lax.rsqrt(jnp.sum(codes * codes, 0, keepdims=True) + 1e-06)
    ).astype(BF16)
    gv_ref[...] = jnp.zeros_like(gv_ref)
    loss_ref[...] = jnp.zeros_like(loss_ref)

    def lower(rows):
        masked = flag_ref[rows, 0:1]
        wh = held[5][:, :D]
        resid = h_ref[rows] + vec(10)
        hat, root = norm_parts(resid)
        second = (hat * vec(11) + vec(12)).astype(BF16)
        z2_ref[rows] = second
        head = product_nt(second, wh) + vec(13, CD)
        root_head = lax.rsqrt(jnp.sum(head * head, -1, keepdims=True) + 1e-06)
        unit = head * root_head
        unit_low = unit.astype(BF16)
        uc_ref[rows] = unit_low
        logits = temper * product(unit_low, cu_ref[...])
        code = lax.broadcasted_iota(jnp.int32, logits.shape, 1).astype(F32)
        logits = jnp.where(code < CODES, logits, -1e30)
        top = jnp.max(logits, -1, keepdims=True)
        power = jnp.exp(logits - top)
        total = jnp.sum(power, -1, keepdims=True)
        onehot = code == flag_ref[rows, 2:3]
        picked = jnp.sum(jnp.where(onehot, logits, 0.0), -1, keepdims=True)
        losses = top + jnp.log(total) - picked
        loss_ref[...] += jnp.sum(jnp.where(masked > 0.0, losses, 0.0), 0, keepdims=True)
        chances = power * (1.0 / total)
        d_logit = (
            temper
            * (jnp.where(masked > 0.0, chances - jnp.where(onehot, 1.0, 0.0), 0.0) * scale)
        ).astype(BF16)
        dlog_ref[rows] = d_logit
        d_unit = product_nt(d_logit, cu_ref[...])
        d_head = (
            root_head * (d_unit - unit * jnp.sum(d_unit * unit, -1, keepdims=True))
        ).astype(BF16)
        dc_ref[rows] = d_head
        gv_ref[13:14, :CD] += column_sum(d_head.astype(F32))
        d_second = product(d_head, wh)
        gv_ref[11:12, :D] += column_sum(d_second * hat)
        gv_ref[12:13, :D] += column_sum(d_second)
        d_resid = norm_back(d_second, hat, root, vec(11))
        dr2_ref[rows] = d_resid
        d_lower = d_resid.astype(BF16)
        df_ref[rows] = d_lower
        gv_ref[10:11, :D] += column_sum(d_lower.astype(F32))

    each_tile(lower)
    for k in range(9, len(kept)):
        leave(k)

    for i in range(n):
        core_copy(i, 0, 0, False).wait_send()
        for d in range(1, chips):
            xy_send(i, d).wait_send()
            core_copy(i, d, 0, False).wait_send()
            if parts[i].share:
                z_copy(i, d, False).wait_send()
                core_copy(i, d, 1, False).wait_send()
    for d in range(1, shards):
        vec_send(d).wait_send()
    for e in range(1, groups):
        group_copy(e).wait_send()
    for copy in outs + copies:
        copy.wait()


FORWARD_VALUES = (
    (8, F32),
    (CH, BF16),
    (D, BF16),
    (3 * D, BF16),
    (D, BF16),
    (D, F32),
    (D, BF16),
    (FF, BF16),
    (FF, F32),
    (D, BF16),
    (CD, BF16),
    (CPAD, BF16),
    (CD, BF16),
    (D, BF16),
    (D, F32),
)


def forward(groups, shards, lengths, starts, x, labels, weights):
    parts = weight_parts(shards)
    n = len(parts)
    chips = shards // 2
    frames = x.shape[0]
    hbm = pl.BlockSpec(memory_space=pl.ANY)
    vmem = pl.BlockSpec(memory_space=pltpu.VMEM)
    smem = pl.BlockSpec(memory_space=pltpu.SMEM)
    dma = pltpu.SemaphoreType.DMA
    arrays = [(CH, D), (D, 3 * D), (D, D), (D, FF), (FF, D), (CD, HEAD_COLS)]
    many = len(FORWARD_VALUES)
    results = pl.pallas_call(
        functools.partial(forward_kernel, parts, groups, shards),
        in_specs=[smem] * 2 + [vmem] * 7,
        out_specs=[hbm] * 7 + [vmem] * 3 + [hbm] * many,
        out_shape=[jax.ShapeDtypeStruct(shape, BF16) for shape in arrays]
        + [jax.ShapeDtypeStruct((16, FF), F32)]
        + [jax.ShapeDtypeStruct((8, 128), F32)] * 2
        + [jax.ShapeDtypeStruct((16, FF), F32)]
        + [jax.ShapeDtypeStruct((frames, width), kind) for width, kind in FORWARD_VALUES],
        scratch_shapes=[pltpu.VMEM(shape, BF16) for shape in arrays]
        + [
            pltpu.VMEM((frames, width), kind)
            for width, kind in FORWARD_VALUES
            if width != 3 * D
        ]
        + [
            pltpu.VMEM((shards, 16, FF // shards), BF16),
            pltpu.VMEM((16, FF), F32),
            pltpu.VMEM((CD, CPAD), BF16),
            pltpu.VMEM((8, 128), F32),
            pltpu.VMEM((groups, 8, 128), F32),
            pltpu.VMEM((shards, 8, 128), F32),
            dma((2, n, chips)),
            dma((2, n, chips)),
            dma((2, n, chips, 2)),
            dma((2, shards)),
            dma((2, groups)),
            dma((2, shards)),
            dma((7 + many,)),
        ],
        compiler_params=pltpu.CompilerParams(
            collective_id=2, has_side_effects=True, vmem_limit_bytes=64 * 1024 * 1024 - 65536
        ),
        name="forward",
    )(lengths, starts, x, labels, *weights)
    return results[:6], results[6], results[7], results[8], results[9], results[10:]


class Chunk:
    def __init__(self, rows, group, slot, sum_slot, wide_xy, wide_z, ring=True):
        self.ring = ring
        self.used = sum(rows)
        self.starts = [sum(rows[:i]) for i in range(len(rows))]
        self.rows = ceil_to(self.used, 16 * group)
        self.part = self.rows // group
        self.slot = slot
        self.sum_slot = sum_slot
        self.kind_xy = F32 if wide_xy else BF16
        self.kind_z = F32 if wide_z else BF16


HEAD_SLOT = 2


def gradient_chunks(groups, shards):
    down, band = FF // shards, D // shards
    half = down // 2
    return [
        Chunk([half], groups, 0, 0, False, True),
        Chunk([half], groups, 1, 1, False, True),
        Chunk([CD // shards] * 2, groups, HEAD_SLOT, 4, True, True),
        Chunk([band] * 2, groups, 0, 2, False, False),
        Chunk([band] * 2, groups, 1, 3, False, False),
        Chunk([band] * 2, groups, 0, 0, False, False),
        Chunk([band] * 2, groups, 1, 1, False, False),
        Chunk([CH // shards, 16], groups, 0, 5, False, False, False),
    ]


def tiles(rows, step, body):
    def once(i, carry):
        body(pl.ds(pl.multiple_of(i * step, step), step))
        return carry

    lax.fori_loop(0, rows // step, once, 0)


def backward_kernel(chunks, groups, shards, *refs):
    chips = shards // 2
    n = len(chunks)
    refs = list(refs)

    def take(count):
        out = refs[:count]
        del refs[:count]
        return out

    weights_hbm = take(6)
    vec_hbm, gvin_ref, loss_ref = take(3)
    (
        flag_hbm,
        a_hbm,
        hid_hbm,
        triple_hbm,
        att_hbm,
        r1_hbm,
        z1_hbm,
        act_hbm,
        slope_hbm,
        z2_hbm,
        uc_hbm,
        dlog_hbm,
        dc_hbm,
        df_hbm,
        dr2_hbm,
    ) = take(len(FORWARD_VALUES))
    (x_hbm,) = take(1)
    win_hbm, wqkv_hbm, wo_hbm, wu_hbm, wd_hbm, head_hbm = weights_hbm
    ring = take(n)
    (stat_out,) = take(1)
    pool, heads, dr1_ref, wide_ref, gv_ref, vec_ref, code_ref, flag_ref = take(8)
    full = take(3)
    pair = take(3)
    send_xy, recv_xy = take(3), take(n)
    acc = take(6)
    send_z, recv_z = take(n), take(n)
    stat_ref, group_all, stat_all = take(3)
    (
        load_sems,
        core_sems,
        credit,
        xy_sems,
        z_sems,
        right_sems,
        left_sems,
        loss_sems,
        stat_sems,
    ) = take(9)

    g = lax.axis_index("group")
    s = lax.axis_index("shard")
    core = lax.rem(s, 2)
    chip = s // 2
    sibling = s + 1 - 2 * core
    parts = FF // D
    frames = x_hbm.shape[0]

    def load(src, dst, sem):
        return pltpu.make_async_copy(src, dst, load_sems.at[sem])

    def cols(ref, c):
        return ref.at[:, c * D : (c + 1) * D]

    loads = {
        "df": load(df_hbm, pool.at[0], 0),
        "z1": load(z1_hbm, pool.at[3], 3),
        "z2": load(z2_hbm, heads.at[0], 8),
        "dc": load(dc_hbm, heads.at[1, :, 0:CD], 9),
        "uc": load(uc_hbm, heads.at[1, :, CD : 2 * CD], 10),
        "dlog": load(dlog_hbm, heads.at[2, :, 0:CPAD], 11),
        "hid": load(hid_hbm, pool.at[0], 0),
        "att": load(att_hbm, pool.at[4], 4),
        "x": load(x_hbm, pool.at[5, :, 0:CH], 5),
        "win": load(win_hbm, pool.at[6, 0:CH], 6),
        "dr2": load(dr2_hbm, dr1_ref, 7),
        "r1": load(r1_hbm, wide_ref, 14),
        "wo": load(wo_hbm, pool.at[2, 0:D], 2),
        "flags": load(flag_hbm, flag_ref, 15),
        "vec": load(vec_hbm, vec_ref, 16),
        "q": load(cols(triple_hbm, 0), heads.at[0], 8),
        "k": load(cols(triple_hbm, 1), heads.at[1], 9),
        "v": load(cols(triple_hbm, 2), heads.at[2], 11),
        "a": load(a_hbm, heads.at[3, :, 0:CH], 12),
        "codes": load(head_hbm.at[:, D:HEAD_COLS], code_ref, 13),
    }
    for c in range(parts):
        loads["act", c] = load(cols(act_hbm, c), pool.at[1 + c % 2], 1 + c % 2)
        loads["slope", c] = load(cols(slope_hbm, c), wide_ref, 14)
        loads["wd", c] = load(wd_hbm.at[c * D : (c + 1) * D], pool.at[2, 0:D], 2)
        loads["wu", c] = load(cols(wu_hbm, c), pool.at[5, 0:D], 5)
    for c in range(3):
        loads["w", c] = load(cols(wqkv_hbm, c), pool.at[1 + c, 0:D], 1 + c)

    def fetch(*names):
        for name in names:
            loads[name].start()

    def ready(*names):
        for name in names:
            loads[name].wait()

    fetch("df", ("act", 0), ("act", 1), "z2", "dc", "uc", "dlog", "codes", ("slope", 0), ("wu", 0))
    fetch("z1", "dr2", "flags", "vec")

    barrier = pltpu.get_barrier_semaphore()
    for e in range(1, shards):
        pl.semaphore_signal(
            barrier, 1, device_id=(g, lax.rem(s + e, shards)), device_id_type=MESH
        )
    for e in range(1, groups):
        pl.semaphore_signal(
            barrier, 1, device_id=(lax.rem(g + e, groups), s), device_id_type=MESH
        )
    pl.semaphore_wait(barrier, shards - 1 + groups - 1)

    def remote(src, dst, send_sem, recv_sem, device):
        return pltpu.make_async_remote_copy(
            src_ref=src,
            dst_ref=dst,
            send_sem=send_sem,
            recv_sem=recv_sem,
            device_id=device,
            device_id_type=MESH,
        )

    def chip_at(d):
        return lax.rem(chip + d, chips)

    order_out = list(range(1, chips)) + [0]

    def core_copy(t, d):
        c = chunks[t]
        q = chip_at(d)
        return remote(
            full[c.slot].at[q, 1 - core, 0 : c.used],
            pair[c.slot].at[q, 0 : c.used],
            core_sems.at[0, t, d],
            core_sems.at[1, t, d],
            (g, sibling),
        )

    before = {}
    for t, c in enumerate(chunks):
        earlier = [i for i in range(t) if chunks[i].slot == c.slot]
        before[t] = earlier[-1] if earlier else None
    last_of = {c.slot: t for t, c in enumerate(chunks)}

    def free_buffer(t):
        if before[t] is not None:
            for d in order_out:
                core_copy(before[t], d).wait_send()

    def stage_pair(t):
        if before[t] is not None:
            pl.semaphore_wait(credit.at[chunks[t].slot], 1)
        for d in order_out:
            core_copy(t, d).start()

    def xy_copy(t, d):
        return remote(
            send_xy[chunks[t].slot].at[d - 1, 0 : chunks[t].used],
            recv_xy[t].at[d - 1],
            xy_sems.at[0, t, d],
            xy_sems.at[1, t, d],
            (g, 2 * chip_at(d) + core),
        )

    def stage_chips(t):
        c = chunks[t]
        own, other = full[c.slot], pair[c.slot]
        for d in order_out:
            q = chip_at(d)
            core_copy(t, d).wait_recv()
            if d > 0 and before[t] is not None:
                xy_copy(before[t], d).wait_send()
            if d == 0:

                def keep(rows):
                    acc[c.sum_slot][rows] = own[q, core, rows] + other[q, rows]

                tiles(c.used, 16, keep)
                if c.rows > c.used:
                    acc[c.sum_slot][c.used : c.rows] = jnp.zeros((c.rows - c.used, D), F32)
            else:

                def send(rows):
                    send_xy[c.slot][d - 1, rows] = (own[q, core, rows] + other[q, rows]).astype(
                        c.kind_xy
                    )

                tiles(c.used, 16, send)
                xy_copy(t, d).start()
        if t != last_of[c.slot]:
            pl.semaphore_signal(
                credit.at[c.slot], 1, device_id=(g, sibling), device_id_type=MESH
            )

    def z_copy(t, e):
        return remote(
            send_z[t].at[e - 1],
            recv_z[t].at[e - 1],
            z_sems.at[0, t, e],
            z_sems.at[1, t, e],
            (lax.rem(g + e, groups), s),
        )

    def stage_group(t):
        c = chunks[t]
        total_ref = acc[c.sum_slot]
        for d in range(1, chips):
            xy_copy(t, d).wait_recv()

        def add(rows):
            total = total_ref[rows]
            for d in range(1, chips):
                total = total + recv_xy[t][d - 1, rows].astype(F32)
            total_ref[rows] = total

        tiles(c.used, 16, add)
        for e in range(1, groups):
            base = pl.multiple_of(lax.rem(g + e, groups) * c.part, 16)

            def send(rows):
                here = pl.ds(pl.multiple_of(base + rows.start, 16), 16)
                send_z[t][e - 1, rows] = total_ref[here].astype(BF16)

            tiles(c.part, 16, send)
            z_copy(t, e).start()

    def part_rows(t, p):
        return pl.ds(pl.multiple_of(p * chunks[t].part, 16), chunks[t].part)

    def ring_copy(t, k, way, back=0):
        p = g - k if way == 0 else g + k
        side = lax.rem(g + 1, groups) if way == 0 else lax.rem(g + groups - 1, groups)
        sems = right_sems if way == 0 else left_sems
        rows = part_rows(t, p)
        return remote(
            ring[t].at[rows],
            ring[t].at[rows],
            sems.at[0, t, k],
            sems.at[1, t, k - back],
            (side, s),
        )

    def near_copy(t, e, p):
        rows = part_rows(t, p)
        return remote(
            ring[t].at[rows],
            ring[t].at[rows],
            right_sems.at[0, t, e],
            right_sems.at[1, t, e],
            (lax.rem(g + e, groups), s),
        )

    def holds(k, way):
        return g >= k if way == 0 else g + k < groups

    def sends(k, way):
        return (g >= k) & (g < groups - 1) if way == 0 else (g + k < groups) & (g > 0)

    def stage_total(t):
        c = chunks[t]
        total_ref = acc[c.sum_slot]
        for e in range(1, groups):
            z_copy(t, e).wait_recv()
        base = pl.multiple_of(g * c.part, 16)

        def add(i, sums):
            rows = pl.ds(pl.multiple_of(i * 16, 16), 16)
            here = pl.ds(pl.multiple_of(base + i * 16, 16), 16)
            total = total_ref[here]
            for e in range(1, groups):
                total = total + recv_z[t][e - 1, rows].astype(F32)
            total = total.astype(c.kind_z)
            ring[t][here] = total
            total = total.astype(F32)
            total = total * total
            return sums + total[:8] + total[8:]

        squares[0] = lax.fori_loop(0, c.part // 16, add, squares[0])
        if not c.ring:
            for e in range(1, groups):
                near_copy(t, e, g).start()
            return
        for way in (0, 1):

            @pl.when(sends(0, way))
            def _():
                ring_copy(t, 0, way).start()

    def stage_ring(t, k):
        if not chunks[t].ring:
            if k == 1:
                for e in range(1, groups):
                    near_copy(t, e, lax.rem(g + groups - e, groups)).wait_recv()
            return
        for way in (0, 1):

            @pl.when(holds(k, way))
            def _():
                ring_copy(t, k, way, 1).wait_recv()

            if k < groups - 1:

                @pl.when(sends(k, way))
                def _():
                    ring_copy(t, k, way).start()

    done = [0] * n
    squares = [jnp.zeros((8, D), F32)]

    def step(t):
        now = done[t]
        done[t] += 1
        if now == 0:
            stage_pair(t)
        elif now == 1:
            same = [u for u in range(t) if chunks[u].sum_slot == chunks[t].sum_slot]
            assert all(done[u] > 3 for u in same)
            stage_chips(t)
        elif now == 2:
            stage_group(t)
        elif now == 3:
            stage_total(t)
        else:
            stage_ring(t, now - 3)

    plan = iter(BACKWARD_PLAN)

    def tick():
        for t in next(plan):
            step(t)

    def scatter(value, slots, at, per, first_shard, col=0):
        count = value.shape[0] // per
        each = per // len(slots)
        for k in range(count):
            shard = first_shard * 1 + k
            for i, slot in enumerate(slots):
                rows = value[k * per + i * each : k * per + (i + 1) * each]
                full[slot][
                    shard // 2, lax.rem(shard, 2), at : at + each, col : col + rows.shape[1]
                ] = rows

    def grad(left, right, slots, at, per, block, col=0):
        width = left.shape[1]

        def once(i, carry):
            some = left[:, pl.ds(pl.multiple_of(i * block, 128), block)]
            scatter(product_tn(some, right[...]), slots, at, per, i * (block // per), col)
            return carry

        lax.fori_loop(0, width // block, once, 0)

    down, band, deep, first = FF // shards, D // shards, CD // shards, CH // shards
    wide = FF // shards
    pairs = D // 128

    ready("df")
    for c in range(parts):
        ready(("act", c))
        for i in range(2):
            value = product_tn(
                pool[1 + c % 2, :, i * (D // 2) : (i + 1) * (D // 2)], pool[0]
            )
            scatter(value, [0, 1], 0, down, (c * D + i * (D // 2)) // down)
        if c + 2 < parts:
            fetch(("act", c + 2))
    fetch(("wd", 0))
    tick()
    ready("z2", "dc", "uc", "dlog", "codes")
    scatter(product_tn(heads[1, :, 0:CD], heads[0]), [HEAD_SLOT], 0, deep, 0)
    d_unit = product_tn(heads[1, :, CD : 2 * CD], heads[2, :, 0:CPAD])
    codes = code_ref[...].astype(F32)
    root = lax.rsqrt(jnp.sum(codes * codes, 0, keepdims=True) + 1e-06)
    unit = codes * root
    d_codes = root * (d_unit - unit * jnp.sum(d_unit * unit, 0, keepdims=True))
    scatter(d_codes, [HEAD_SLOT], deep, deep, 0)
    full[HEAD_SLOT][:, :, deep : 2 * deep, CPAD:D] = jnp.zeros((chips, 2, deep, D - CPAD), F32)
    fetch("q", "k", "v", "att", "win")
    tick()
    ready("z1", "dr2", "flags", "vec")
    gv_ref[...] = gvin_ref[...]

    def each_tile(body, begin=0, end=None):
        def once(i, carry):
            body(pl.ds(pl.multiple_of(i * 256, 256), 256))
            return carry

        lax.fori_loop(begin, frames // 256 if end is None else end, once, 0)

    for t, first_part in ((3, 0), (4, 2)):
        for i in range(2):
            c = first_part + i
            span = slice(c * D, (c + 1) * D)
            ready(("slope", c), ("wd", c), ("wu", c))

            def lower(rows):
                d_before = wide_ref[rows] * product_nt(pool[0, rows], pool[2, 0:D])
                d_before = d_before.astype(BF16)
                pool[1, rows] = d_before
                gv_ref[9:10, span] += column_sum(d_before.astype(F32))
                dr1_ref[rows] += product_nt(d_before, pool[5, 0:D])

            each_tile(lower)
            tick()
            if i == 0:
                free_buffer(t)
            if c + 1 < parts:
                fetch(("slope", c + 1), ("wd", c + 1), ("wu", c + 1))
            else:
                fetch("r1", "wo", "hid")
            grad(pool.at[3], pool.at[1], [chunks[t].slot], i * band, band, D // 2)
            tick()
    ready("r1", "wo")

    def branch(rows):
        hat, root = norm_parts(wide_ref[rows])
        d_first = dr1_ref[rows]
        gv_ref[7:8, :D] += column_sum(d_first * hat)
        gv_ref[8:9, :D] += column_sum(d_first)
        d_resid = norm_back(d_first, hat, root, vec_ref[7:8, :D])
        dr1_ref[rows] = d_resid
        d_branch = d_resid.astype(BF16)
        pool[5, rows] = d_branch
        gv_ref[6:7, :D] += column_sum(d_branch.astype(F32))
        heads[3, rows] = product_nt(d_branch, pool[2, 0:D]).astype(BF16)

    each_tile(branch)
    for c in range(3):
        fetch(("w", c))
    tick()

    halves = half_masks()
    utters = frames // LEN

    def attention(i, carry):
        rows = pl.ds(pl.multiple_of(lax.rem(i, utters) * LEN, LEN), LEN)
        lanes = pl.ds(pl.multiple_of((i // utters) * 128, 128), 128)
        shift = flag_ref[rows, 1:2]
        keys, values = heads[1, rows, lanes], heads[2, rows, lanes]
        dq = dk = dv = None
        for half in halves:
            query = heads[0, rows, lanes] * half
            upstream = heads[3, rows, lanes] * half
            scores = product_nt(keys, query) * HEAD_DIM ** (-0.5) + shift
            power = jnp.exp(scores - jnp.max(scores, 0, keepdims=True))
            probs = power * (1.0 / jnp.sum(power, 0, keepdims=True))
            part_v = product(probs.astype(BF16), upstream)
            d_probs = product_nt(values, upstream)
            weight = jnp.sum(probs * d_probs, 0, keepdims=True)
            d_scores = (probs * (d_probs - weight) * HEAD_DIM ** (-0.5)).astype(BF16)
            part_k = product(d_scores, query)
            part_q = product_tn(d_scores, keys * half)
            dq = part_q if dq is None else dq + part_q
            dk = part_k if dk is None else dk + part_k
            dv = part_v if dv is None else dv + part_v
        heads[0, rows, lanes] = dq.astype(BF16)
        heads[1, rows, lanes] = dk.astype(BF16)
        heads[2, rows, lanes] = dv.astype(BF16)
        return carry

    ready("q", "k", "v")
    rounds = utters * pairs
    middle = D // 2

    def attend(begin, end):
        cut = [begin + (end - begin) * i // 3 for i in range(4)]
        for i in range(3):
            lax.fori_loop(cut[i], cut[i + 1], attention, 0)
            tick()

    attend(0, rounds // 2)
    ready("hid", "att")
    free_buffer(5)
    grad(pool.at[0], heads.at[0, :, 0:middle], [0], 0, band, middle)
    grad(pool.at[0], heads.at[1, :, 0:middle], [0], 0, band, middle, middle)
    grad(pool.at[4], pool.at[5], [0], band, band, middle)
    tick()
    fetch("x")
    attend(rounds // 2, rounds)
    fetch("a")
    free_buffer(6)
    grad(pool.at[0], heads.at[2], [1], 0, band, middle)
    grad(pool.at[0], heads.at[0, :, middle:D], [1], band, band, middle)
    grad(pool.at[0], heads.at[1, :, middle:D], [1], band, band, middle, middle)
    tick()
    ready(("w", 0), ("w", 1), ("w", 2), "win", "x")

    def back(rows):
        dq, dk, dv = heads[0, rows], heads[1, rows], heads[2, rows]
        gv_ref[4:5, :D] += column_sum(dq.astype(F32))
        gv_ref[5:6, :D] += column_sum(dv.astype(F32))
        d_hidden = (
            dr1_ref[rows]
            + product_nt(dq, pool[1, 0:D])
            + product_nt(dk, pool[2, 0:D])
            + product_nt(dv, pool[3, 0:D])
        )
        masked = flag_ref[rows, 0:1] > 0.0
        gv_ref[3:4, :D] += column_sum(jnp.where(masked, d_hidden, 0.0))
        d_proj = jnp.where(masked, 0.0, d_hidden).astype(BF16)
        pool[4, rows] = d_proj
        gv_ref[2:3, :D] += column_sum(d_proj.astype(F32))
        d_normed = product_nt(d_proj, pool[6, 0:CH])
        hat, _ = norm_parts(pool[5, rows, 0:CH].astype(F32))
        gv_ref[0:1, :CH] += column_sum(d_normed * hat)
        gv_ref[1:2, :CH] += column_sum(d_normed)

    each_tile(back, 0, 2)
    tick()
    each_tile(back, 2)
    tick()
    ready("a")
    free_buffer(7)
    grad(heads.at[3, :, 0:CH], pool.at[4], [0], 0, first, CH // 2)
    for b in range(shards):
        full[0][b // 2, b % 2, first : first + 16, 0:wide] = gv_ref[:, b * wide : (b + 1) * wide]
        full[0][b // 2, b % 2, first : first + 16, wide:D] = jnp.zeros((16, D - wide), F32)
    final = 3 + groups
    rest = list(next(plan))

    def advance(enough):
        while rest and not enough():
            step(rest.pop(0))

    def group_copy(e):
        return remote(
            stat_ref.at[0],
            group_all.at[g],
            loss_sems.at[0, e],
            loss_sems.at[1, e],
            (lax.rem(g + e, groups), s),
        )

    def stat_copy(e):
        return remote(
            stat_ref.at[1],
            stat_all.at[s],
            stat_sems.at[0, e],
            stat_sems.at[1, e],
            (g, lax.rem(s + e, shards)),
        )

    advance(lambda: min(done) > 3)
    lane = lax.broadcasted_iota(jnp.int32, (8, 128), 1)
    stat_ref[0] = jnp.where(lane == 0, jnp.sum(squares[0]), loss_ref[...])
    for e in range(1, groups):
        group_copy(e).start()
    group_all[g] = stat_ref[0]
    left_over = len(rest) - 3
    advance(lambda: len(rest) <= left_over)
    for e in range(1, groups):
        group_copy(e).wait_recv()
    total = group_all[0]
    for p in range(1, groups):
        total = total + group_all[p]
    stat_ref[1] = total
    for e in range(1, shards):
        stat_copy(e).start()
    stat_all[s] = total
    advance(lambda: False)
    while min(done) < final:
        step(done.index(min(done)))
    for e in range(1, shards):
        stat_copy(e).wait_recv()
    total = stat_all[0]
    for p in range(1, shards):
        total = total + stat_all[p]
    stat_out[...] = total
    for t in range(n):
        if t == last_of[chunks[t].slot]:
            for d in order_out:
                core_copy(t, d).wait_send()
            for d in range(1, chips):
                xy_copy(t, d).wait_send()
        for e in range(1, groups):
            z_copy(t, e).wait_send()
            if not chunks[t].ring:
                near_copy(t, e, g).wait_send()
        for k in range(groups - 1 if chunks[t].ring else 0):
            for way in (0, 1):

                @pl.when(sends(k, way))
                def _():
                    ring_copy(t, k, way).wait_send()

    for e in range(1, groups):
        group_copy(e).wait_send()
    for e in range(1, shards):
        stat_copy(e).wait_send()


def backward(groups, shards, weights, vecs, gv, loss, values, x):
    chunks = gradient_chunks(groups, shards)
    chips = shards // 2
    n = len(chunks)
    frames = x.shape[0]
    hbm = pl.BlockSpec(memory_space=pl.ANY)
    vmem = pl.BlockSpec(memory_space=pltpu.VMEM)
    dma = pltpu.SemaphoreType.DMA
    deepest = [max(c.used for c in chunks if c.slot == i) for i in range(3)]
    sums = [max(c.rows for c in chunks if c.sum_slot == i) for i in range(6)]
    results = pl.pallas_call(
        functools.partial(backward_kernel, chunks, groups, shards),
        in_specs=[hbm] * 7 + [vmem] * 2 + [hbm] * (len(values) + 1),
        out_specs=[vmem] * (n + 1),
        out_shape=[jax.ShapeDtypeStruct((c.rows, D), c.kind_z) for c in chunks]
        + [jax.ShapeDtypeStruct((8, 128), F32)],
        scratch_shapes=[
            pltpu.VMEM((7, frames, D), BF16),
            pltpu.VMEM((4, frames, D), BF16),
            pltpu.VMEM((frames, D), F32),
            pltpu.VMEM((frames, D), F32),
            pltpu.VMEM((16, FF), F32),
            pltpu.VMEM((16, FF), F32),
            pltpu.VMEM((CD, CPAD), BF16),
            pltpu.VMEM((frames, 8), F32),
        ]
        + [pltpu.VMEM((chips, 2, rows, D), F32) for rows in deepest]
        + [pltpu.VMEM((chips, rows, D), F32) for rows in deepest]
        + [
            pltpu.VMEM((chips - 1, rows, D), F32 if i == HEAD_SLOT else BF16)
            for i, rows in enumerate(deepest)
        ]
        + [pltpu.VMEM((chips - 1, c.used, D), c.kind_xy) for c in chunks]
        + [pltpu.VMEM((rows, D), F32) for rows in sums]
        + [pltpu.VMEM((groups - 1, c.part, D), BF16) for c in chunks] * 2
        + [
            pltpu.VMEM((2, 8, 128), F32),
            pltpu.VMEM((groups, 8, 128), F32),
            pltpu.VMEM((shards, 8, 128), F32),
        ]
        + [
            dma((17,)),
            dma((2, n, chips)),
            pltpu.SemaphoreType.REGULAR((3,)),
            dma((2, n, chips)),
            dma((2, n, groups)),
            dma((2, n, groups)),
            dma((2, n, groups)),
            dma((2, groups)),
            dma((2, shards)),
        ],
        compiler_params=pltpu.CompilerParams(
            collective_id=1, has_side_effects=True, vmem_limit_bytes=64 * 1024 * 1024 - 65536
        ),
        name="backward",
    )(*weights, vecs, gv, loss, *values, x)
    return results[:n], results[n]


def adam_kernel(step_ref, stat_ref, count_ref, *refs):
    w, m, v = refs[0:5], refs[5:10], refs[10:15]
    g_head, g_tail = refs[15:17]
    early_ref, late_ref = refs[17:19]
    halves = refs[19:23]
    outs = [refs[23 + 5 * i : 28 + 5 * i] for i in range(4)]
    norm_ref, loss_ref = refs[43:45]
    step = pl.program_id(0)
    fix_one, fix_two = (
        1.0 - lax.fori_loop(0, step_ref[0], lambda _, value: value * beta, jnp.float32(1.0))
        for beta in (beta_one, beta_two)
    )
    norm = jnp.sqrt(stat_ref[0:1, 0:1])
    factor = jnp.minimum(1.0, clip_norm / (norm + 1e-06))

    def update(i, grad, where=...):
        shrink = 0.0 if i == 4 else decay
        weight, moment, square = w[i][where], m[i][where], v[i][where]
        grad = grad.astype(F32) * factor
        moment = beta_one * moment + (1.0 - beta_one) * grad
        square = beta_two * square + (1.0 - beta_two) * grad * grad
        stepped = moment / fix_one / (jnp.sqrt(square / fix_two) + adam_eps)
        weight = weight - rate * (stepped + shrink * weight)
        for out, value in zip(outs, (weight, moment, square, weight.astype(BF16))):
            out[i][where] = value

    def both(early):
        @pl.when(early == (step < 2))
        def _():
            up, down = halves[0 if early else 1 :: 2]
            update(1, up[...], 1)
            update(2, down[...])

    depth = w[1].shape[1]
    upper, lower = slice(0, depth), slice(depth, 2 * depth)
    left, right = slice(0, D // 2), slice(D // 2, D)

    @pl.when(step == 0)
    def _():
        update(1, early_ref[upper, left], (0, slice(None), left))
        update(1, late_ref[lower, left], (0, slice(None), right))

    @pl.when(step == 1)
    def _():
        update(1, early_ref[upper, right], (0, slice(None), left))
        update(1, late_ref[lower, right], (0, slice(None), right))

    @pl.when(step == 2)
    def _():
        update(1, late_ref[upper], 0)

    @pl.when(step == 3)
    def _():
        update(1, early_ref[lower], 0)

    both(True)
    both(False)

    @pl.when(step == 0)
    def _():
        first, deep = w[0].shape[0], w[3].shape[0]
        norm_ref[...] = norm
        loss_ref[...] = stat_ref[0:1, 1:2] / count_ref[0:1, 0:1]
        update(0, g_tail[:first])
        update(3, g_head[:deep], (slice(None), slice(0, D)))
        update(3, g_head[deep : 2 * deep, :CODES], (slice(None), slice(D, D + CODES)))
        update(4, g_tail[first : first + NVEC, : w[4].shape[1]])


def adam(steps, stat, count, weights, moments, seconds, sums):
    parts = FF // D
    depth = weights[1].shape[1]
    tall = weights[2].shape[0] // parts

    def fixed(a):
        return pl.BlockSpec(a.shape, lambda i: (0,) * a.ndim)

    w_specs = [
        fixed(weights[0]),
        pl.BlockSpec((2, depth, D), lambda i: (0, 0, i)),
        pl.BlockSpec((tall, D), lambda i: (i, 0)),
        fixed(weights[3]),
        fixed(weights[4]),
    ]
    g_specs = [fixed(sums[i]) for i in (2, 7, 5, 6)]
    for rows in (depth, tall):
        g_specs.append(pl.BlockSpec((rows, D), lambda i: (jnp.minimum(i, 1), 0)))
        g_specs.append(pl.BlockSpec((rows, D), lambda i: (jnp.maximum(i - 2, 0), 0)))
    shapes = [jax.ShapeDtypeStruct(w.shape, F32) for w in weights]
    low = [jax.ShapeDtypeStruct(w.shape, BF16) for w in weights]
    outs = pl.pallas_call(
        adam_kernel,
        grid=(parts,),
        in_specs=[pl.BlockSpec(memory_space=pltpu.SMEM), fixed(stat), fixed(count)]
        + w_specs * 3
        + g_specs,
        out_specs=w_specs * 4 + [pl.BlockSpec((1, 1), lambda i: (0, 0))] * 2,
        out_shape=shapes * 3 + low + [jax.ShapeDtypeStruct((1, 1), F32)] * 2,
        compiler_params=params(),
        name="adam",
    )(
        steps,
        stat,
        count,
        *weights,
        *moments,
        *seconds,
        *[sums[i] for i in (2, 7, 5, 6, 3, 4, 0, 1)],
    )
    return [outs[i * 5 : (i + 1) * 5] for i in range(4)] + list(outs[20:])


def per_device(
    features,
    lengths,
    starts,
    labels,
    step_count,
    weight_in,
    weight_rows,
    weight_down,
    weight_head,
    vectors,
    moment_in,
    moment_rows,
    moment_down,
    moment_head,
    moment_vectors,
    second_in,
    second_rows,
    second_down,
    second_head,
    second_vectors,
):
    masters = (weight_in, weight_rows, weight_down, weight_head, vectors)
    moments = (moment_in, moment_rows, moment_down, moment_head, moment_vectors)
    seconds = (second_in, second_rows, second_down, second_head, second_vectors)
    groups, shards = lax.axis_size("group"), lax.axis_size("shard")
    x = features.reshape(-1, CH)

    def turned(arrays):
        return [a.T if i == 3 else a for i, a in enumerate(arrays)]

    weights, vecs, count, loss, gv, values = forward(
        groups, shards, lengths, starts, x, labels, turned(masters)
    )
    sums, stat = backward(groups, shards, weights, vecs, gv, loss, values, x)
    *updated, norm, loss = adam(
        step_count, stat, count, turned(masters), turned(moments), turned(seconds), sums
    )
    new_w, new_m, new_v, copies = (turned(out) for out in updated)
    return (
        *new_w,
        *new_m,
        *new_v,
        *copies,
        jnp.reshape(loss, (1,)),
        jnp.reshape(norm, (1,)),
    )


def solution(mesh):
    weights = (
        P("shard", None),
        P(None, "shard", None),
        P("shard", None),
        P(None, "shard"),
        P(None, "shard"),
    )
    both = ("group", "shard")
    in_specs = (P(both, None, None), P(both), P(both, None), P(both, None), P()) + weights * 3
    out_specs = weights * 4 + (P(), P())
    return jax.shard_map(
        per_device, mesh=mesh, in_specs=in_specs, out_specs=out_specs, check_vma=False
    )
```

```python
import functools

import jax
import jax.numpy as jnp
from jax import lax
from jax.experimental import pallas as pl
from jax.experimental.pallas import tpu as pltpu
from jax.sharding import PartitionSpec as P

D = 768
CH = 512
HEADS = 12
HEAD_DIM = 64
FF = 3072
CD = 256
CODES = 500
CPAD = 512
LEN = 512
SPAN = 10
NVEC = 14

beta_one = 0.9
beta_two = 0.999
rate = 0.03
decay = 0.01
adam_eps = 1e-08
clip_norm = 0.01
temper = 10.0

F32 = jnp.float32
BF16 = jnp.bfloat16
VMEM_BYTES = 60 * 1024 * 1024


def product(left, right):
    return jnp.dot(left, right, preferred_element_type=F32)


def product_nt(left, right):
    return lax.dot_general(left, right, (((1,), (1,)), ((), ())), preferred_element_type=F32)


def product_tn(left, right):
    return lax.dot_general(left, right, (((0,), (0,)), ((), ())), preferred_element_type=F32)


def norm_parts(values):
    centred = values - jnp.mean(values, -1, keepdims=True)
    root = lax.rsqrt(jnp.mean(centred * centred, -1, keepdims=True) + 1e-05)
    return centred * root, root


def norm_back(upstream, hat, root, gain):
    scaled = upstream * gain
    return root * (
        scaled
        - jnp.mean(scaled, -1, keepdims=True)
        - hat * jnp.mean(scaled * hat, -1, keepdims=True)
    )


def column_sum(values):
    return jnp.sum(values, 0, keepdims=True)


def gelu_pair(e):
    root = 0.7071067811865476
    reach = jnp.abs(e) * root
    tail = jnp.exp(-0.5 * e * e)
    t = 1.0 / (1.0 + 0.3275911 * reach)
    poly = t * (
        0.254829592
        + t * (-0.284496736 + t * (1.421413741 + t * (-1.453152027 + t * 1.061405429)))
    )
    half = 0.5 * poly * tail
    phi = jnp.where(e < 0.0, half, 1.0 - half)
    return e * phi, phi + e * tail * 0.3989422804014327


def params(limit=VMEM_BYTES):
    return pltpu.CompilerParams(vmem_limit_bytes=limit)


def half_masks():
    lane = lax.broadcasted_iota(jnp.int32, (1, 128), 1)
    return [(lane < HEAD_DIM).astype(BF16), (lane >= HEAD_DIM).astype(BF16)]


MESH = pl.DeviceIdType.MESH


def ceil_to(value, step):
    return -(-value // step) * step


class Part:
    def __init__(self, array, every, low, rows, col, cols):
        self.array, self.every, self.low, self.rows = array, every, low, rows
        self.col, self.cols = col, cols
        share = (rows * 2 // 5) // 16 * 16
        self.share = max(share, 16) if rows >= 32 else 0


HEAD_COLS = D + CPAD


def weight_parts(shards):
    band, down = D // shards, FF // shards
    third = D // 3
    return [
        Part(0, CH // shards, 0, CH // shards, 0, D),
        Part(1, band, 0, band, 0, D),
        Part(1, band, 0, band, D, D),
        Part(1, band, 0, band, 2 * D, D),
        Part(2, band, 0, band, 0, D),
        Part(5, CD // shards, 0, CD // shards, 0, HEAD_COLS),
        Part(3, band, 0, band, 0, 2 * D),
        Part(3, band, 0, band, 2 * D, 2 * D),
        Part(4, down, 0, down, 0, third),
        Part(4, down, 0, down, third, third),
        Part(4, down, 0, down, 2 * third, third),
    ]


FORWARD_PLAN = (
    (),
    (0, 1, 0, 0,),
    (2, 1, 3, 1,),
    (4, 2, 5, 3, 2,),
    (3,),
    (4,),
    (6, 5, 4,),
    (),
    (7, 5,),
    (6,),
    (8, 6,),
    (9, 7,),
    (10, 8, 7,),
    (),
    (9, 8,),
    (10, 9,),
    (10,),
    (),
    (),
    (),
)
BACKWARD_PLAN = (
    (0, 1,),
    (2,),
    (0,),
    (1,),
    (2,),
    (3,),
    (),
    (3, 0,),
    (),
    (4,),
    (),
    (4, 1, 0,),
    (2,),
    (1,),
    (5, 0,),
    (5, 3, 0, 1, 2,),
    (),
    (4, 3, 0,),
    (6, 1, 2,),
    (6, 5,),
    (1, 3, 4, 2,),
    (7, 7, 5, 3, 6, 4, 2, 5, 3, 7, 6, 4, 5, 7, 6, 4, 5, 7, 7, 7, 6, 6,),
)


def forward_kernel(parts, groups, shards, *refs):
    chips = shards // 2
    n = len(parts)
    refs = list(refs)

    def take(count):
        out = refs[:count]
        del refs[:count]
        return out

    len_ref, start_ref, x_ref, label_ref, win_ref, rows_ref, down_ref, head_ref, vecs_ref = take(9)
    out_w = take(6)
    vec_out, total_ref, loss_ref, gv_ref = take(4)
    out_v = take(len(FORWARD_VALUES))
    held = take(6)
    kept = take(len(FORWARD_VALUES) - 1)
    (
        flag_ref,
        a_ref,
        hb_ref,
        att_ref,
        r1_ref,
        z1_ref,
        act_ref,
        slope_ref,
        z2_ref,
        uc_ref,
        dlog_ref,
        dc_ref,
        df_ref,
        dr2_ref,
    ) = kept
    vec_all, vec_ref, cu_ref, count_ref, group_all, shard_all = take(6)
    h_ref = dr2_ref
    t_ref = act_ref
    kept.insert(3, act_ref.at[:, 0 : 3 * D])
    (xy_sems, z_sems, core_sems, vec_sems, group_sems, shard_sems, out_sems) = take(7)

    g = lax.axis_index("group")
    s = lax.axis_index("shard")
    core = lax.rem(s, 2)
    chip = s // 2
    sibling = s + 1 - 2 * core
    parity = lax.rem(g, 2)
    partner = g + 1 - 2 * parity
    frames = x_ref.shape[0]
    band, first = D // shards, CH // shards
    wide = FF // shards

    barrier = pltpu.get_barrier_semaphore()
    for e in range(1, shards):
        pl.semaphore_signal(
            barrier, 1, device_id=(g, lax.rem(s + e, shards)), device_id_type=MESH
        )
    for e in range(1, groups):
        pl.semaphore_signal(
            barrier, 1, device_id=(lax.rem(g + e, groups), s), device_id_type=MESH
        )

    def remote(ref, send_sem, recv_sem, device, dst=None):
        return pltpu.make_async_remote_copy(
            src_ref=ref,
            dst_ref=ref if dst is None else dst,
            send_sem=send_sem,
            recv_sem=recv_sem,
            device_id=device,
            device_id_type=MESH,
        )

    def region(i, shard, at, size):
        p = parts[i]
        rows = pl.ds(pl.multiple_of(shard * p.every + p.low + at, 16), size)
        return held[p.array].at[rows, p.col : p.col + p.cols]

    def chip_to(d):
        return lax.rem(chip + d, chips)

    def chip_from(d):
        return lax.rem(chip + chips - d, chips)

    def direct(i):
        return parity * parts[i].share, parts[i].rows - parts[i].share

    def xy_send(i, d):
        return remote(
            region(i, s, *direct(i)),
            xy_sems.at[0, i, d],
            xy_sems.at[1, i, d],
            (g, 2 * chip_to(d) + core),
        )

    def xy_here(i, d):
        return remote(
            region(i, 2 * chip_from(d) + core, *direct(i)),
            xy_sems.at[0, i, d],
            xy_sems.at[1, i, d],
            (g, 2 * chip_to(d) + core),
        )

    def z_copy(i, d, arriving):
        rest = parts[i].rows - parts[i].share
        start = (1 - parity if arriving else parity) * rest
        return remote(
            region(i, 2 * chip_from(d) + core, start, parts[i].share),
            z_sems.at[0, i, d],
            z_sems.at[1, i, d],
            (partner, s),
        )

    def core_copy(i, d, which, arriving):
        side = 1 - core if arriving else core
        shard = 2 * chip_from(d) + side
        if d == 0:
            span = (0, parts[i].rows)
        elif which == 0:
            span = direct(i)
        else:
            span = ((1 - parity) * (parts[i].rows - parts[i].share), parts[i].share)
        return remote(
            region(i, shard, *span),
            core_sems.at[0, i, d, which],
            core_sems.at[1, i, d, which],
            (g, sibling),
        )

    def vec_send(d):
        return remote(
            vec_all.at[s], vec_sems.at[0, d], vec_sems.at[1, d], (g, lax.rem(s + d, shards))
        )

    def vec_here(d):
        return remote(
            vec_all.at[lax.rem(s + shards - d, shards)],
            vec_sems.at[0, d],
            vec_sems.at[1, d],
            (g, lax.rem(s + d, shards)),
        )

    def group_copy(e):
        return remote(
            count_ref,
            group_sems.at[0, e],
            group_sems.at[1, e],
            (lax.rem(g + e, groups), s),
            group_all.at[g],
        )

    def shard_copy(e):
        return remote(
            total_ref,
            shard_sems.at[0, e],
            shard_sems.at[1, e],
            (g, lax.rem(s + e, shards)),
            shard_all.at[s],
        )

    def settle(ref, source, every):
        ref[pl.ds(pl.multiple_of(s * every, 16), every)] = source.astype(BF16)

    def launch(*some):
        for i in some:
            for d in range(1, chips):
                xy_send(i, d).start()
            core_copy(i, 0, 0, False).start()

    vec_all[s] = jnp.zeros(vec_all.shape[1:], BF16)
    vec_all[s, 0:NVEC] = vecs_ref[...].astype(BF16)
    settle(held[0], win_ref[...], first)
    settle(held[1], rows_ref[0, :, : 3 * D], band)
    pl.semaphore_wait(barrier, shards - 1 + groups - 1)
    for d in range(1, shards):
        vec_send(d).start()
    launch(0, 1, 2, 3)
    settle(held[2], rows_ref[0, :, 3 * D :], band)
    every = CD // shards
    here = pl.ds(pl.multiple_of(s * every, 16), every)
    held[5][here, D + CPAD - 128 :] = jnp.zeros((every, 128), BF16)
    held[5][here, : D + CODES] = head_ref[...].astype(BF16)
    settle(held[3], rows_ref[1], band)
    settle(held[4], down_ref[...], wide)
    launch(*range(4, n))

    position = lax.broadcasted_iota(jnp.int32, (1, LEN), 1)
    local = jnp.zeros((1, 1), F32)
    for u in range(frames // LEN):
        length = len_ref[u]

        def span(j, inside):
            begin = lax.rem(start_ref[u, j], length - SPAN + 1)
            hit = (position >= begin) & (position < begin + SPAN)
            return jnp.where(hit, 1.0, inside)

        inside = lax.fori_loop(0, start_ref.shape[1], span, jnp.zeros((1, LEN), F32))
        masked = jnp.where(position < length, inside, 0.0)
        shift = jnp.where(position < length, 0.0, -1e30)
        label = label_ref[u : u + 1].astype(F32)
        lines = jnp.concatenate([masked, shift, label, jnp.zeros((5, LEN), F32)], 0)
        flag_ref[u * LEN : (u + 1) * LEN] = lines.T
        local = local + jnp.sum(masked, 1, keepdims=True)
    count_ref[...] = jnp.broadcast_to(local, (8, 128))
    for e in range(1, groups):
        group_copy(e).start()
    group_all[g] = count_ref[...]

    outs = [
        pltpu.make_async_copy(held[k], out_w[k], out_sems.at[k]) for k in range(6)
    ]

    def arrive(i):
        for d in range(1, chips):
            xy_here(i, d).wait_recv()
            if parts[i].share:
                z_copy(i, d, False).start()
            core_copy(i, d, 0, False).start()

    def relay(i):
        if parts[i].share:
            for d in range(1, chips):
                z_copy(i, d, True).wait_recv()
                core_copy(i, d, 1, False).start()

    def complete(i):
        core_copy(i, 0, 0, True).wait_recv()
        for d in range(1, chips):
            core_copy(i, d, 0, True).wait_recv()
            if parts[i].share:
                core_copy(i, d, 1, True).wait_recv()
        if all(done[k] == 3 for k in range(n) if parts[k].array == parts[i].array):
            outs[parts[i].array].start()

    done = [0] * n
    plan = iter(FORWARD_PLAN)

    def tick():
        for i in next(plan):
            done[i] += 1
            (arrive, relay, complete)[done[i] - 1](i)

    for e in range(1, groups):
        group_copy(e).wait_recv()
    total = group_all[0]
    for p in range(1, groups):
        total = total + group_all[p]
    total_ref[...] = total
    for e in range(1, shards):
        shard_copy(e).start()
    shard_all[s] = total

    for d in range(1, shards):
        vec_here(d).wait_recv()
    for b in range(shards):
        vec_ref[:, b * wide : (b + 1) * wide] = vec_all[b].astype(F32)
    vec_copy = pltpu.make_async_copy(vec_ref, vec_out, out_sems.at[6])
    vec_copy.start()

    copies = [vec_copy]

    def leave(k):
        copy = pltpu.make_async_copy(kept[k], out_v[k], out_sems.at[7 + k])
        copy.start()
        copies.append(copy)

    def each_tile(body):
        def once(i, carry):
            body(pl.ds(pl.multiple_of(i * 256, 256), 256))
            return carry

        lax.fori_loop(0, frames // 256, once, 0)

    def vec(row, width=D):
        return vec_ref[row : row + 1, :width]

    def normalise(rows):
        hat, _ = norm_parts(x_ref[rows].astype(F32))
        a_ref[rows] = (hat * vec(0, CH) + vec(1, CH)).astype(BF16)

    tick()
    each_tile(normalise)
    leave(0)
    leave(1)

    def hide(rows):
        hidden = product(a_ref[rows], held[0][...]) + vec(2)
        hidden = jnp.where(flag_ref[rows, 0:1] > 0.0, vec(3), hidden)
        h_ref[rows] = hidden
        hb_ref[rows] = hidden.astype(BF16)

    tick()
    each_tile(hide)
    leave(2)

    def triple(c):
        cols = slice(c * D, (c + 1) * D)

        def body(rows):
            value = product(hb_ref[rows], held[1][:, cols])
            if c != 1:
                value = value + vec((4, 4, 5)[c])
            t_ref[rows, cols] = value.astype(BF16)

        each_tile(body)

    for c in range(3):
        tick()
        triple(c)
    leave(3)
    triple_copy = copies.pop()

    halves = half_masks()
    scale = jnp.bfloat16(HEAD_DIM ** (-0.5))
    pairs = D // 128

    def attention(i, carry):
        u = i // pairs
        j = lax.rem(i, pairs)
        rows = pl.ds(pl.multiple_of(u * LEN, LEN), LEN)

        def lanes(block):
            return pl.ds(pl.multiple_of((j + block * pairs) * 128, 128), 128)

        shift = flag_ref[rows, 1:2]
        keys, values, query = (t_ref[rows, lanes(b)] for b in (1, 2, 0))
        parts_p = []
        for half in halves:
            scores = product_nt(keys, query * (half * scale)) + shift
            power = jnp.exp(scores - jnp.max(scores, 0, keepdims=True))
            parts_p.append((power * (1.0 / jnp.sum(power, 0, keepdims=True))).astype(BF16))
        out = product_tn(
            jnp.concatenate(parts_p, 0), jnp.concatenate([values * half for half in halves], 0)
        )
        att_ref[rows, lanes(0)] = out.astype(BF16)
        return carry

    rounds = (frames // LEN) * pairs
    cut = [rounds * i // 6 for i in range(7)]
    for i in range(6):
        tick()
        lax.fori_loop(cut[i], cut[i + 1], attention, 0)
    leave(4)
    triple_copy.wait()

    def branch(rows):
        resid = h_ref[rows] + product(att_ref[rows], held[2][...]) + vec(6)
        r1_ref[rows] = resid
        hat, _ = norm_parts(resid)
        first = hat * vec(7) + vec(8)
        h_ref[rows] = first
        z1_ref[rows] = first.astype(BF16)

    tick()
    each_tile(branch)
    leave(5)
    leave(6)

    def upper(c):
        cols = slice(c * D, (c + 1) * D)

        def body(rows):
            before = product(z1_ref[rows], held[3][:, cols]) + vec_ref[9:10, cols]
            active, slope = gelu_pair(before)
            act_ref[rows, cols] = active.astype(BF16)
            slope_ref[rows, cols] = slope

        each_tile(body)

    for c in range(FF // D):
        tick()
        upper(c)
    leave(7)
    leave(8)

    def lower_some(k):
        cols = slice(k * (D // 3), (k + 1) * (D // 3))

        def body(rows):
            h_ref[rows, cols] += product(act_ref[rows], held[4][:, cols])

        each_tile(body)

    for k in range(3):
        tick()
        lower_some(k)
    tick()

    for e in range(1, shards):
        shard_copy(e).wait_recv()
    for e in range(1, shards):
        shard_copy(e).wait_send()
    count = shard_all[0]
    for p in range(1, shards):
        count = count + shard_all[p]
    total_ref[...] = count
    per_frame = 1.0 / count[0:1, 0:1]
    codes = held[5][:, D:].astype(F32)
    cu_ref[...] = (
        codes * lax.rsqrt(jnp.sum(codes * codes, 0, keepdims=True) + 1e-06)
    ).astype(BF16)
    gv_ref[...] = jnp.zeros_like(gv_ref)
    loss_ref[...] = jnp.zeros_like(loss_ref)

    def lower(rows):
        masked = flag_ref[rows, 0:1]
        wh = held[5][:, :D]
        resid = h_ref[rows] + vec(10)
        hat, root = norm_parts(resid)
        second = (hat * vec(11) + vec(12)).astype(BF16)
        z2_ref[rows] = second
        head = product_nt(second, wh) + vec(13, CD)
        root_head = lax.rsqrt(jnp.sum(head * head, -1, keepdims=True) + 1e-06)
        unit = head * root_head
        unit_low = unit.astype(BF16)
        uc_ref[rows] = unit_low
        logits = temper * product(unit_low, cu_ref[...])
        code = lax.broadcasted_iota(jnp.int32, logits.shape, 1).astype(F32)
        logits = jnp.where(code < CODES, logits, -1e30)
        top = jnp.max(logits, -1, keepdims=True)
        power = jnp.exp(logits - top)
        total = jnp.sum(power, -1, keepdims=True)
        onehot = code == flag_ref[rows, 2:3]
        picked = jnp.sum(jnp.where(onehot, logits, 0.0), -1, keepdims=True)
        losses = top + jnp.log(total) - picked
        loss_ref[...] += jnp.sum(jnp.where(masked > 0.0, losses, 0.0), 0, keepdims=True)
        chances = power * (1.0 / total)
        d_logit = (
            temper
            * (jnp.where(masked > 0.0, chances - jnp.where(onehot, 1.0, 0.0), 0.0) * per_frame)
        ).astype(BF16)
        dlog_ref[rows] = d_logit
        d_unit = product_nt(d_logit, cu_ref[...])
        d_head = (
            root_head * (d_unit - unit * jnp.sum(d_unit * unit, -1, keepdims=True))
        ).astype(BF16)
        dc_ref[rows] = d_head
        gv_ref[13:14, :CD] += column_sum(d_head.astype(F32))
        d_second = product(d_head, wh)
        gv_ref[11:12, :D] += column_sum(d_second * hat)
        gv_ref[12:13, :D] += column_sum(d_second)
        d_resid = norm_back(d_second, hat, root, vec(11))
        dr2_ref[rows] = d_resid
        d_lower = d_resid.astype(BF16)
        df_ref[rows] = d_lower
        gv_ref[10:11, :D] += column_sum(d_lower.astype(F32))

    each_tile(lower)
    for k in range(9, len(kept)):
        leave(k)

    for i in range(n):
        core_copy(i, 0, 0, False).wait_send()
        for d in range(1, chips):
            xy_send(i, d).wait_send()
            core_copy(i, d, 0, False).wait_send()
            if parts[i].share:
                z_copy(i, d, False).wait_send()
                core_copy(i, d, 1, False).wait_send()
    for d in range(1, shards):
        vec_send(d).wait_send()
    for e in range(1, groups):
        group_copy(e).wait_send()
    for copy in outs + copies:
        copy.wait()


FORWARD_VALUES = (
    (8, F32),
    (CH, BF16),
    (D, BF16),
    (3 * D, BF16),
    (D, BF16),
    (D, F32),
    (D, BF16),
    (FF, BF16),
    (FF, F32),
    (D, BF16),
    (CD, BF16),
    (CPAD, BF16),
    (CD, BF16),
    (D, BF16),
    (D, F32),
)


def forward(groups, shards, lengths, starts, x, labels, weights):
    parts = weight_parts(shards)
    n = len(parts)
    chips = shards // 2
    frames = x.shape[0]
    hbm = pl.BlockSpec(memory_space=pl.ANY)
    vmem = pl.BlockSpec(memory_space=pltpu.VMEM)
    smem = pl.BlockSpec(memory_space=pltpu.SMEM)
    dma = pltpu.SemaphoreType.DMA
    arrays = [(CH, D), (D, 3 * D), (D, D), (D, FF), (FF, D), (CD, HEAD_COLS)]
    many = len(FORWARD_VALUES)
    results = pl.pallas_call(
        functools.partial(forward_kernel, parts, groups, shards),
        in_specs=[smem] * 2 + [vmem] * 7,
        out_specs=[hbm] * 7 + [vmem] * 3 + [hbm] * many,
        out_shape=[jax.ShapeDtypeStruct(shape, BF16) for shape in arrays]
        + [jax.ShapeDtypeStruct((16, FF), F32)]
        + [jax.ShapeDtypeStruct((8, 128), F32)] * 2
        + [jax.ShapeDtypeStruct((16, FF), F32)]
        + [jax.ShapeDtypeStruct((frames, width), kind) for width, kind in FORWARD_VALUES],
        scratch_shapes=[pltpu.VMEM(shape, BF16) for shape in arrays]
        + [
            pltpu.VMEM((frames, width), kind)
            for width, kind in FORWARD_VALUES
            if width != 3 * D
        ]
        + [
            pltpu.VMEM((shards, 16, FF // shards), BF16),
            pltpu.VMEM((16, FF), F32),
            pltpu.VMEM((CD, CPAD), BF16),
            pltpu.VMEM((8, 128), F32),
            pltpu.VMEM((groups, 8, 128), F32),
            pltpu.VMEM((shards, 8, 128), F32),
            dma((2, n, chips)),
            dma((2, n, chips)),
            dma((2, n, chips, 2)),
            dma((2, shards)),
            dma((2, groups)),
            dma((2, shards)),
            dma((7 + many,)),
        ],
        compiler_params=pltpu.CompilerParams(
            collective_id=2, has_side_effects=True, vmem_limit_bytes=64 * 1024 * 1024 - 65536
        ),
        name="forward",
    )(lengths, starts, x, labels, *weights)
    return results[:6], results[6], results[7], results[8], results[9], results[10:]


class Chunk:
    def __init__(self, rows, group, slot, sum_slot, wide_xy, wide_z, ring=True):
        self.ring = ring
        self.used = sum(rows)
        self.starts = [sum(rows[:i]) for i in range(len(rows))]
        self.rows = ceil_to(self.used, 16 * group)
        self.part = self.rows // group
        self.slot = slot
        self.sum_slot = sum_slot
        self.kind_xy = F32 if wide_xy else BF16
        self.kind_z = F32 if wide_z else BF16


HEAD_SLOT = 2


def gradient_chunks(groups, shards):
    down, band = FF // shards, D // shards
    half = down // 2
    return [
        Chunk([half], groups, 0, 0, False, True),
        Chunk([half], groups, 1, 1, False, True),
        Chunk([CD // shards] * 2, groups, HEAD_SLOT, 4, True, True),
        Chunk([band] * 2, groups, 0, 2, False, False),
        Chunk([band] * 2, groups, 1, 3, False, False),
        Chunk([band] * 2, groups, 0, 0, False, False),
        Chunk([band] * 2, groups, 1, 1, False, False),
        Chunk([CH // shards, 16], groups, 0, 5, False, True, False),
    ]


def tiles(rows, step, body):
    def once(i, carry):
        body(pl.ds(pl.multiple_of(i * step, step), step))
        return carry

    lax.fori_loop(0, rows // step, once, 0)


def backward_kernel(chunks, groups, shards, *refs):
    chips = shards // 2
    n = len(chunks)
    refs = list(refs)

    def take(count):
        out = refs[:count]
        del refs[:count]
        return out

    weights_hbm = take(6)
    vec_hbm, gvin_ref, loss_ref = take(3)
    (
        flag_hbm,
        a_hbm,
        hid_hbm,
        triple_hbm,
        att_hbm,
        r1_hbm,
        z1_hbm,
        act_hbm,
        slope_hbm,
        z2_hbm,
        uc_hbm,
        dlog_hbm,
        dc_hbm,
        df_hbm,
        dr2_hbm,
    ) = take(len(FORWARD_VALUES))
    (x_hbm,) = take(1)
    win_hbm, wqkv_hbm, wo_hbm, wu_hbm, wd_hbm, head_hbm = weights_hbm
    ring = take(n)
    (stat_out,) = take(1)
    pool, heads, dr1_ref, wide_ref, gv_ref, vec_ref, code_ref, flag_ref = take(8)
    full = take(3)
    pair = take(3)
    send_xy, recv_xy = take(3), take(n)
    acc = take(6)
    send_z, recv_z = take(n), take(n)
    stat_ref, group_all, stat_all = take(3)
    (
        load_sems,
        core_sems,
        credit,
        xy_sems,
        z_sems,
        right_sems,
        left_sems,
        loss_sems,
        stat_sems,
    ) = take(9)

    g = lax.axis_index("group")
    s = lax.axis_index("shard")
    core = lax.rem(s, 2)
    chip = s // 2
    sibling = s + 1 - 2 * core
    parts = FF // D
    frames = x_hbm.shape[0]

    def load(src, dst, sem):
        return pltpu.make_async_copy(src, dst, load_sems.at[sem])

    def cols(ref, c):
        return ref.at[:, c * D : (c + 1) * D]

    loads = {
        "df": load(df_hbm, pool.at[0], 0),
        "z1": load(z1_hbm, pool.at[3], 3),
        "z2": load(z2_hbm, heads.at[0], 8),
        "dc": load(dc_hbm, heads.at[1, :, 0:CD], 9),
        "uc": load(uc_hbm, heads.at[1, :, CD : 2 * CD], 10),
        "dlog": load(dlog_hbm, heads.at[2, :, 0:CPAD], 11),
        "hid": load(hid_hbm, pool.at[0], 0),
        "att": load(att_hbm, pool.at[4], 4),
        "x": load(x_hbm, pool.at[5, :, 0:CH], 5),
        "win": load(win_hbm, pool.at[6, 0:CH], 6),
        "dr2": load(dr2_hbm, dr1_ref, 7),
        "r1": load(r1_hbm, wide_ref, 14),
        "wo": load(wo_hbm, pool.at[2, 0:D], 2),
        "flags": load(flag_hbm, flag_ref, 15),
        "vec": load(vec_hbm, vec_ref, 16),
        "q": load(cols(triple_hbm, 0), heads.at[0], 8),
        "k": load(cols(triple_hbm, 1), heads.at[1], 9),
        "v": load(cols(triple_hbm, 2), heads.at[2], 11),
        "a": load(a_hbm, heads.at[3, :, 0:CH], 12),
        "codes": load(head_hbm.at[:, D:HEAD_COLS], code_ref, 13),
    }
    for c in range(parts):
        loads["act", c] = load(cols(act_hbm, c), pool.at[1 + c % 2], 1 + c % 2)
        loads["slope", c] = load(cols(slope_hbm, c), wide_ref, 14)
        loads["wd", c] = load(wd_hbm.at[c * D : (c + 1) * D], pool.at[2, 0:D], 2)
        loads["wu", c] = load(cols(wu_hbm, c), pool.at[5, 0:D], 5)
    for c in range(3):
        loads["w", c] = load(cols(wqkv_hbm, c), pool.at[1 + c, 0:D], 1 + c)

    def fetch(*names):
        for name in names:
            loads[name].start()

    def ready(*names):
        for name in names:
            loads[name].wait()

    fetch("df", ("act", 0), ("act", 1), "z2", "dc", "uc", "dlog", "codes", ("slope", 0), ("wu", 0))
    fetch("z1", "dr2", "flags", "vec")

    barrier = pltpu.get_barrier_semaphore()
    for e in range(1, shards):
        pl.semaphore_signal(
            barrier, 1, device_id=(g, lax.rem(s + e, shards)), device_id_type=MESH
        )
    for e in range(1, groups):
        pl.semaphore_signal(
            barrier, 1, device_id=(lax.rem(g + e, groups), s), device_id_type=MESH
        )
    pl.semaphore_wait(barrier, shards - 1 + groups - 1)

    def remote(src, dst, send_sem, recv_sem, device):
        return pltpu.make_async_remote_copy(
            src_ref=src,
            dst_ref=dst,
            send_sem=send_sem,
            recv_sem=recv_sem,
            device_id=device,
            device_id_type=MESH,
        )

    def chip_at(d):
        return lax.rem(chip + d, chips)

    order_out = list(range(1, chips)) + [0]

    def core_copy(t, d):
        c = chunks[t]
        q = chip_at(d)
        return remote(
            full[c.slot].at[q, 1 - core, 0 : c.used],
            pair[c.slot].at[q, 0 : c.used],
            core_sems.at[0, t, d],
            core_sems.at[1, t, d],
            (g, sibling),
        )

    before = {}
    for t, c in enumerate(chunks):
        earlier = [i for i in range(t) if chunks[i].slot == c.slot]
        before[t] = earlier[-1] if earlier else None
    last_of = {c.slot: t for t, c in enumerate(chunks)}

    def free_buffer(t):
        if before[t] is not None:
            for d in order_out:
                core_copy(before[t], d).wait_send()

    def stage_pair(t):
        if before[t] is not None:
            pl.semaphore_wait(credit.at[chunks[t].slot], 1)
        for d in order_out:
            core_copy(t, d).start()

    def xy_copy(t, d):
        return remote(
            send_xy[chunks[t].slot].at[d - 1, 0 : chunks[t].used],
            recv_xy[t].at[d - 1],
            xy_sems.at[0, t, d],
            xy_sems.at[1, t, d],
            (g, 2 * chip_at(d) + core),
        )

    def stage_chips(t):
        c = chunks[t]
        own, other = full[c.slot], pair[c.slot]
        for d in order_out:
            q = chip_at(d)
            core_copy(t, d).wait_recv()
            if d > 0 and before[t] is not None:
                xy_copy(before[t], d).wait_send()
            if d == 0:

                def keep(rows):
                    acc[c.sum_slot][rows] = own[q, core, rows] + other[q, rows]

                tiles(c.used, 16, keep)
                if c.rows > c.used:
                    acc[c.sum_slot][c.used : c.rows] = jnp.zeros((c.rows - c.used, D), F32)
            else:

                def send(rows):
                    send_xy[c.slot][d - 1, rows] = (own[q, core, rows] + other[q, rows]).astype(
                        c.kind_xy
                    )

                tiles(c.used, 16, send)
                xy_copy(t, d).start()
        if t != last_of[c.slot]:
            pl.semaphore_signal(
                credit.at[c.slot], 1, device_id=(g, sibling), device_id_type=MESH
            )

    def z_copy(t, e):
        return remote(
            send_z[t].at[e - 1],
            recv_z[t].at[e - 1],
            z_sems.at[0, t, e],
            z_sems.at[1, t, e],
            (lax.rem(g + e, groups), s),
        )

    def stage_group(t):
        c = chunks[t]
        total_ref = acc[c.sum_slot]
        for d in range(1, chips):
            xy_copy(t, d).wait_recv()

        def add(rows):
            total = total_ref[rows]
            for d in range(1, chips):
                total = total + recv_xy[t][d - 1, rows].astype(F32)
            total_ref[rows] = total

        tiles(c.used, 16, add)
        for e in range(1, groups):
            base = pl.multiple_of(lax.rem(g + e, groups) * c.part, 16)

            def send(rows):
                here = pl.ds(pl.multiple_of(base + rows.start, 16), 16)
                send_z[t][e - 1, rows] = total_ref[here].astype(BF16)

            tiles(c.part, 16, send)
            z_copy(t, e).start()

    def part_rows(t, p):
        return pl.ds(pl.multiple_of(p * chunks[t].part, 16), chunks[t].part)

    def ring_copy(t, k, way, back=0):
        p = g - k if way == 0 else g + k
        side = lax.rem(g + 1, groups) if way == 0 else lax.rem(g + groups - 1, groups)
        sems = right_sems if way == 0 else left_sems
        rows = part_rows(t, p)
        return remote(
            ring[t].at[rows],
            ring[t].at[rows],
            sems.at[0, t, k],
            sems.at[1, t, k - back],
            (side, s),
        )

    def near_copy(t, e, p):
        rows = part_rows(t, p)
        return remote(
            ring[t].at[rows],
            ring[t].at[rows],
            right_sems.at[0, t, e],
            right_sems.at[1, t, e],
            (lax.rem(g + e, groups), s),
        )

    def holds(k, way):
        return g >= k if way == 0 else g + k < groups

    def sends(k, way):
        return (g >= k) & (g < groups - 1) if way == 0 else (g + k < groups) & (g > 0)

    def stage_total(t):
        c = chunks[t]
        total_ref = acc[c.sum_slot]
        for e in range(1, groups):
            z_copy(t, e).wait_recv()
        base = pl.multiple_of(g * c.part, 16)

        def add(i, sums):
            rows = pl.ds(pl.multiple_of(i * 16, 16), 16)
            here = pl.ds(pl.multiple_of(base + i * 16, 16), 16)
            total = total_ref[here]
            for e in range(1, groups):
                total = total + recv_z[t][e - 1, rows].astype(F32)
            total = total.astype(c.kind_z)
            ring[t][here] = total
            total = total.astype(F32)
            total = total * total
            return sums + total[:8] + total[8:]

        squares[0] = lax.fori_loop(0, c.part // 16, add, squares[0])
        if not c.ring:
            for e in range(1, groups):
                near_copy(t, e, g).start()
            return
        for way in (0, 1):

            @pl.when(sends(0, way))
            def _():
                ring_copy(t, 0, way).start()

    def stage_ring(t, k):
        if not chunks[t].ring:
            if k == 1:
                for e in range(1, groups):
                    near_copy(t, e, lax.rem(g + groups - e, groups)).wait_recv()
            return
        for way in (0, 1):

            @pl.when(holds(k, way))
            def _():
                ring_copy(t, k, way, 1).wait_recv()

            if k < groups - 1:

                @pl.when(sends(k, way))
                def _():
                    ring_copy(t, k, way).start()

    done = [0] * n
    squares = [jnp.zeros((8, D), F32)]

    def step(t):
        now = done[t]
        done[t] += 1
        if now == 0:
            stage_pair(t)
        elif now == 1:
            same = [u for u in range(t) if chunks[u].sum_slot == chunks[t].sum_slot]
            assert all(done[u] > 3 for u in same)
            stage_chips(t)
        elif now == 2:
            stage_group(t)
        elif now == 3:
            stage_total(t)
        else:
            stage_ring(t, now - 3)

    plan = iter(BACKWARD_PLAN)

    def tick():
        for t in next(plan):
            step(t)

    def scatter(value, slots, at, per, first_shard, col=0):
        count = value.shape[0] // per
        each = per // len(slots)
        for k in range(count):
            shard = first_shard * 1 + k
            for i, slot in enumerate(slots):
                rows = value[k * per + i * each : k * per + (i + 1) * each]
                full[slot][
                    shard // 2, lax.rem(shard, 2), at : at + each, col : col + rows.shape[1]
                ] = rows

    def grad(left, right, slots, at, per, block, col=0):
        width = left.shape[1]

        def once(i, carry):
            some = left[:, pl.ds(pl.multiple_of(i * block, 128), block)]
            scatter(product_tn(some, right[...]), slots, at, per, i * (block // per), col)
            return carry

        lax.fori_loop(0, width // block, once, 0)

    down, band, deep, first = FF // shards, D // shards, CD // shards, CH // shards
    wide = FF // shards
    pairs = D // 128

    ready("df")
    for c in range(parts):
        ready(("act", c))
        for i in range(2):
            value = product_tn(
                pool[1 + c % 2, :, i * (D // 2) : (i + 1) * (D // 2)], pool[0]
            )
            scatter(value, [0, 1], 0, down, (c * D + i * (D // 2)) // down)
        if c + 2 < parts:
            fetch(("act", c + 2))
    fetch(("wd", 0))
    tick()
    ready("z2", "dc", "uc", "dlog", "codes")
    scatter(product_tn(heads[1, :, 0:CD], heads[0]), [HEAD_SLOT], 0, deep, 0)
    d_unit = product_tn(heads[1, :, CD : 2 * CD], heads[2, :, 0:CPAD])
    codes = code_ref[...].astype(F32)
    root = lax.rsqrt(jnp.sum(codes * codes, 0, keepdims=True) + 1e-06)
    unit = codes * root
    d_codes = root * (d_unit - unit * jnp.sum(d_unit * unit, 0, keepdims=True))
    scatter(d_codes, [HEAD_SLOT], deep, deep, 0)
    full[HEAD_SLOT][:, :, deep : 2 * deep, CPAD:D] = jnp.zeros((chips, 2, deep, D - CPAD), F32)
    fetch("q", "k", "v", "att", "win")
    tick()
    ready("z1", "dr2", "flags", "vec")
    gv_ref[...] = gvin_ref[...]

    def each_tile(body, begin=0, end=None):
        def once(i, carry):
            body(pl.ds(pl.multiple_of(i * 256, 256), 256))
            return carry

        lax.fori_loop(begin, frames // 256 if end is None else end, once, 0)

    for t, first_part in ((3, 0), (4, 2)):
        for i in range(2):
            c = first_part + i
            span = slice(c * D, (c + 1) * D)
            ready(("slope", c), ("wd", c), ("wu", c))

            def lower(rows):
                d_before = wide_ref[rows] * product_nt(pool[0, rows], pool[2, 0:D])
                d_before = d_before.astype(BF16)
                pool[1, rows] = d_before
                gv_ref[9:10, span] += column_sum(d_before.astype(F32))
                dr1_ref[rows] += product_nt(d_before, pool[5, 0:D])

            each_tile(lower)
            tick()
            if i == 0:
                free_buffer(t)
            if c + 1 < parts:
                fetch(("slope", c + 1), ("wd", c + 1), ("wu", c + 1))
            else:
                fetch("r1", "wo", "hid")
            grad(pool.at[3], pool.at[1], [chunks[t].slot], i * band, band, D // 2)
            tick()
    ready("r1", "wo")

    def branch(rows):
        hat, root = norm_parts(wide_ref[rows])
        d_first = dr1_ref[rows]
        gv_ref[7:8, :D] += column_sum(d_first * hat)
        gv_ref[8:9, :D] += column_sum(d_first)
        d_resid = norm_back(d_first, hat, root, vec_ref[7:8, :D])
        dr1_ref[rows] = d_resid
        d_branch = d_resid.astype(BF16)
        pool[5, rows] = d_branch
        gv_ref[6:7, :D] += column_sum(d_branch.astype(F32))
        heads[3, rows] = product_nt(d_branch, pool[2, 0:D]).astype(BF16)

    each_tile(branch)
    for c in range(3):
        fetch(("w", c))
    tick()

    halves = half_masks()
    utters = frames // LEN

    def attention(i, carry):
        rows = pl.ds(pl.multiple_of(lax.rem(i, utters) * LEN, LEN), LEN)
        lanes = pl.ds(pl.multiple_of((i // utters) * 128, 128), 128)
        shift = flag_ref[rows, 1:2]
        keys, values = heads[1, rows, lanes], heads[2, rows, lanes]
        dq = dk = dv = None
        for half in halves:
            query = heads[0, rows, lanes] * half
            upstream = heads[3, rows, lanes] * half
            scores = product_nt(keys, query) * HEAD_DIM ** (-0.5) + shift
            power = jnp.exp(scores - jnp.max(scores, 0, keepdims=True))
            probs = power * (1.0 / jnp.sum(power, 0, keepdims=True))
            part_v = product(probs.astype(BF16), upstream)
            d_probs = product_nt(values, upstream)
            weight = jnp.sum(probs * d_probs, 0, keepdims=True)
            d_scores = (probs * (d_probs - weight) * HEAD_DIM ** (-0.5)).astype(BF16)
            part_k = product(d_scores, query)
            part_q = product_tn(d_scores, keys * half)
            dq = part_q if dq is None else dq + part_q
            dk = part_k if dk is None else dk + part_k
            dv = part_v if dv is None else dv + part_v
        heads[0, rows, lanes] = dq.astype(BF16)
        heads[1, rows, lanes] = dk.astype(BF16)
        heads[2, rows, lanes] = dv.astype(BF16)
        return carry

    ready("q", "k", "v")
    rounds = utters * pairs
    middle = D // 2

    def attend(begin, end):
        cut = [begin + (end - begin) * i // 3 for i in range(4)]
        for i in range(3):
            lax.fori_loop(cut[i], cut[i + 1], attention, 0)
            tick()

    attend(0, rounds // 2)
    ready("hid", "att")
    free_buffer(5)
    grad(pool.at[0], heads.at[0, :, 0:middle], [0], 0, band, middle)
    grad(pool.at[0], heads.at[1, :, 0:middle], [0], 0, band, middle, middle)
    grad(pool.at[4], pool.at[5], [0], band, band, middle)
    tick()
    fetch("x")
    attend(rounds // 2, rounds)
    fetch("a")
    free_buffer(6)
    grad(pool.at[0], heads.at[2], [1], 0, band, middle)
    grad(pool.at[0], heads.at[0, :, middle:D], [1], band, band, middle)
    grad(pool.at[0], heads.at[1, :, middle:D], [1], band, band, middle, middle)
    tick()
    ready(("w", 0), ("w", 1), ("w", 2), "win", "x")

    def back(rows):
        dq, dk, dv = heads[0, rows], heads[1, rows], heads[2, rows]
        gv_ref[4:5, :D] += column_sum(dq.astype(F32))
        gv_ref[5:6, :D] += column_sum(dv.astype(F32))
        d_hidden = (
            dr1_ref[rows]
            + product_nt(dq, pool[1, 0:D])
            + product_nt(dk, pool[2, 0:D])
            + product_nt(dv, pool[3, 0:D])
        )
        masked = flag_ref[rows, 0:1] > 0.0
        gv_ref[3:4, :D] += column_sum(jnp.where(masked, d_hidden, 0.0))
        d_proj = jnp.where(masked, 0.0, d_hidden).astype(BF16)
        pool[4, rows] = d_proj
        gv_ref[2:3, :D] += column_sum(d_proj.astype(F32))
        d_normed = product_nt(d_proj, pool[6, 0:CH])
        hat, _ = norm_parts(pool[5, rows, 0:CH].astype(F32))
        gv_ref[0:1, :CH] += column_sum(d_normed * hat)
        gv_ref[1:2, :CH] += column_sum(d_normed)

    each_tile(back, 0, 2)
    tick()
    each_tile(back, 2)
    tick()
    ready("a")
    free_buffer(7)
    grad(heads.at[3, :, 0:CH], pool.at[4], [0], 0, first, CH // 2)
    for b in range(shards):
        full[0][b // 2, b % 2, first : first + 16, 0:wide] = gv_ref[:, b * wide : (b + 1) * wide]
        full[0][b // 2, b % 2, first : first + 16, wide:D] = jnp.zeros((16, D - wide), F32)
    final = 3 + groups
    rest = list(next(plan))

    def advance(enough):
        while rest and not enough():
            step(rest.pop(0))

    def group_copy(e):
        return remote(
            stat_ref.at[0],
            group_all.at[g],
            loss_sems.at[0, e],
            loss_sems.at[1, e],
            (lax.rem(g + e, groups), s),
        )

    def stat_copy(e):
        return remote(
            stat_ref.at[1],
            stat_all.at[s],
            stat_sems.at[0, e],
            stat_sems.at[1, e],
            (g, lax.rem(s + e, shards)),
        )

    advance(lambda: min(done) > 3)
    lane = lax.broadcasted_iota(jnp.int32, (8, 128), 1)
    stat_ref[0] = jnp.where(lane == 0, jnp.sum(squares[0]), loss_ref[...])
    for e in range(1, groups):
        group_copy(e).start()
    group_all[g] = stat_ref[0]
    left_over = len(rest) - 3
    advance(lambda: len(rest) <= left_over)
    for e in range(1, groups):
        group_copy(e).wait_recv()
    total = group_all[0]
    for p in range(1, groups):
        total = total + group_all[p]
    stat_ref[1] = total
    for e in range(1, shards):
        stat_copy(e).start()
    stat_all[s] = total
    advance(lambda: False)
    while min(done) < final:
        step(done.index(min(done)))
    for e in range(1, shards):
        stat_copy(e).wait_recv()
    total = stat_all[0]
    for p in range(1, shards):
        total = total + stat_all[p]
    stat_out[...] = total
    for t in range(n):
        if t == last_of[chunks[t].slot]:
            for d in order_out:
                core_copy(t, d).wait_send()
            for d in range(1, chips):
                xy_copy(t, d).wait_send()
        for e in range(1, groups):
            z_copy(t, e).wait_send()
            if not chunks[t].ring:
                near_copy(t, e, g).wait_send()
        for k in range(groups - 1 if chunks[t].ring else 0):
            for way in (0, 1):

                @pl.when(sends(k, way))
                def _():
                    ring_copy(t, k, way).wait_send()

    for e in range(1, groups):
        group_copy(e).wait_send()
    for e in range(1, shards):
        stat_copy(e).wait_send()


def backward(groups, shards, weights, vecs, gv, loss, values, x):
    chunks = gradient_chunks(groups, shards)
    chips = shards // 2
    n = len(chunks)
    frames = x.shape[0]
    hbm = pl.BlockSpec(memory_space=pl.ANY)
    vmem = pl.BlockSpec(memory_space=pltpu.VMEM)
    dma = pltpu.SemaphoreType.DMA
    deepest = [max(c.used for c in chunks if c.slot == i) for i in range(3)]
    sums = [max(c.rows for c in chunks if c.sum_slot == i) for i in range(6)]
    results = pl.pallas_call(
        functools.partial(backward_kernel, chunks, groups, shards),
        in_specs=[hbm] * 7 + [vmem] * 2 + [hbm] * (len(values) + 1),
        out_specs=[vmem] * (n + 1),
        out_shape=[jax.ShapeDtypeStruct((c.rows, D), c.kind_z) for c in chunks]
        + [jax.ShapeDtypeStruct((8, 128), F32)],
        scratch_shapes=[
            pltpu.VMEM((7, frames, D), BF16),
            pltpu.VMEM((4, frames, D), BF16),
            pltpu.VMEM((frames, D), F32),
            pltpu.VMEM((frames, D), F32),
            pltpu.VMEM((16, FF), F32),
            pltpu.VMEM((16, FF), F32),
            pltpu.VMEM((CD, CPAD), BF16),
            pltpu.VMEM((frames, 8), F32),
        ]
        + [pltpu.VMEM((chips, 2, rows, D), F32) for rows in deepest]
        + [pltpu.VMEM((chips, rows, D), F32) for rows in deepest]
        + [
            pltpu.VMEM((chips - 1, rows, D), F32 if i == HEAD_SLOT else BF16)
            for i, rows in enumerate(deepest)
        ]
        + [pltpu.VMEM((chips - 1, c.used, D), c.kind_xy) for c in chunks]
        + [pltpu.VMEM((rows, D), F32) for rows in sums]
        + [pltpu.VMEM((groups - 1, c.part, D), BF16) for c in chunks] * 2
        + [
            pltpu.VMEM((2, 8, 128), F32),
            pltpu.VMEM((groups, 8, 128), F32),
            pltpu.VMEM((shards, 8, 128), F32),
        ]
        + [
            dma((17,)),
            dma((2, n, chips)),
            pltpu.SemaphoreType.REGULAR((3,)),
            dma((2, n, chips)),
            dma((2, n, groups)),
            dma((2, n, groups)),
            dma((2, n, groups)),
            dma((2, groups)),
            dma((2, shards)),
        ],
        compiler_params=pltpu.CompilerParams(
            collective_id=1, has_side_effects=True, vmem_limit_bytes=64 * 1024 * 1024 - 65536
        ),
        name="backward",
    )(*weights, vecs, gv, loss, *values, x)
    return results[:n], results[n]


def adam_kernel(step_ref, stat_ref, count_ref, *refs):
    w, m, v = refs[0:5], refs[5:10], refs[10:15]
    g_head, g_tail = refs[15:17]
    early_ref, late_ref = refs[17:19]
    halves = refs[19:23]
    outs = [refs[23 + 5 * i : 28 + 5 * i] for i in range(4)]
    norm_ref, loss_ref = refs[43:45]
    step = pl.program_id(0)
    fix_one, fix_two = (
        1.0 - lax.fori_loop(0, step_ref[0], lambda _, value: value * beta, jnp.float32(1.0))
        for beta in (beta_one, beta_two)
    )
    norm = jnp.sqrt(stat_ref[0:1, 0:1])
    factor = jnp.minimum(1.0, clip_norm / (norm + 1e-06))

    def update(i, grad, where=...):
        shrink = 0.0 if i == 4 else decay
        weight, moment, square = w[i][where], m[i][where], v[i][where]
        grad = grad.astype(F32) * factor
        moment = beta_one * moment + (1.0 - beta_one) * grad
        square = beta_two * square + (1.0 - beta_two) * grad * grad
        stepped = moment / fix_one / (jnp.sqrt(square / fix_two) + adam_eps)
        weight = weight - rate * (stepped + shrink * weight)
        for out, value in zip(outs, (weight, moment, square, weight.astype(BF16))):
            out[i][where] = value

    def both(early):
        @pl.when(early == (step < 2))
        def _():
            up, down = halves[0 if early else 1 :: 2]
            update(1, up[...], 1)
            update(2, down[...])

    depth = w[1].shape[1]
    upper, lower = slice(0, depth), slice(depth, 2 * depth)
    left, right = slice(0, D // 2), slice(D // 2, D)

    @pl.when(step == 0)
    def _():
        update(1, early_ref[upper, left], (0, slice(None), left))
        update(1, late_ref[lower, left], (0, slice(None), right))

    @pl.when(step == 1)
    def _():
        update(1, early_ref[upper, right], (0, slice(None), left))
        update(1, late_ref[lower, right], (0, slice(None), right))

    @pl.when(step == 2)
    def _():
        update(1, late_ref[upper], 0)

    @pl.when(step == 3)
    def _():
        update(1, early_ref[lower], 0)

    both(True)
    both(False)

    @pl.when(step == 0)
    def _():
        first, deep = w[0].shape[0], w[3].shape[0]
        norm_ref[...] = norm
        loss_ref[...] = stat_ref[0:1, 1:2] / count_ref[0:1, 0:1]
        update(0, g_tail[:first])
        update(3, g_head[:deep], (slice(None), slice(0, D)))
        update(3, g_head[deep : 2 * deep, :CODES], (slice(None), slice(D, D + CODES)))
        update(4, g_tail[first : first + NVEC, : w[4].shape[1]])


def adam(steps, stat, count, weights, moments, seconds, sums):
    parts = FF // D
    depth = weights[1].shape[1]
    tall = weights[2].shape[0] // parts

    def fixed(a):
        return pl.BlockSpec(a.shape, lambda i: (0,) * a.ndim)

    w_specs = [
        fixed(weights[0]),
        pl.BlockSpec((2, depth, D), lambda i: (0, 0, i)),
        pl.BlockSpec((tall, D), lambda i: (i, 0)),
        fixed(weights[3]),
        fixed(weights[4]),
    ]
    g_specs = [fixed(sums[i]) for i in (2, 7, 5, 6)]
    for rows in (depth, tall):
        g_specs.append(pl.BlockSpec((rows, D), lambda i: (jnp.minimum(i, 1), 0)))
        g_specs.append(pl.BlockSpec((rows, D), lambda i: (jnp.maximum(i - 2, 0), 0)))
    shapes = [jax.ShapeDtypeStruct(w.shape, F32) for w in weights]
    low = [jax.ShapeDtypeStruct(w.shape, BF16) for w in weights]
    outs = pl.pallas_call(
        adam_kernel,
        grid=(parts,),
        in_specs=[pl.BlockSpec(memory_space=pltpu.SMEM), fixed(stat), fixed(count)]
        + w_specs * 3
        + g_specs,
        out_specs=w_specs * 4 + [pl.BlockSpec((1, 1), lambda i: (0, 0))] * 2,
        out_shape=shapes * 3 + low + [jax.ShapeDtypeStruct((1, 1), F32)] * 2,
        compiler_params=params(),
        name="adam",
    )(
        steps,
        stat,
        count,
        *weights,
        *moments,
        *seconds,
        *[sums[i] for i in (2, 7, 5, 6, 3, 4, 0, 1)],
    )
    return [outs[i * 5 : (i + 1) * 5] for i in range(4)] + list(outs[20:])


def per_device(
    features,
    lengths,
    starts,
    labels,
    step_count,
    weight_in,
    weight_rows,
    weight_down,
    weight_head,
    vectors,
    moment_in,
    moment_rows,
    moment_down,
    moment_head,
    moment_vectors,
    second_in,
    second_rows,
    second_down,
    second_head,
    second_vectors,
):
    masters = (weight_in, weight_rows, weight_down, weight_head, vectors)
    moments = (moment_in, moment_rows, moment_down, moment_head, moment_vectors)
    seconds = (second_in, second_rows, second_down, second_head, second_vectors)
    groups, shards = lax.axis_size("group"), lax.axis_size("shard")
    x = features.reshape(-1, CH)

    def turned(arrays):
        return [a.T if i == 3 else a for i, a in enumerate(arrays)]

    weights, vecs, count, loss, gv, values = forward(
        groups, shards, lengths, starts, x, labels, turned(masters)
    )
    sums, stat = backward(groups, shards, weights, vecs, gv, loss, values, x)
    *updated, norm, loss = adam(
        step_count, stat, count, turned(masters), turned(moments), turned(seconds), sums
    )
    new_w, new_m, new_v, copies = (turned(out) for out in updated)
    return (
        *new_w,
        *new_m,
        *new_v,
        *copies,
        jnp.reshape(loss, (1,)),
        jnp.reshape(norm, (1,)),
    )


def solution(mesh):
    weights = (
        P("shard", None),
        P(None, "shard", None),
        P("shard", None),
        P(None, "shard"),
        P(None, "shard"),
    )
    both = ("group", "shard")
    in_specs = (P(both, None, None), P(both), P(both, None), P(both, None), P()) + weights * 3
    out_specs = weights * 4 + (P(), P())
    return jax.shard_map(
        per_device, mesh=mesh, in_specs=in_specs, out_specs=out_specs, check_vma=False
    )
```

```python
import functools

import jax
import jax.numpy as jnp
from jax import lax
from jax.experimental import pallas as pl
from jax.experimental.pallas import tpu as pltpu
from jax.sharding import PartitionSpec as P

D = 768
CH = 512
HEADS = 12
HEAD_DIM = 64
FF = 3072
CD = 256
CODES = 500
CPAD = 512
LEN = 512
SPAN = 10
NVEC = 14

beta_one = 0.9
beta_two = 0.999
rate = 0.03
decay = 0.01
adam_eps = 1e-08
clip_norm = 0.01
temper = 10.0

F32 = jnp.float32
BF16 = jnp.bfloat16
VMEM_BYTES = 60 * 1024 * 1024


def product(left, right):
    return jnp.dot(left, right, preferred_element_type=F32)


def product_nt(left, right):
    return lax.dot_general(left, right, (((1,), (1,)), ((), ())), preferred_element_type=F32)


def product_tn(left, right):
    return lax.dot_general(left, right, (((0,), (0,)), ((), ())), preferred_element_type=F32)


def norm_parts(values):
    centred = values - jnp.mean(values, -1, keepdims=True)
    root = lax.rsqrt(jnp.mean(centred * centred, -1, keepdims=True) + 1e-05)
    return centred * root, root


def norm_back(upstream, hat, root, gain):
    scaled = upstream * gain
    return root * (
        scaled
        - jnp.mean(scaled, -1, keepdims=True)
        - hat * jnp.mean(scaled * hat, -1, keepdims=True)
    )


def column_sum(values):
    return jnp.sum(values, 0, keepdims=True)


def gelu_pair(e):
    root = 0.7071067811865476
    reach = jnp.abs(e) * root
    tail = jnp.exp(-0.5 * e * e)
    t = 1.0 / (1.0 + 0.3275911 * reach)
    poly = t * (
        0.254829592
        + t * (-0.284496736 + t * (1.421413741 + t * (-1.453152027 + t * 1.061405429)))
    )
    half = 0.5 * poly * tail
    phi = jnp.where(e < 0.0, half, 1.0 - half)
    return e * phi, phi + e * tail * 0.3989422804014327


def params(limit=VMEM_BYTES):
    return pltpu.CompilerParams(vmem_limit_bytes=limit)


def half_masks():
    lane = lax.broadcasted_iota(jnp.int32, (1, 128), 1)
    return [(lane < HEAD_DIM).astype(BF16), (lane >= HEAD_DIM).astype(BF16)]


MESH = pl.DeviceIdType.MESH


def ceil_to(value, step):
    return -(-value // step) * step


class Part:
    def __init__(self, array, every, low, rows, col, cols):
        self.array, self.every, self.low, self.rows = array, every, low, rows
        self.col, self.cols = col, cols
        share = (rows * 2 // 5) // 16 * 16
        self.share = max(share, 16) if rows >= 32 else 0


HEAD_COLS = D + CPAD


def weight_parts(shards):
    band, down = D // shards, FF // shards
    third = D // 3
    return [
        Part(0, CH // shards, 0, CH // shards, 0, D),
        Part(1, band, 0, band, 0, D),
        Part(1, band, 0, band, D, D),
        Part(1, band, 0, band, 2 * D, D),
        Part(2, band, 0, band, 0, D),
        Part(5, CD // shards, 0, CD // shards, 0, HEAD_COLS),
        Part(3, band, 0, band, 0, 2 * D),
        Part(3, band, 0, band, 2 * D, 2 * D),
        Part(4, down, 0, down, 0, third),
        Part(4, down, 0, down, third, third),
        Part(4, down, 0, down, 2 * third, third),
    ]


FORWARD_PLAN = (
    (),
    (0, 1, 0, 0,),
    (2, 1, 3, 1,),
    (4, 2, 5, 3, 2,),
    (3,),
    (4,),
    (6, 5,),
    (4,),
    (5,),
    (7, 6,),
    (8,),
    (6, 9,),
    (7,),
    (10, 8,),
    (7,),
    (9, 8,),
    (10,),
    (9,),
    (10,),
    (),
)
BACKWARD_PLAN = (
    (0, 1,),
    (2,),
    (0,),
    (1,),
    (2,),
    (3,),
    (),
    (3, 0,),
    (),
    (4,),
    (),
    (4, 1, 0,),
    (2,),
    (1,),
    (5, 0,),
    (5, 3, 0, 1, 2,),
    (),
    (4, 3, 0,),
    (6, 1, 2,),
    (6, 5,),
    (1, 3, 4, 2,),
    (7, 7, 5, 3, 6, 4, 2, 5, 3, 7, 6, 4, 5, 7, 6, 4, 5, 7, 7, 7, 6, 6,),
)


def forward_kernel(parts, groups, shards, *refs):
    chips = shards // 2
    n = len(parts)
    refs = list(refs)

    def take(count):
        out = refs[:count]
        del refs[:count]
        return out

    len_ref, start_ref, x_ref, label_ref, win_ref, rows_ref, down_ref, head_ref, vecs_ref = take(9)
    out_w = take(6)
    vec_out, total_ref, loss_ref, gv_ref = take(4)
    out_v = take(len(FORWARD_VALUES))
    held = take(6)
    kept = take(len(FORWARD_VALUES) - 1)
    (
        flag_ref,
        a_ref,
        hb_ref,
        att_ref,
        r1_ref,
        z1_ref,
        act_ref,
        slope_ref,
        z2_ref,
        uc_ref,
        dlog_ref,
        dc_ref,
        df_ref,
        dr2_ref,
    ) = kept
    vec_all, vec_ref, cu_ref, count_ref, group_all, shard_all = take(6)
    h_ref = dr2_ref
    t_ref = act_ref
    kept.insert(3, act_ref.at[:, 0 : 3 * D])
    (xy_sems, z_sems, core_sems, vec_sems, group_sems, shard_sems, out_sems) = take(7)

    g = lax.axis_index("group")
    s = lax.axis_index("shard")
    core = lax.rem(s, 2)
    chip = s // 2
    sibling = s + 1 - 2 * core
    parity = lax.rem(g, 2)
    partner = g + 1 - 2 * parity
    frames = x_ref.shape[0]
    band, first = D // shards, CH // shards
    wide = FF // shards

    barrier = pltpu.get_barrier_semaphore()
    for e in range(1, shards):
        pl.semaphore_signal(
            barrier, 1, device_id=(g, lax.rem(s + e, shards)), device_id_type=MESH
        )
    for e in range(1, groups):
        pl.semaphore_signal(
            barrier, 1, device_id=(lax.rem(g + e, groups), s), device_id_type=MESH
        )

    def remote(ref, send_sem, recv_sem, device, dst=None):
        return pltpu.make_async_remote_copy(
            src_ref=ref,
            dst_ref=ref if dst is None else dst,
            send_sem=send_sem,
            recv_sem=recv_sem,
            device_id=device,
            device_id_type=MESH,
        )

    def region(i, shard, at, size):
        p = parts[i]
        rows = pl.ds(pl.multiple_of(shard * p.every + p.low + at, 16), size)
        return held[p.array].at[rows, p.col : p.col + p.cols]

    def chip_to(d):
        return lax.rem(chip + d, chips)

    def chip_from(d):
        return lax.rem(chip + chips - d, chips)

    def direct(i):
        return parity * parts[i].share, parts[i].rows - parts[i].share

    def xy_send(i, d):
        return remote(
            region(i, s, *direct(i)),
            xy_sems.at[0, i, d],
            xy_sems.at[1, i, d],
            (g, 2 * chip_to(d) + core),
        )

    def xy_here(i, d):
        return remote(
            region(i, 2 * chip_from(d) + core, *direct(i)),
            xy_sems.at[0, i, d],
            xy_sems.at[1, i, d],
            (g, 2 * chip_to(d) + core),
        )

    def z_copy(i, d, arriving):
        rest = parts[i].rows - parts[i].share
        start = (1 - parity if arriving else parity) * rest
        return remote(
            region(i, 2 * chip_from(d) + core, start, parts[i].share),
            z_sems.at[0, i, d],
            z_sems.at[1, i, d],
            (partner, s),
        )

    def core_copy(i, d, which, arriving):
        side = 1 - core if arriving else core
        shard = 2 * chip_from(d) + side
        if d == 0:
            span = (0, parts[i].rows)
        elif which == 0:
            span = direct(i)
        else:
            span = ((1 - parity) * (parts[i].rows - parts[i].share), parts[i].share)
        return remote(
            region(i, shard, *span),
            core_sems.at[0, i, d, which],
            core_sems.at[1, i, d, which],
            (g, sibling),
        )

    def vec_send(d):
        return remote(
            vec_all.at[s], vec_sems.at[0, d], vec_sems.at[1, d], (g, lax.rem(s + d, shards))
        )

    def vec_here(d):
        return remote(
            vec_all.at[lax.rem(s + shards - d, shards)],
            vec_sems.at[0, d],
            vec_sems.at[1, d],
            (g, lax.rem(s + d, shards)),
        )

    def group_copy(e):
        return remote(
            count_ref,
            group_sems.at[0, e],
            group_sems.at[1, e],
            (lax.rem(g + e, groups), s),
            group_all.at[g],
        )

    def shard_copy(e):
        return remote(
            total_ref,
            shard_sems.at[0, e],
            shard_sems.at[1, e],
            (g, lax.rem(s + e, shards)),
            shard_all.at[s],
        )

    def settle(ref, source, every):
        ref[pl.ds(pl.multiple_of(s * every, 16), every)] = source.astype(BF16)

    def launch(*some):
        for i in some:
            for d in range(1, chips):
                xy_send(i, d).start()
            core_copy(i, 0, 0, False).start()

    vec_all[s] = jnp.zeros(vec_all.shape[1:], BF16)
    vec_all[s, 0:NVEC] = vecs_ref[...].astype(BF16)
    settle(held[0], win_ref[...], first)
    settle(held[1], rows_ref[0, :, : 3 * D], band)
    pl.semaphore_wait(barrier, shards - 1 + groups - 1)
    for d in range(1, shards):
        vec_send(d).start()
    launch(0, 1, 2, 3)
    settle(held[2], rows_ref[0, :, 3 * D :], band)
    every = CD // shards
    here = pl.ds(pl.multiple_of(s * every, 16), every)
    held[5][here, D + CPAD - 128 :] = jnp.zeros((every, 128), BF16)
    held[5][here, : D + CODES] = head_ref[...].astype(BF16)
    settle(held[3], rows_ref[1], band)
    settle(held[4], down_ref[...], wide)
    launch(*range(4, n))

    position = lax.broadcasted_iota(jnp.int32, (1, LEN), 1)
    local = jnp.zeros((1, 1), F32)
    for u in range(frames // LEN):
        length = len_ref[u]

        def span(j, inside):
            begin = lax.rem(start_ref[u, j], length - SPAN + 1)
            hit = (position >= begin) & (position < begin + SPAN)
            return jnp.where(hit, 1.0, inside)

        inside = lax.fori_loop(0, start_ref.shape[1], span, jnp.zeros((1, LEN), F32))
        masked = jnp.where(position < length, inside, 0.0)
        shift = jnp.where(position < length, 0.0, -1e30)
        label = label_ref[u : u + 1].astype(F32)
        lines = jnp.concatenate([masked, shift, label, jnp.zeros((5, LEN), F32)], 0)
        flag_ref[u * LEN : (u + 1) * LEN] = lines.T
        local = local + jnp.sum(masked, 1, keepdims=True)
    count_ref[...] = jnp.broadcast_to(local, (8, 128))
    for e in range(1, groups):
        group_copy(e).start()
    group_all[g] = count_ref[...]

    outs = [
        pltpu.make_async_copy(held[k], out_w[k], out_sems.at[k]) for k in range(6)
    ]

    def arrive(i):
        for d in range(1, chips):
            xy_here(i, d).wait_recv()
            if parts[i].share:
                z_copy(i, d, False).start()
            core_copy(i, d, 0, False).start()

    def relay(i):
        if parts[i].share:
            for d in range(1, chips):
                z_copy(i, d, True).wait_recv()
                core_copy(i, d, 1, False).start()

    def complete(i):
        core_copy(i, 0, 0, True).wait_recv()
        for d in range(1, chips):
            core_copy(i, d, 0, True).wait_recv()
            if parts[i].share:
                core_copy(i, d, 1, True).wait_recv()
        if all(done[k] == 3 for k in range(n) if parts[k].array == parts[i].array):
            outs[parts[i].array].start()

    done = [0] * n
    plan = iter(FORWARD_PLAN)

    def tick():
        for i in next(plan):
            done[i] += 1
            (arrive, relay, complete)[done[i] - 1](i)

    for e in range(1, groups):
        group_copy(e).wait_recv()
    total = group_all[0]
    for p in range(1, groups):
        total = total + group_all[p]
    total_ref[...] = total
    for e in range(1, shards):
        shard_copy(e).start()
    shard_all[s] = total

    for d in range(1, shards):
        vec_here(d).wait_recv()
    for b in range(shards):
        vec_ref[:, b * wide : (b + 1) * wide] = vec_all[b].astype(F32)
    vec_copy = pltpu.make_async_copy(vec_ref, vec_out, out_sems.at[6])
    vec_copy.start()

    copies = [vec_copy]

    def leave(k):
        copy = pltpu.make_async_copy(kept[k], out_v[k], out_sems.at[7 + k])
        copy.start()
        copies.append(copy)

    def each_tile(body):
        def once(i, carry):
            body(pl.ds(pl.multiple_of(i * 256, 256), 256))
            return carry

        lax.fori_loop(0, frames // 256, once, 0)

    def vec(row, width=D):
        return vec_ref[row : row + 1, :width]

    def normalise(rows):
        hat, _ = norm_parts(x_ref[rows].astype(F32))
        a_ref[rows] = (hat * vec(0, CH) + vec(1, CH)).astype(BF16)

    tick()
    each_tile(normalise)
    leave(0)
    leave(1)

    def hide(rows):
        hidden = product(a_ref[rows], held[0][...]) + vec(2)
        hidden = jnp.where(flag_ref[rows, 0:1] > 0.0, vec(3), hidden)
        h_ref[rows] = hidden
        hb_ref[rows] = hidden.astype(BF16)

    tick()
    each_tile(hide)
    leave(2)

    def triple(c):
        cols = slice(c * D, (c + 1) * D)

        def body(rows):
            value = product(hb_ref[rows], held[1][:, cols])
            if c != 1:
                value = value + vec((4, 4, 5)[c])
            t_ref[rows, cols] = value.astype(BF16)

        each_tile(body)

    for c in range(3):
        tick()
        triple(c)
    leave(3)
    triple_copy = copies.pop()

    halves = half_masks()
    scale = jnp.bfloat16(HEAD_DIM ** (-0.5))
    pairs = D // 128

    def attention(i, carry):
        u = i // pairs
        j = lax.rem(i, pairs)
        rows = pl.ds(pl.multiple_of(u * LEN, LEN), LEN)

        def lanes(block):
            return pl.ds(pl.multiple_of((j + block * pairs) * 128, 128), 128)

        shift = flag_ref[rows, 1:2]
        keys, values, query = (t_ref[rows, lanes(b)] for b in (1, 2, 0))
        parts_p = []
        for half in halves:
            scores = product_nt(keys, query * (half * scale)) + shift
            power = jnp.exp(scores - jnp.max(scores, 0, keepdims=True))
            parts_p.append((power * (1.0 / jnp.sum(power, 0, keepdims=True))).astype(BF16))
        out = product_tn(
            jnp.concatenate(parts_p, 0), jnp.concatenate([values * half for half in halves], 0)
        )
        att_ref[rows, lanes(0)] = out.astype(BF16)
        return carry

    rounds = (frames // LEN) * pairs
    cut = [rounds * i // 6 for i in range(7)]
    for i in range(6):
        tick()
        lax.fori_loop(cut[i], cut[i + 1], attention, 0)
    leave(4)
    triple_copy.wait()

    def branch(rows):
        resid = h_ref[rows] + product(att_ref[rows], held[2][...]) + vec(6)
        r1_ref[rows] = resid
        hat, _ = norm_parts(resid)
        first = hat * vec(7) + vec(8)
        h_ref[rows] = first
        z1_ref[rows] = first.astype(BF16)

    tick()
    each_tile(branch)
    leave(5)
    leave(6)

    def upper(c):
        cols = slice(c * D, (c + 1) * D)

        def body(rows):
            before = product(z1_ref[rows], held[3][:, cols]) + vec_ref[9:10, cols]
            active, slope = gelu_pair(before)
            act_ref[rows, cols] = active.astype(BF16)
            slope_ref[rows, cols] = slope

        each_tile(body)

    for c in range(FF // D):
        tick()
        upper(c)
    leave(7)
    leave(8)

    def lower_some(k):
        cols = slice(k * (D // 3), (k + 1) * (D // 3))

        def body(rows):
            h_ref[rows, cols] += product(act_ref[rows], held[4][:, cols])

        each_tile(body)

    for k in range(3):
        tick()
        lower_some(k)
    tick()

    for e in range(1, shards):
        shard_copy(e).wait_recv()
    for e in range(1, shards):
        shard_copy(e).wait_send()
    count = shard_all[0]
    for p in range(1, shards):
        count = count + shard_all[p]
    total_ref[...] = count
    per_frame = 1.0 / count[0:1, 0:1]
    codes = held[5][:, D:].astype(F32)
    cu_ref[...] = (
        codes * lax.rsqrt(jnp.sum(codes * codes, 0, keepdims=True) + 1e-06)
    ).astype(BF16)
    gv_ref[...] = jnp.zeros_like(gv_ref)
    loss_ref[...] = jnp.zeros_like(loss_ref)

    def lower(rows):
        masked = flag_ref[rows, 0:1]
        wh = held[5][:, :D]
        resid = h_ref[rows] + vec(10)
        hat, root = norm_parts(resid)
        second = (hat * vec(11) + vec(12)).astype(BF16)
        z2_ref[rows] = second
        head = product_nt(second, wh) + vec(13, CD)
        root_head = lax.rsqrt(jnp.sum(head * head, -1, keepdims=True) + 1e-06)
        unit = head * root_head
        unit_low = unit.astype(BF16)
        uc_ref[rows] = unit_low
        logits = temper * product(unit_low, cu_ref[...])
        code = lax.broadcasted_iota(jnp.int32, logits.shape, 1).astype(F32)
        logits = jnp.where(code < CODES, logits, -1e30)
        top = jnp.max(logits, -1, keepdims=True)
        power = jnp.exp(logits - top)
        total = jnp.sum(power, -1, keepdims=True)
        onehot = code == flag_ref[rows, 2:3]
        picked = jnp.sum(jnp.where(onehot, logits, 0.0), -1, keepdims=True)
        losses = top + jnp.log(total) - picked
        loss_ref[...] += jnp.sum(jnp.where(masked > 0.0, losses, 0.0), 0, keepdims=True)
        chances = power * (1.0 / total)
        d_logit = (
            temper
            * (jnp.where(masked > 0.0, chances - jnp.where(onehot, 1.0, 0.0), 0.0) * per_frame)
        ).astype(BF16)
        dlog_ref[rows] = d_logit
        d_unit = product_nt(d_logit, cu_ref[...])
        d_head = (
            root_head * (d_unit - unit * jnp.sum(d_unit * unit, -1, keepdims=True))
        ).astype(BF16)
        dc_ref[rows] = d_head
        gv_ref[13:14, :CD] += column_sum(d_head.astype(F32))
        d_second = product(d_head, wh)
        gv_ref[11:12, :D] += column_sum(d_second * hat)
        gv_ref[12:13, :D] += column_sum(d_second)
        d_resid = norm_back(d_second, hat, root, vec(11))
        dr2_ref[rows] = d_resid
        d_lower = d_resid.astype(BF16)
        df_ref[rows] = d_lower
        gv_ref[10:11, :D] += column_sum(d_lower.astype(F32))

    each_tile(lower)
    for k in range(9, len(kept)):
        leave(k)

    for i in range(n):
        core_copy(i, 0, 0, False).wait_send()
        for d in range(1, chips):
            xy_send(i, d).wait_send()
            core_copy(i, d, 0, False).wait_send()
            if parts[i].share:
                z_copy(i, d, False).wait_send()
                core_copy(i, d, 1, False).wait_send()
    for d in range(1, shards):
        vec_send(d).wait_send()
    for e in range(1, groups):
        group_copy(e).wait_send()
    for copy in outs + copies:
        copy.wait()


FORWARD_VALUES = (
    (8, F32),
    (CH, BF16),
    (D, BF16),
    (3 * D, BF16),
    (D, BF16),
    (D, F32),
    (D, BF16),
    (FF, BF16),
    (FF, F32),
    (D, BF16),
    (CD, BF16),
    (CPAD, BF16),
    (CD, BF16),
    (D, BF16),
    (D, F32),
)


def forward(groups, shards, lengths, starts, x, labels, weights):
    parts = weight_parts(shards)
    n = len(parts)
    chips = shards // 2
    frames = x.shape[0]
    hbm = pl.BlockSpec(memory_space=pl.ANY)
    vmem = pl.BlockSpec(memory_space=pltpu.VMEM)
    smem = pl.BlockSpec(memory_space=pltpu.SMEM)
    dma = pltpu.SemaphoreType.DMA
    arrays = [(CH, D), (D, 3 * D), (D, D), (D, FF), (FF, D), (CD, HEAD_COLS)]
    many = len(FORWARD_VALUES)
    results = pl.pallas_call(
        functools.partial(forward_kernel, parts, groups, shards),
        in_specs=[smem] * 2 + [vmem] * 7,
        out_specs=[hbm] * 7 + [vmem] * 3 + [hbm] * many,
        out_shape=[jax.ShapeDtypeStruct(shape, BF16) for shape in arrays]
        + [jax.ShapeDtypeStruct((16, FF), F32)]
        + [jax.ShapeDtypeStruct((8, 128), F32)] * 2
        + [jax.ShapeDtypeStruct((16, FF), F32)]
        + [jax.ShapeDtypeStruct((frames, width), kind) for width, kind in FORWARD_VALUES],
        scratch_shapes=[pltpu.VMEM(shape, BF16) for shape in arrays]
        + [
            pltpu.VMEM((frames, width), kind)
            for width, kind in FORWARD_VALUES
            if width != 3 * D
        ]
        + [
            pltpu.VMEM((shards, 16, FF // shards), BF16),
            pltpu.VMEM((16, FF), F32),
            pltpu.VMEM((CD, CPAD), BF16),
            pltpu.VMEM((8, 128), F32),
            pltpu.VMEM((groups, 8, 128), F32),
            pltpu.VMEM((shards, 8, 128), F32),
            dma((2, n, chips)),
            dma((2, n, chips)),
            dma((2, n, chips, 2)),
            dma((2, shards)),
            dma((2, groups)),
            dma((2, shards)),
            dma((7 + many,)),
        ],
        compiler_params=pltpu.CompilerParams(
            collective_id=2, has_side_effects=True, vmem_limit_bytes=64 * 1024 * 1024 - 65536
        ),
        name="forward",
    )(lengths, starts, x, labels, *weights)
    return results[:6], results[6], results[7], results[8], results[9], results[10:]


class Chunk:
    def __init__(self, rows, group, slot, sum_slot, wide_xy, wide_z, ring=True):
        self.ring = ring
        self.used = sum(rows)
        self.starts = [sum(rows[:i]) for i in range(len(rows))]
        self.rows = ceil_to(self.used, 16 * group)
        self.part = self.rows // group
        self.slot = slot
        self.sum_slot = sum_slot
        self.kind_xy = F32 if wide_xy else BF16
        self.kind_z = F32 if wide_z else BF16


HEAD_SLOT = 2


def gradient_chunks(groups, shards):
    down, band = FF // shards, D // shards
    half = down // 2
    return [
        Chunk([half], groups, 0, 0, False, True),
        Chunk([half], groups, 1, 1, False, True),
        Chunk([CD // shards] * 2, groups, HEAD_SLOT, 4, True, True),
        Chunk([band] * 2, groups, 0, 2, False, False),
        Chunk([band] * 2, groups, 1, 3, False, False),
        Chunk([band] * 2, groups, 0, 0, False, False),
        Chunk([band] * 2, groups, 1, 1, False, False),
        Chunk([CH // shards, 16], groups, 0, 5, False, True, False),
    ]


def tiles(rows, step, body):
    def once(i, carry):
        body(pl.ds(pl.multiple_of(i * step, step), step))
        return carry

    lax.fori_loop(0, rows // step, once, 0)


def backward_kernel(chunks, groups, shards, *refs):
    chips = shards // 2
    n = len(chunks)
    refs = list(refs)

    def take(count):
        out = refs[:count]
        del refs[:count]
        return out

    weights_hbm = take(6)
    vec_hbm, gvin_ref, loss_ref = take(3)
    (
        flag_hbm,
        a_hbm,
        hid_hbm,
        triple_hbm,
        att_hbm,
        r1_hbm,
        z1_hbm,
        act_hbm,
        slope_hbm,
        z2_hbm,
        uc_hbm,
        dlog_hbm,
        dc_hbm,
        df_hbm,
        dr2_hbm,
    ) = take(len(FORWARD_VALUES))
    (x_hbm,) = take(1)
    win_hbm, wqkv_hbm, wo_hbm, wu_hbm, wd_hbm, head_hbm = weights_hbm
    ring = take(n)
    (stat_out,) = take(1)
    pool, heads, dr1_ref, wide_ref, gv_ref, vec_ref, code_ref, flag_ref = take(8)
    full = take(3)
    pair = take(3)
    send_xy, recv_xy = take(3), take(n)
    acc = take(6)
    send_z, recv_z = take(n), take(n)
    stat_ref, group_all, stat_all = take(3)
    (
        load_sems,
        core_sems,
        credit,
        xy_sems,
        z_sems,
        right_sems,
        left_sems,
        loss_sems,
        stat_sems,
    ) = take(9)

    g = lax.axis_index("group")
    s = lax.axis_index("shard")
    core = lax.rem(s, 2)
    chip = s // 2
    sibling = s + 1 - 2 * core
    parts = FF // D
    frames = x_hbm.shape[0]

    def load(src, dst, sem):
        return pltpu.make_async_copy(src, dst, load_sems.at[sem])

    def cols(ref, c):
        return ref.at[:, c * D : (c + 1) * D]

    loads = {
        "df": load(df_hbm, pool.at[0], 0),
        "z1": load(z1_hbm, pool.at[3], 3),
        "z2": load(z2_hbm, heads.at[0], 8),
        "dc": load(dc_hbm, heads.at[1, :, 0:CD], 9),
        "uc": load(uc_hbm, heads.at[1, :, CD : 2 * CD], 10),
        "dlog": load(dlog_hbm, heads.at[2, :, 0:CPAD], 11),
        "hid": load(hid_hbm, pool.at[0], 0),
        "att": load(att_hbm, pool.at[4], 4),
        "x": load(x_hbm, pool.at[5, :, 0:CH], 5),
        "win": load(win_hbm, pool.at[6, 0:CH], 6),
        "dr2": load(dr2_hbm, dr1_ref, 7),
        "r1": load(r1_hbm, wide_ref, 14),
        "wo": load(wo_hbm, pool.at[2, 0:D], 2),
        "flags": load(flag_hbm, flag_ref, 15),
        "vec": load(vec_hbm, vec_ref, 16),
        "q": load(cols(triple_hbm, 0), heads.at[0], 8),
        "k": load(cols(triple_hbm, 1), heads.at[1], 9),
        "v": load(cols(triple_hbm, 2), heads.at[2], 11),
        "a": load(a_hbm, heads.at[3, :, 0:CH], 12),
        "codes": load(head_hbm.at[:, D:HEAD_COLS], code_ref, 13),
    }
    for c in range(parts):
        loads["act", c] = load(cols(act_hbm, c), pool.at[1 + c % 2], 1 + c % 2)
        loads["slope", c] = load(cols(slope_hbm, c), wide_ref, 14)
        loads["wd", c] = load(wd_hbm.at[c * D : (c + 1) * D], pool.at[2, 0:D], 2)
        loads["wu", c] = load(cols(wu_hbm, c), pool.at[5, 0:D], 5)
    for c in range(3):
        loads["w", c] = load(cols(wqkv_hbm, c), pool.at[1 + c, 0:D], 1 + c)

    def fetch(*names):
        for name in names:
            loads[name].start()

    def ready(*names):
        for name in names:
            loads[name].wait()

    fetch("df", ("act", 0), ("act", 1), "z2", "dc", "uc", "dlog", "codes", ("slope", 0), ("wu", 0))
    fetch("z1", "dr2", "flags", "vec")

    barrier = pltpu.get_barrier_semaphore()
    for e in range(1, shards):
        pl.semaphore_signal(
            barrier, 1, device_id=(g, lax.rem(s + e, shards)), device_id_type=MESH
        )
    for e in range(1, groups):
        pl.semaphore_signal(
            barrier, 1, device_id=(lax.rem(g + e, groups), s), device_id_type=MESH
        )
    pl.semaphore_wait(barrier, shards - 1 + groups - 1)

    def remote(src, dst, send_sem, recv_sem, device):
        return pltpu.make_async_remote_copy(
            src_ref=src,
            dst_ref=dst,
            send_sem=send_sem,
            recv_sem=recv_sem,
            device_id=device,
            device_id_type=MESH,
        )

    def chip_at(d):
        return lax.rem(chip + d, chips)

    order_out = list(range(1, chips)) + [0]

    def core_copy(t, d):
        c = chunks[t]
        q = chip_at(d)
        return remote(
            full[c.slot].at[q, 1 - core, 0 : c.used],
            pair[c.slot].at[q, 0 : c.used],
            core_sems.at[0, t, d],
            core_sems.at[1, t, d],
            (g, sibling),
        )

    before = {}
    for t, c in enumerate(chunks):
        earlier = [i for i in range(t) if chunks[i].slot == c.slot]
        before[t] = earlier[-1] if earlier else None
    last_of = {c.slot: t for t, c in enumerate(chunks)}

    def free_buffer(t):
        if before[t] is not None:
            for d in order_out:
                core_copy(before[t], d).wait_send()

    def stage_pair(t):
        if before[t] is not None:
            pl.semaphore_wait(credit.at[chunks[t].slot], 1)
        for d in order_out:
            core_copy(t, d).start()

    def xy_copy(t, d):
        return remote(
            send_xy[chunks[t].slot].at[d - 1, 0 : chunks[t].used],
            recv_xy[t].at[d - 1],
            xy_sems.at[0, t, d],
            xy_sems.at[1, t, d],
            (g, 2 * chip_at(d) + core),
        )

    def stage_chips(t):
        c = chunks[t]
        own, other = full[c.slot], pair[c.slot]
        for d in order_out:
            q = chip_at(d)
            core_copy(t, d).wait_recv()
            if d > 0 and before[t] is not None:
                xy_copy(before[t], d).wait_send()
            if d == 0:

                def keep(rows):
                    acc[c.sum_slot][rows] = own[q, core, rows] + other[q, rows]

                tiles(c.used, 16, keep)
                if c.rows > c.used:
                    acc[c.sum_slot][c.used : c.rows] = jnp.zeros((c.rows - c.used, D), F32)
            else:

                def send(rows):
                    send_xy[c.slot][d - 1, rows] = (own[q, core, rows] + other[q, rows]).astype(
                        c.kind_xy
                    )

                tiles(c.used, 16, send)
                xy_copy(t, d).start()
        if t != last_of[c.slot]:
            pl.semaphore_signal(
                credit.at[c.slot], 1, device_id=(g, sibling), device_id_type=MESH
            )

    def z_copy(t, e):
        return remote(
            send_z[t].at[e - 1],
            recv_z[t].at[e - 1],
            z_sems.at[0, t, e],
            z_sems.at[1, t, e],
            (lax.rem(g + e, groups), s),
        )

    def stage_group(t):
        c = chunks[t]
        total_ref = acc[c.sum_slot]
        for d in range(1, chips):
            xy_copy(t, d).wait_recv()

        def add(rows):
            total = total_ref[rows]
            for d in range(1, chips):
                total = total + recv_xy[t][d - 1, rows].astype(F32)
            total_ref[rows] = total

        tiles(c.used, 16, add)
        for e in range(1, groups):
            base = pl.multiple_of(lax.rem(g + e, groups) * c.part, 16)

            def send(rows):
                here = pl.ds(pl.multiple_of(base + rows.start, 16), 16)
                send_z[t][e - 1, rows] = total_ref[here].astype(BF16)

            tiles(c.part, 16, send)
            z_copy(t, e).start()

    def part_rows(t, p):
        return pl.ds(pl.multiple_of(p * chunks[t].part, 16), chunks[t].part)

    def ring_copy(t, k, way, back=0):
        p = g - k if way == 0 else g + k
        side = lax.rem(g + 1, groups) if way == 0 else lax.rem(g + groups - 1, groups)
        sems = right_sems if way == 0 else left_sems
        rows = part_rows(t, p)
        return remote(
            ring[t].at[rows],
            ring[t].at[rows],
            sems.at[0, t, k],
            sems.at[1, t, k - back],
            (side, s),
        )

    def near_copy(t, e, p):
        rows = part_rows(t, p)
        return remote(
            ring[t].at[rows],
            ring[t].at[rows],
            right_sems.at[0, t, e],
            right_sems.at[1, t, e],
            (lax.rem(g + e, groups), s),
        )

    def holds(k, way):
        return g >= k if way == 0 else g + k < groups

    def sends(k, way):
        return (g >= k) & (g < groups - 1) if way == 0 else (g + k < groups) & (g > 0)

    def stage_total(t):
        c = chunks[t]
        total_ref = acc[c.sum_slot]
        for e in range(1, groups):
            z_copy(t, e).wait_recv()
        base = pl.multiple_of(g * c.part, 16)

        def add(i, sums):
            rows = pl.ds(pl.multiple_of(i * 16, 16), 16)
            here = pl.ds(pl.multiple_of(base + i * 16, 16), 16)
            total = total_ref[here]
            for e in range(1, groups):
                total = total + recv_z[t][e - 1, rows].astype(F32)
            total = total.astype(c.kind_z)
            ring[t][here] = total
            total = total.astype(F32)
            total = total * total
            return sums + total[:8] + total[8:]

        squares[0] = lax.fori_loop(0, c.part // 16, add, squares[0])
        if not c.ring:
            for e in range(1, groups):
                near_copy(t, e, g).start()
            return
        for way in (0, 1):

            @pl.when(sends(0, way))
            def _():
                ring_copy(t, 0, way).start()

    def stage_ring(t, k):
        if not chunks[t].ring:
            if k == 1:
                for e in range(1, groups):
                    near_copy(t, e, lax.rem(g + groups - e, groups)).wait_recv()
            return
        for way in (0, 1):

            @pl.when(holds(k, way))
            def _():
                ring_copy(t, k, way, 1).wait_recv()

            if k < groups - 1:

                @pl.when(sends(k, way))
                def _():
                    ring_copy(t, k, way).start()

    done = [0] * n
    squares = [jnp.zeros((8, D), F32)]

    def step(t):
        now = done[t]
        done[t] += 1
        if now == 0:
            stage_pair(t)
        elif now == 1:
            same = [u for u in range(t) if chunks[u].sum_slot == chunks[t].sum_slot]
            assert all(done[u] > 3 for u in same)
            stage_chips(t)
        elif now == 2:
            stage_group(t)
        elif now == 3:
            stage_total(t)
        else:
            stage_ring(t, now - 3)

    plan = iter(BACKWARD_PLAN)

    def tick():
        for t in next(plan):
            step(t)

    def scatter(value, slots, at, per, first_shard, col=0):
        count = value.shape[0] // per
        each = per // len(slots)
        for k in range(count):
            shard = first_shard * 1 + k
            for i, slot in enumerate(slots):
                rows = value[k * per + i * each : k * per + (i + 1) * each]
                full[slot][
                    shard // 2, lax.rem(shard, 2), at : at + each, col : col + rows.shape[1]
                ] = rows

    def grad(left, right, slots, at, per, block, col=0):
        width = left.shape[1]

        def once(i, carry):
            some = left[:, pl.ds(pl.multiple_of(i * block, 128), block)]
            scatter(product_tn(some, right[...]), slots, at, per, i * (block // per), col)
            return carry

        lax.fori_loop(0, width // block, once, 0)

    down, band, deep, first = FF // shards, D // shards, CD // shards, CH // shards
    wide = FF // shards
    pairs = D // 128

    ready("df")
    for c in range(parts):
        ready(("act", c))
        for i in range(2):
            value = product_tn(
                pool[1 + c % 2, :, i * (D // 2) : (i + 1) * (D // 2)], pool[0]
            )
            scatter(value, [0, 1], 0, down, (c * D + i * (D // 2)) // down)
        if c + 2 < parts:
            fetch(("act", c + 2))
    fetch(("wd", 0))
    tick()
    ready("z2", "dc", "uc", "dlog", "codes")
    scatter(product_tn(heads[1, :, 0:CD], heads[0]), [HEAD_SLOT], 0, deep, 0)
    d_unit = product_tn(heads[1, :, CD : 2 * CD], heads[2, :, 0:CPAD])
    codes = code_ref[...].astype(F32)
    root = lax.rsqrt(jnp.sum(codes * codes, 0, keepdims=True) + 1e-06)
    unit = codes * root
    d_codes = root * (d_unit - unit * jnp.sum(d_unit * unit, 0, keepdims=True))
    scatter(d_codes, [HEAD_SLOT], deep, deep, 0)
    full[HEAD_SLOT][:, :, deep : 2 * deep, CPAD:D] = jnp.zeros((chips, 2, deep, D - CPAD), F32)
    fetch("q", "k", "v", "att", "win")
    tick()
    ready("z1", "dr2", "flags", "vec")
    gv_ref[...] = gvin_ref[...]

    def each_tile(body, begin=0, end=None):
        def once(i, carry):
            body(pl.ds(pl.multiple_of(i * 256, 256), 256))
            return carry

        lax.fori_loop(begin, frames // 256 if end is None else end, once, 0)

    for t, first_part in ((3, 0), (4, 2)):
        for i in range(2):
            c = first_part + i
            span = slice(c * D, (c + 1) * D)
            ready(("slope", c), ("wd", c), ("wu", c))

            def lower(rows):
                d_before = wide_ref[rows] * product_nt(pool[0, rows], pool[2, 0:D])
                d_before = d_before.astype(BF16)
                pool[1, rows] = d_before
                gv_ref[9:10, span] += column_sum(d_before.astype(F32))
                dr1_ref[rows] += product_nt(d_before, pool[5, 0:D])

            each_tile(lower)
            tick()
            if i == 0:
                free_buffer(t)
            if c + 1 < parts:
                fetch(("slope", c + 1), ("wd", c + 1), ("wu", c + 1))
            else:
                fetch("r1", "wo", "hid")
            grad(pool.at[3], pool.at[1], [chunks[t].slot], i * band, band, D // 2)
            tick()
    ready("r1", "wo")

    def branch(rows):
        hat, root = norm_parts(wide_ref[rows])
        d_first = dr1_ref[rows]
        gv_ref[7:8, :D] += column_sum(d_first * hat)
        gv_ref[8:9, :D] += column_sum(d_first)
        d_resid = norm_back(d_first, hat, root, vec_ref[7:8, :D])
        dr1_ref[rows] = d_resid
        d_branch = d_resid.astype(BF16)
        pool[5, rows] = d_branch
        gv_ref[6:7, :D] += column_sum(d_branch.astype(F32))
        heads[3, rows] = product_nt(d_branch, pool[2, 0:D]).astype(BF16)

    each_tile(branch)
    for c in range(3):
        fetch(("w", c))
    tick()

    halves = half_masks()
    utters = frames // LEN
    scale = jnp.bfloat16(HEAD_DIM ** (-0.5))

    def attention(i, carry):
        rows = pl.ds(pl.multiple_of(lax.rem(i, utters) * LEN, LEN), LEN)
        lanes = pl.ds(pl.multiple_of((i // utters) * 128, 128), 128)
        shift = flag_ref[rows, 1:2]
        keys, values = heads[1, rows, lanes], heads[2, rows, lanes]
        probs_low, d_low, queries, ups = [], [], [], []
        for half in halves:
            query = heads[0, rows, lanes] * (half * scale)
            upstream = heads[3, rows, lanes] * half
            scores = product_nt(keys, query) + shift
            power = jnp.exp(scores - jnp.max(scores, 0, keepdims=True))
            probs = power * (1.0 / jnp.sum(power, 0, keepdims=True))
            d_probs = product_nt(values, upstream)
            weight = jnp.sum(probs * d_probs, 0, keepdims=True)
            probs_low.append(probs.astype(BF16))
            d_low.append((probs * (d_probs - weight)).astype(BF16))
            queries.append(query)
            ups.append(upstream)
        dv = product(jnp.concatenate(probs_low, 1), jnp.concatenate(ups, 0))
        dk = product(jnp.concatenate(d_low, 1), jnp.concatenate(queries, 0))
        dq = product_tn(
            jnp.concatenate(d_low, 0),
            jnp.concatenate([keys * (half * scale) for half in halves], 0),
        )
        heads[0, rows, lanes] = dq.astype(BF16)
        heads[1, rows, lanes] = dk.astype(BF16)
        heads[2, rows, lanes] = dv.astype(BF16)
        return carry

    ready("q", "k", "v")
    rounds = utters * pairs
    middle = D // 2

    def attend(begin, end):
        cut = [begin + (end - begin) * i // 3 for i in range(4)]
        for i in range(3):
            lax.fori_loop(cut[i], cut[i + 1], attention, 0)
            tick()

    attend(0, rounds // 2)
    ready("hid", "att")
    free_buffer(5)
    grad(pool.at[0], heads.at[0, :, 0:middle], [0], 0, band, middle)
    grad(pool.at[0], heads.at[1, :, 0:middle], [0], 0, band, middle, middle)
    grad(pool.at[4], pool.at[5], [0], band, band, middle)
    tick()
    fetch("x")
    attend(rounds // 2, rounds)
    fetch("a")
    free_buffer(6)
    grad(pool.at[0], heads.at[2], [1], 0, band, middle)
    grad(pool.at[0], heads.at[0, :, middle:D], [1], band, band, middle)
    grad(pool.at[0], heads.at[1, :, middle:D], [1], band, band, middle, middle)
    tick()
    ready(("w", 0), ("w", 1), ("w", 2), "win", "x")

    def back(rows):
        dq, dk, dv = heads[0, rows], heads[1, rows], heads[2, rows]
        gv_ref[4:5, :D] += column_sum(dq.astype(F32))
        gv_ref[5:6, :D] += column_sum(dv.astype(F32))
        d_hidden = (
            dr1_ref[rows]
            + product_nt(dq, pool[1, 0:D])
            + product_nt(dk, pool[2, 0:D])
            + product_nt(dv, pool[3, 0:D])
        )
        masked = flag_ref[rows, 0:1] > 0.0
        gv_ref[3:4, :D] += column_sum(jnp.where(masked, d_hidden, 0.0))
        d_proj = jnp.where(masked, 0.0, d_hidden).astype(BF16)
        pool[4, rows] = d_proj
        gv_ref[2:3, :D] += column_sum(d_proj.astype(F32))
        d_normed = product_nt(d_proj, pool[6, 0:CH])
        hat, _ = norm_parts(pool[5, rows, 0:CH].astype(F32))
        gv_ref[0:1, :CH] += column_sum(d_normed * hat)
        gv_ref[1:2, :CH] += column_sum(d_normed)

    each_tile(back, 0, 2)
    tick()
    each_tile(back, 2)
    tick()
    ready("a")
    free_buffer(7)
    grad(heads.at[3, :, 0:CH], pool.at[4], [0], 0, first, CH // 2)
    for b in range(shards):
        full[0][b // 2, b % 2, first : first + 16, 0:wide] = gv_ref[:, b * wide : (b + 1) * wide]
        full[0][b // 2, b % 2, first : first + 16, wide:D] = jnp.zeros((16, D - wide), F32)
    final = 3 + groups
    rest = list(next(plan))

    def advance(enough):
        while rest and not enough():
            step(rest.pop(0))

    def group_copy(e):
        return remote(
            stat_ref.at[0],
            group_all.at[g],
            loss_sems.at[0, e],
            loss_sems.at[1, e],
            (lax.rem(g + e, groups), s),
        )

    def stat_copy(e):
        return remote(
            stat_ref.at[1],
            stat_all.at[s],
            stat_sems.at[0, e],
            stat_sems.at[1, e],
            (g, lax.rem(s + e, shards)),
        )

    advance(lambda: min(done) > 3)
    lane = lax.broadcasted_iota(jnp.int32, (8, 128), 1)
    stat_ref[0] = jnp.where(lane == 0, jnp.sum(squares[0]), loss_ref[...])
    for e in range(1, groups):
        group_copy(e).start()
    group_all[g] = stat_ref[0]
    left_over = len(rest) - 3
    advance(lambda: len(rest) <= left_over)
    for e in range(1, groups):
        group_copy(e).wait_recv()
    total = group_all[0]
    for p in range(1, groups):
        total = total + group_all[p]
    stat_ref[1] = total
    for e in range(1, shards):
        stat_copy(e).start()
    stat_all[s] = total
    advance(lambda: False)
    while min(done) < final:
        step(done.index(min(done)))
    for e in range(1, shards):
        stat_copy(e).wait_recv()
    total = stat_all[0]
    for p in range(1, shards):
        total = total + stat_all[p]
    stat_out[...] = total
    for t in range(n):
        if t == last_of[chunks[t].slot]:
            for d in order_out:
                core_copy(t, d).wait_send()
            for d in range(1, chips):
                xy_copy(t, d).wait_send()
        for e in range(1, groups):
            z_copy(t, e).wait_send()
            if not chunks[t].ring:
                near_copy(t, e, g).wait_send()
        for k in range(groups - 1 if chunks[t].ring else 0):
            for way in (0, 1):

                @pl.when(sends(k, way))
                def _():
                    ring_copy(t, k, way).wait_send()

    for e in range(1, groups):
        group_copy(e).wait_send()
    for e in range(1, shards):
        stat_copy(e).wait_send()


def backward(groups, shards, weights, vecs, gv, loss, values, x):
    chunks = gradient_chunks(groups, shards)
    chips = shards // 2
    n = len(chunks)
    frames = x.shape[0]
    hbm = pl.BlockSpec(memory_space=pl.ANY)
    vmem = pl.BlockSpec(memory_space=pltpu.VMEM)
    dma = pltpu.SemaphoreType.DMA
    deepest = [max(c.used for c in chunks if c.slot == i) for i in range(3)]
    sums = [max(c.rows for c in chunks if c.sum_slot == i) for i in range(6)]
    results = pl.pallas_call(
        functools.partial(backward_kernel, chunks, groups, shards),
        in_specs=[hbm] * 7 + [vmem] * 2 + [hbm] * (len(values) + 1),
        out_specs=[vmem] * (n + 1),
        out_shape=[jax.ShapeDtypeStruct((c.rows, D), c.kind_z) for c in chunks]
        + [jax.ShapeDtypeStruct((8, 128), F32)],
        scratch_shapes=[
            pltpu.VMEM((7, frames, D), BF16),
            pltpu.VMEM((4, frames, D), BF16),
            pltpu.VMEM((frames, D), F32),
            pltpu.VMEM((frames, D), F32),
            pltpu.VMEM((16, FF), F32),
            pltpu.VMEM((16, FF), F32),
            pltpu.VMEM((CD, CPAD), BF16),
            pltpu.VMEM((frames, 8), F32),
        ]
        + [pltpu.VMEM((chips, 2, rows, D), F32) for rows in deepest]
        + [pltpu.VMEM((chips, rows, D), F32) for rows in deepest]
        + [
            pltpu.VMEM((chips - 1, rows, D), F32 if i == HEAD_SLOT else BF16)
            for i, rows in enumerate(deepest)
        ]
        + [pltpu.VMEM((chips - 1, c.used, D), c.kind_xy) for c in chunks]
        + [pltpu.VMEM((rows, D), F32) for rows in sums]
        + [pltpu.VMEM((groups - 1, c.part, D), BF16) for c in chunks] * 2
        + [
            pltpu.VMEM((2, 8, 128), F32),
            pltpu.VMEM((groups, 8, 128), F32),
            pltpu.VMEM((shards, 8, 128), F32),
        ]
        + [
            dma((17,)),
            dma((2, n, chips)),
            pltpu.SemaphoreType.REGULAR((3,)),
            dma((2, n, chips)),
            dma((2, n, groups)),
            dma((2, n, groups)),
            dma((2, n, groups)),
            dma((2, groups)),
            dma((2, shards)),
        ],
        compiler_params=pltpu.CompilerParams(
            collective_id=1, has_side_effects=True, vmem_limit_bytes=64 * 1024 * 1024 - 65536
        ),
        name="backward",
    )(*weights, vecs, gv, loss, *values, x)
    return results[:n], results[n]


def adam_kernel(step_ref, stat_ref, count_ref, *refs):
    w, m, v = refs[0:5], refs[5:10], refs[10:15]
    g_head, g_tail = refs[15:17]
    early_ref, late_ref = refs[17:19]
    halves = refs[19:23]
    outs = [refs[23 + 5 * i : 28 + 5 * i] for i in range(4)]
    norm_ref, loss_ref = refs[43:45]
    step = pl.program_id(0)
    fix_one, fix_two = (
        1.0 - lax.fori_loop(0, step_ref[0], lambda _, value: value * beta, jnp.float32(1.0))
        for beta in (beta_one, beta_two)
    )
    norm = jnp.sqrt(stat_ref[0:1, 0:1])
    factor = jnp.minimum(1.0, clip_norm / (norm + 1e-06))

    def update(i, grad, where=...):
        shrink = 0.0 if i == 4 else decay
        weight, moment, square = w[i][where], m[i][where], v[i][where]
        grad = grad.astype(F32) * factor
        moment = beta_one * moment + (1.0 - beta_one) * grad
        square = beta_two * square + (1.0 - beta_two) * grad * grad
        stepped = moment * (1.0 / fix_one) / (jnp.sqrt(square * (1.0 / fix_two)) + adam_eps)
        weight = weight - rate * (stepped + shrink * weight)
        for out, value in zip(outs, (weight, moment, square, weight.astype(BF16))):
            out[i][where] = value

    def both(early):
        @pl.when(early == (step < 2))
        def _():
            up, down = halves[0 if early else 1 :: 2]
            update(1, up[...], 1)
            update(2, down[...])

    depth = w[1].shape[1]
    upper, lower = slice(0, depth), slice(depth, 2 * depth)
    left, right = slice(0, D // 2), slice(D // 2, D)

    @pl.when(step == 0)
    def _():
        update(1, early_ref[upper, left], (0, slice(None), left))
        update(1, late_ref[lower, left], (0, slice(None), right))

    @pl.when(step == 1)
    def _():
        update(1, early_ref[upper, right], (0, slice(None), left))
        update(1, late_ref[lower, right], (0, slice(None), right))

    @pl.when(step == 2)
    def _():
        update(1, late_ref[upper], 0)

    @pl.when(step == 3)
    def _():
        update(1, early_ref[lower], 0)

    both(True)
    both(False)

    @pl.when(step == 0)
    def _():
        first, deep = w[0].shape[0], w[3].shape[0]
        norm_ref[...] = norm
        loss_ref[...] = stat_ref[0:1, 1:2] / count_ref[0:1, 0:1]
        update(0, g_tail[:first])
        update(3, g_head[:deep], (slice(None), slice(0, D)))
        update(3, g_head[deep : 2 * deep, :CODES], (slice(None), slice(D, D + CODES)))
        update(4, g_tail[first : first + NVEC, : w[4].shape[1]])


def adam(steps, stat, count, weights, moments, seconds, sums):
    parts = FF // D
    depth = weights[1].shape[1]
    tall = weights[2].shape[0] // parts

    def fixed(a):
        return pl.BlockSpec(a.shape, lambda i: (0,) * a.ndim)

    w_specs = [
        fixed(weights[0]),
        pl.BlockSpec((2, depth, D), lambda i: (0, 0, i)),
        pl.BlockSpec((tall, D), lambda i: (i, 0)),
        fixed(weights[3]),
        fixed(weights[4]),
    ]
    g_specs = [fixed(sums[i]) for i in (2, 7, 5, 6)]
    for rows in (depth, tall):
        g_specs.append(pl.BlockSpec((rows, D), lambda i: (jnp.minimum(i, 1), 0)))
        g_specs.append(pl.BlockSpec((rows, D), lambda i: (jnp.maximum(i - 2, 0), 0)))
    shapes = [jax.ShapeDtypeStruct(w.shape, F32) for w in weights]
    low = [jax.ShapeDtypeStruct(w.shape, BF16) for w in weights]
    outs = pl.pallas_call(
        adam_kernel,
        grid=(parts,),
        in_specs=[pl.BlockSpec(memory_space=pltpu.SMEM), fixed(stat), fixed(count)]
        + w_specs * 3
        + g_specs,
        out_specs=w_specs * 4 + [pl.BlockSpec((1, 1), lambda i: (0, 0))] * 2,
        out_shape=shapes * 3 + low + [jax.ShapeDtypeStruct((1, 1), F32)] * 2,
        compiler_params=params(),
        name="adam",
    )(
        steps,
        stat,
        count,
        *weights,
        *moments,
        *seconds,
        *[sums[i] for i in (2, 7, 5, 6, 3, 4, 0, 1)],
    )
    return [outs[i * 5 : (i + 1) * 5] for i in range(4)] + list(outs[20:])


def per_device(
    features,
    lengths,
    starts,
    labels,
    step_count,
    weight_in,
    weight_rows,
    weight_down,
    weight_head,
    vectors,
    moment_in,
    moment_rows,
    moment_down,
    moment_head,
    moment_vectors,
    second_in,
    second_rows,
    second_down,
    second_head,
    second_vectors,
):
    masters = (weight_in, weight_rows, weight_down, weight_head, vectors)
    moments = (moment_in, moment_rows, moment_down, moment_head, moment_vectors)
    seconds = (second_in, second_rows, second_down, second_head, second_vectors)
    groups, shards = lax.axis_size("group"), lax.axis_size("shard")
    x = features.reshape(-1, CH)

    def turned(arrays):
        return [a.T if i == 3 else a for i, a in enumerate(arrays)]

    weights, vecs, count, loss, gv, values = forward(
        groups, shards, lengths, starts, x, labels, turned(masters)
    )
    sums, stat = backward(groups, shards, weights, vecs, gv, loss, values, x)
    *updated, norm, loss = adam(
        step_count, stat, count, turned(masters), turned(moments), turned(seconds), sums
    )
    new_w, new_m, new_v, copies = (turned(out) for out in updated)
    return (
        *new_w,
        *new_m,
        *new_v,
        *copies,
        jnp.reshape(loss, (1,)),
        jnp.reshape(norm, (1,)),
    )


def solution(mesh):
    weights = (
        P("shard", None),
        P(None, "shard", None),
        P("shard", None),
        P(None, "shard"),
        P(None, "shard"),
    )
    both = ("group", "shard")
    in_specs = (P(both, None, None), P(both), P(both, None), P(both, None), P()) + weights * 3
    out_specs = weights * 4 + (P(), P())
    return jax.shard_map(
        per_device, mesh=mesh, in_specs=in_specs, out_specs=out_specs, check_vma=False
    )
```
